256 devices in a mesh: dp: 32 (over z_hi, x, core), node: 8 (over y, z_lo).
Axes of the slice: x: 4, y: 4, z: 8 (z_hi: 4, z_lo: 2; z = z_hi * 2 + z_lo), core: 2. Of those that a mesh axis runs over, the one named last changes fastest.
Arguments:
- x_band: bfloat16 [32768, 512], P(('dp', 'node')), may hold values from -6 to 6
- d_gate_up: bfloat16 [32768, 18432], P(('dp', 'node')), may hold values from -0.125 to 0.125
- owner: int32 [36], replicated, may hold values from 0 to 31, as said below
- stat_left: float32 [32, 2, 512, 512], P('dp', None, 'node'), as said below
- stat_right: float32 [32, 2, 512, 512], P('dp', None, 'node'), as said below
Outputs:
- directions: bfloat16 [512, 18432], P('node')
- stat_left_new: float32 [32, 2, 512, 512], P('dp', None, 'node')
- stat_right_new: float32 [32, 2, 512, 512], P('dp', None, 'node')
The draws below stay inside these ranges and needn't reach their ends.
Inputs may be any that keep to these rules, and one draw needn't show every extreme that they name: owner[0], ..., owner[31] name every index of dp once, and owner[b] = owner[b - 32] for b >= 32; block b sits in slot b // 32 of its owner. Each stat_left[o, s] is symmetric positive definite. Each stat_right[o, s] is symmetric positive definite.
All inputs are finite; a program needn't handle non-finite values.
Results may differ from the reference program's by a relative error of at most 0.023.
Values may be sent and summed in bfloat16 or wider, within the bound.
No kernel may reach another device: no remote copies, remote signals or barrier semaphores. Data moves between devices by JAX's collectives and lax.ppermute only.
A program may use at most 128 MiB of HBM per device.

```python
import jax
import jax.numpy as jnp
from jax import lax

B = 512
TOK_DEV = 128
SLOTS = 2
ITERS = 2
BUCKET = 36
TOKENS = 32768
N_DP = 32
N_NODE = 8


def definite_draw(key, top_scale, rough, lowest_off):
    key_off, key_diag = jax.random.split(key)
    entries = jax.random.uniform(key_off, (N_DP, SLOTS, B, B), jnp.float32, lowest_off, 1.0)
    entries = (entries + jnp.swapaxes(entries, -1, -2)) * 0.5
    ramp = jnp.arange(B, dtype=jnp.float32) / B
    noise = jax.random.uniform(key_diag, (N_DP, SLOTS, B), jnp.float32)
    diagonal = jnp.exp(jnp.log(top_scale) * ramp) * (1.0 + rough * noise)
    largest = top_scale * (1.0 + rough)
    root_diag = jnp.sqrt(diagonal)
    coupling = root_diag[..., :, None] * root_diag[..., None, :] * (1.0 / (B * jnp.sqrt(largest)))
    identity = jnp.eye(B, dtype=jnp.float32)
    return entries * coupling * (1.0 - identity) + identity * diagonal[..., None]


def draw_owner(key, part):
    key = jax.random.fold_in(key, 5)
    shuffled = jax.random.permutation(key, N_DP)
    return shuffled[jnp.arange(BUCKET) % N_DP].astype(jnp.int32)


def draw_stat_left(key, part):
    key = jax.random.fold_in(key, 11)
    return definite_draw(key, 10.0, 0.5, -1.0)


def draw_stat_right(key, part):
    key = jax.random.fold_in(key, 17)
    return definite_draw(key, 10.0, 0.5, -1.0)


def with_spikes(drawn, own_key, source, target, parts, factor):
    def block_of(dim):
        return (jnp.arange(drawn.shape[dim]) // (drawn.shape[dim] // parts)).reshape((-1,) + (1,) * (drawn.ndim - 1 - dim))

    first = jax.random.permutation(own_key, parts)[block_of(target)]
    other_side = (block_of(target) + parts // 2) % parts
    return jnp.where((block_of(source) == first) | (block_of(source) == other_side), factor * drawn, drawn)


def block_scale(stream_key, extent, pieces, smallest, top_value):
    loudness, own = 1.0, jax.random.fold_in(stream_key, 6)
    for dim, blocks in pieces:
        steps = jnp.exp(jax.random.uniform(jax.random.fold_in(own, dim), (blocks,), jnp.float32, smallest / len(pieces), top_value / len(pieces)))
        loudness = loudness * jnp.repeat(steps, extent[dim] // blocks).reshape([-1 if axis == dim else 1 for axis in range(len(extent))])
    return loudness


def centred(own_key, dims, spread, reach, shards=(), kind=jnp.bfloat16):
    drawn = spread * jax.random.normal(own_key, dims, jnp.float32)
    if shards:
        drawn = drawn * block_scale(own_key, dims, shards, -0.22, 0.18)
    return jnp.clip(drawn, -reach, reach).astype(kind)


def gaussian_with(own_key, shape, spread, reach, cuts, heavy, kind=jnp.bfloat16):
    values = spread * jax.random.normal(own_key, shape, jnp.float32)
    if cuts:
        values = values * block_scale(own_key, shape, cuts, -0.22, 0.18)
    return jnp.clip(with_spikes(values, jax.random.fold_in(own_key, 3), *heavy), -reach, reach).astype(kind)


def setup_inputs(seed: int = 0) -> dict:
    splits = jax.random.split(jax.random.key(seed), 6)
    x_band = centred(splits[0], (TOKENS, B), 1.0, 6.0, ((0, 256),))
    d_gate_up = gaussian_with(splits[1], (TOKENS, BUCKET * B), (TOKENS ** -0.5), 0.125, ((0, 256),), (0, 1, 256, 6.0))
    owner = draw_owner(jax.random.fold_in(splits[5], 71), 0)
    stat_left = draw_stat_left(jax.random.fold_in(splits[5], 71), 0)
    stat_right = draw_stat_right(jax.random.fold_in(splits[5], 71), 0)
    return {"x_band": x_band, "d_gate_up": d_gate_up, "owner": owner, "stat_left": stat_left, "stat_right": stat_right}


BETA = 0.9

def batched(first_matrix, second_matrix):
    return jnp.einsum('kij,kjl->kil', first_matrix, second_matrix, precision=lax.Precision.HIGHEST)

def newton_root(statistic):
    block_order = statistic.shape[-1]
    identity = jnp.eye(block_order, dtype=statistic.dtype)
    norm_scale = block_order * jnp.sqrt(lax.optimization_barrier(jnp.mean(statistic * statistic, axis=(1, 2))) + 1e-06)
    inverse_root = identity[None] * (norm_scale ** (-0.25))[:, None, None]
    moment = statistic / norm_scale[:, None, None]
    for iteration in range(ITERS):
        factor = (5.0 * identity - moment) * 0.25
        inverse_root = batched(inverse_root, factor)
        if iteration + 1 < ITERS:
            square = batched(factor, factor)
            fourth = batched(square, square)
            moment = batched(fourth, moment)
    return inverse_root

def reference(x_band, d_gate_up, owner, stat_left, stat_right):
    devices_all = N_DP * N_NODE
    activations = x_band.reshape(devices_all, TOK_DEV, B)
    cotangents = d_gate_up.reshape(devices_all, TOK_DEV, BUCKET * B)

    def accumulate(running, device_pair):
        partial_value = jnp.dot(device_pair[0].T, device_pair[1], preferred_element_type=jnp.float32)
        rounded = lax.optimization_barrier(partial_value.astype(jnp.bfloat16))
        return (running + rounded.astype(jnp.float32), None)
    gradient, unused = lax.scan(accumulate, jnp.zeros((B, BUCKET * B), jnp.float32), (activations, cotangents))
    gradient_low = gradient.astype(jnp.bfloat16)
    blocks = gradient_low.reshape(B, BUCKET, B).transpose(1, 0, 2)
    first_owners = owner[:N_DP]
    owner_ids = jnp.arange(N_DP, dtype=jnp.int32)
    position = lax.optimization_barrier(jnp.sum(owner_ids[None, :] * (first_owners[None, :] == owner_ids[:, None]).astype(jnp.int32), axis=1))
    slot_block = position[:, None] + N_DP * jnp.arange(SLOTS, dtype=jnp.int32)[None, :]
    is_valid = (slot_block < BUCKET).astype(jnp.bfloat16)
    slot_grad = blocks[jnp.minimum(slot_block, BUCKET - 1)] * is_valid[..., None, None]
    slot_float = slot_grad.astype(jnp.float32)
    left_new = BETA * stat_left + jnp.einsum('osic,osjc->osij', slot_float, slot_float) / B
    right_new = BETA * stat_right + jnp.einsum('osci,oscj->osij', slot_float, slot_float) / B

    def owner_work(owner_items):
        left_one, right_one, grad_one = owner_items
        problems = jnp.stack([left_one, right_one], axis=1).reshape(2 * SLOTS, B, B)
        rounded_roots = lax.optimization_barrier(newton_root(problems).astype(jnp.bfloat16))
        inverse_roots = rounded_roots.astype(jnp.float32).reshape(SLOTS, 2, B, B)
        half_product = jnp.einsum('sij,sjc->sic', inverse_roots[:, 0], grad_one.astype(jnp.float32))
        half_low = lax.optimization_barrier(half_product.astype(jnp.bfloat16))
        result = jnp.einsum('sic,scd->sid', half_low.astype(jnp.float32), inverse_roots[:, 1])
        return result.astype(jnp.bfloat16)
    directed = lax.map(owner_work, (left_new, right_new, slot_grad))
    picked = directed[owner, jnp.arange(BUCKET, dtype=jnp.int32) // N_DP]
    directions = picked.transpose(1, 0, 2).reshape(B, BUCKET * B)
    return (directions, left_new, right_new)
```

```python
import math

import jax
import jax.numpy as jnp
import numpy as np
from jax import lax
from jax.experimental import pallas as pl
from jax.experimental.pallas import tpu as pltpu
from jax.sharding import Mesh, PartitionSpec as P

B = 512
SLOTS = 2
BETA = 0.9
EXTRA_CHUNK = 128
FLOW = B + EXTRA_CHUNK
HALF = B // 2

FINE = ("z_hi", "x", "core", "y", "z_lo")
FINE_SIZES = (4, 4, 2, 4, 2)
VMEM_LIMIT = 48 * 1024 * 1024

COEF = [6.25 / 4, -(1.25 + 1.25**5) / 4] + [
    -math.comb(5, k) * 1.25 ** (5 - k) * (-0.25) ** k / 4 for k in range(1, 6)
]

ANY = pl.BlockSpec(memory_space=pl.ANY)
SMEM = pl.BlockSpec(memory_space=pltpu.SMEM)
VMEM = pl.BlockSpec(memory_space=pltpu.VMEM)
PARAMS = pltpu.CompilerParams(vmem_limit_bytes=VMEM_LIMIT)


def swap(value, axis, mask):
    size = FINE_SIZES[FINE.index(axis)]
    return lax.ppermute(value, axis, [(i, i ^ mask) for i in range(size)])


def swap_core(value, axis, mask):
    size = FINE_SIZES[FINE.index(axis)]
    if axis == "x":
        pairs = [(i * 2 + c, (i ^ mask) * 2 + 1 - c) for i in range(size) for c in range(2)]
        return lax.ppermute(value, ("x", "core"), pairs)
    pairs = [(c * size + i, (1 - c) * size + (i ^ mask)) for i in range(size) for c in range(2)]
    return lax.ppermute(value, ("core", "y"), pairs)


def aligned(index, step):
    return pl.multiple_of(index * step, step)


def fill_positions(owner, position):
    for block in range(32):
        position[owner[block]] = block


X_MSG = 3 * FLOW + B
Y_MSG = 3 * B + B
OWN_MSG = 2 * FLOW + 2 * B + B
X_FWD = slice(2 * FLOW, 3 * FLOW + HALF)
Y_FWD = slice(2 * B, 3 * B + HALF)


def pack_kernel(owner, place, d, xb, own, core, x1c, x1s, x3c, x3s, y1c, y1s, y3c, y3s, position, sem):
    fill_positions(owner, position)
    my_x, my_core, my_y = place[1], place[2], place[3]
    copies = []

    def copy(source, first, width, target, at):
        copies.append(
            pltpu.make_async_copy(source.at[:, pl.ds(first, width)], target.at[:, pl.ds(at, width)], sem)
        )
        copies[-1].start()

    def flow_x(flow, r, core_to, target, at):
        to_x = my_x ^ r
        block = position[(flow * 4 + to_x) * 2 + core_to]
        copy(d, aligned(block, B), B, target, at)
        chunk = (2 * flow * 4) + to_x * 2 + core_to
        copy(d, pl.multiple_of(32 * B + chunk * EXTRA_CHUNK, EXTRA_CHUNK), EXTRA_CHUNK, target, at + B)

    def flow_y(flow, r, core_to, target, at):
        to_y = my_y ^ r
        for q in range(4):
            block = position[(flow * 4 + (my_x ^ q)) * 2 + core_to]
            copy(d, pl.multiple_of(block * B + to_y * 128, 128), 128, target, at + q * 128)

    def halves(target, at, order):
        for i, h in enumerate(order):
            copy(xb, h * HALF, HALF, target, at + i * HALF)

    def x_message(target, core_to, near, through):
        flow_x(0, near, core_to, target, 0)
        flow_x(1, near, core_to, target, FLOW)
        flow_x(through, 2, core_to, target, 2 * FLOW)
        halves(target, 3 * FLOW, (through, 1 - through))

    def y_message(target, core_to, near, through):
        flow_y(2, near, core_to, target, 0)
        flow_y(3, near, core_to, target, B)
        flow_y(2 + through, 2, core_to, target, 2 * B)
        halves(target, 3 * B, (through, 1 - through))

    other = 1 - my_core
    for x1, x3, y1, y3, to in ((x1c, x3c, y1c, y3c, my_core), (x1s, x3s, y1s, y3s, other)):
        x_message(x1, to, 1, 0)
        x_message(x3, to, 3, 1)
        y_message(y1, to, 1, 0)
        y_message(y3, to, 3, 1)
    for target, to in ((core, other), (own, my_core)):
        flow_x(0, 0, to, target, 0)
        flow_x(1, 0, to, target, FLOW)
        flow_y(2, 0, to, target, 2 * FLOW)
        flow_y(3, 0, to, target, 2 * FLOW + B)
        halves(target, 2 * FLOW + 2 * B, (0, 1))
    for c in copies:
        c.wait()


def pack(owner, place, d, xb):
    rows = d.shape[0]
    widths = [OWN_MSG] * 2 + [X_MSG] * 4 + [Y_MSG] * 4
    return pl.pallas_call(
        pack_kernel,
        out_shape=[jax.ShapeDtypeStruct((rows, w), jnp.bfloat16) for w in widths],
        in_specs=[SMEM, SMEM, ANY, ANY],
        out_specs=[ANY] * len(widths),
        scratch_shapes=[pltpu.SMEM((32,), jnp.int32), pltpu.SemaphoreType.DMA],
        compiler_params=PARAMS,
        name="pack",
    )(owner, place, d, xb)


def contract_rows(a, b):
    return lax.dot_general(a, b, (((0,), (0,)), ((), ())), preferred_element_type=jnp.float32)


def partial_kernel(place, own, core, x1c, x1s, x3c, x3s, y1c, y1s, y3c, y3s, f0, f1, f2, f3,
                   py0, py1, py2, py3, px0, px1, px2, px3, xs, ds, xt, dt):
    my_y = place[3]
    t = own.shape[0]
    end = 2 * FLOW + 2 * B
    for i, ref in enumerate((own, core)):
        rows = pl.ds(i * t, t)
        xs[rows, :] = ref[:, end:]
        xt[rows, :] = ref[:, end:]
        ds[rows, :] = ref[:, : 2 * FLOW]
        dt[rows, :] = ref[:, 2 * FLOW : end]
    for i, ref in enumerate((x1c, x1s, x3c, x3s)):
        rows = pl.ds((2 + i) * t, t)
        ds[rows, :] = ref[:, : 2 * FLOW]
        first = 3 * FLOW
        low, high = (first, first + HALF) if i < 2 else (first + HALF, first)
        xs[rows, :HALF] = ref[:, low : low + HALF]
        xs[rows, HALF:] = ref[:, high : high + HALF]
    for i, ref in enumerate((y1c, y1s, y3c, y3s)):
        rows = pl.ds((2 + i) * t, t)
        dt[rows, :] = ref[:, : 2 * B]
        first = 3 * B
        low, high = (first, first + HALF) if i < 2 else (first + HALF, first)
        xt[rows, :HALF] = ref[:, low : low + HALF]
        xt[rows, HALF:] = ref[:, high : high + HALF]
    rows = pl.ds(6 * t, 2 * t)
    for i, ref in enumerate((f0, f1)):
        ds[rows, i * FLOW : (i + 1) * FLOW] = ref[:, :FLOW]
        xs[rows, i * HALF : (i + 1) * HALF] = ref[:, FLOW:]
    for i, ref in enumerate((f2, f3)):
        dt[rows, i * B : (i + 1) * B] = ref[:, :B]
        xt[rows, i * HALF : (i + 1) * HALF] = ref[:, B:]
    for s, ref in enumerate((py0, py1, py2, py3)):
        features = xs[:, pl.ds(aligned(my_y ^ s, 128), 128)]
        ref[...] = contract_rows(features, ds[...]).astype(ref.dtype)
    for flow in range(2):
        product = contract_rows(xt[...], dt[:, flow * B : (flow + 1) * B])
        for q, ref in enumerate((px0, px1, px2, px3)):
            ref[:, flow * 128 : (flow + 1) * 128] = product[:, q * 128 : (q + 1) * 128].astype(ref.dtype)


def partials(place, pieces):
    t = pieces[0].shape[0]
    kinds = [jnp.float32] + [jnp.bfloat16] * 3
    return pl.pallas_call(
        partial_kernel,
        out_shape=[jax.ShapeDtypeStruct((128, 2 * FLOW), k) for k in kinds]
        + [jax.ShapeDtypeStruct((B, 256), k) for k in kinds],
        in_specs=[SMEM] + [VMEM] * len(pieces),
        out_specs=[VMEM] * 8,
        scratch_shapes=[
            pltpu.VMEM((8 * t, B), jnp.bfloat16),
            pltpu.VMEM((8 * t, 2 * FLOW), jnp.bfloat16),
            pltpu.VMEM((8 * t, B), jnp.bfloat16),
            pltpu.VMEM((8 * t, 2 * B), jnp.bfloat16),
        ],
        compiler_params=PARAMS,
        name="partials",
    )(place, *pieces)


PIECE = 80


def ring_sum_kernel(py0, ry1, ry2, ry3, px0, rx1, rx2, rx3, out):
    wide = py0[...] + ry1[...].astype(jnp.float32) + ry2[...].astype(jnp.float32) + ry3[...].astype(jnp.float32)
    tall = px0[...] + rx1[...].astype(jnp.float32) + rx2[...].astype(jnp.float32) + rx3[...].astype(jnp.float32)
    wide = wide.astype(jnp.bfloat16)
    tall = tall.astype(jnp.bfloat16)
    for z in range(4):
        for low in range(2):
            first = (z * 2 + low) * PIECE
            if z < 2:
                out[first : first + 64, :] = wide[low * 64 : low * 64 + 64, z * FLOW : z * FLOW + B]
            else:
                for g in range(4):
                    from_row = low * 256 + g * 64
                    out[first : first + 64, g * 128 : (g + 1) * 128] = tall[
                        from_row : from_row + 64, (z - 2) * 128 : (z - 1) * 128
                    ]
            k = (z * 2 + low) * 16
            for flow in range(2):
                out[first + 64 : first + PIECE, flow * 128 : (flow + 1) * 128] = wide[
                    k : k + 16, flow * FLOW + B : (flow + 1) * FLOW
                ]
            out[first + 64 : first + PIECE, 256:] = jnp.zeros((16, 256), jnp.bfloat16)


def ring_sum(parts):
    return pl.pallas_call(
        ring_sum_kernel,
        out_shape=jax.ShapeDtypeStruct((8 * PIECE, B), jnp.bfloat16),
        in_specs=[VMEM] * 8,
        out_specs=VMEM,
        compiler_params=PARAMS,
        name="ring_sum",
    )(*parts)


def root_kernel(place, own, far, r1, r2, r3, left_all, right_all, left_rows, right_rows,
                directions, left_new, right_new, g0, g1, a_ref, m_ref):
    my_z, my_y, my_low = place[0], place[3], place[4]
    node = my_y * 2 + my_low
    first_row = aligned(node, 64)
    for r in range(4):
        at_y = my_y ^ r
        for w in range(2):
            at_low = my_low ^ w
            if r == 0:
                piece, base = (own, far)[w], 0
            else:
                piece, base = (r1, r2, r3)[r - 1], w * 128

            @pl.when(my_z < 2)
            def _():
                g0[pl.ds(pl.multiple_of(at_y * 128 + at_low * 64, 64), 64), :] = piece[base : base + 64, :]

            @pl.when(my_z >= 2)
            def _():
                for g in range(4):
                    g0[
                        pl.ds(pl.multiple_of(at_low * 256 + g * 64, 64), 64),
                        pl.ds(aligned(at_y, 128), 128),
                    ] = piece[base : base + 64, g * 128 : (g + 1) * 128]

            for z in range(4):
                g1[pl.ds(pl.multiple_of(at_y * 128 + (z * 2 + at_low) * 16, 16), 16), :] = piece[
                    base + 64 + z * 16 : base + 64 + (z + 1) * 16, :
                ]

    def scaled(gram, statistic, old_rows, new_rows, slot, which):
        a_ref[which] = gram
        rows = a_ref[which, pl.ds(first_row, 64), :]
        new_rows[slot] = BETA * old_rows[slot] + rows * (1.0 / B)
        full = BETA * statistic[slot].astype(jnp.float32) + gram * (1.0 / B)
        norm = B * jnp.sqrt(jnp.sum(full * full, keepdims=True) * (1.0 / (B * B)) + 1e-06)
        matrix = full / norm
        a_ref[which] = matrix
        m_ref[which] = matrix.astype(jnp.bfloat16)
        return lax.rsqrt(jnp.sqrt(norm))

    for slot, g_ref in enumerate((g0, g1)):
        g = g_ref[...]
        left_gram = lax.dot_general(g, g, (((1,), (1,)), ((), ())), preferred_element_type=jnp.float32)
        right_gram = contract_rows(g, g)
        left_scale = scaled(left_gram, left_all, left_rows, left_new, slot, 0)
        right_scale = scaled(right_gram, right_all, right_rows, right_new, slot, 1)
        power = a_ref[0, pl.ds(first_row, 64), :]
        column = lax.broadcasted_iota(jnp.int32, (64, B), 1)
        row = lax.broadcasted_iota(jnp.int32, (64, B), 0) + first_row
        total = jnp.where(row == column, COEF[0], 0.0) + COEF[1] * power
        for k in range(2, 7):
            power = jnp.dot(power.astype(jnp.bfloat16), m_ref[0], preferred_element_type=jnp.float32)
            total = total + COEF[k] * power
        root = (total * left_scale).astype(jnp.bfloat16)
        half = jnp.dot(root, g, preferred_element_type=jnp.float32).astype(jnp.bfloat16)
        power = half.astype(jnp.float32)
        total = COEF[0] * power
        for k in range(1, 7):
            power = jnp.dot(power.astype(jnp.bfloat16), m_ref[1], preferred_element_type=jnp.float32)
            total = total + COEF[k] * power
        directions[slot * 64 : (slot + 1) * 64, :] = (total * right_scale).astype(jnp.bfloat16)


def roots(place, pieces, left_all, right_all, left_rows, right_rows):
    return pl.pallas_call(
        root_kernel,
        out_shape=[
            jax.ShapeDtypeStruct((SLOTS * 64, B), jnp.bfloat16),
            jax.ShapeDtypeStruct((SLOTS, 64, B), jnp.float32),
            jax.ShapeDtypeStruct((SLOTS, 64, B), jnp.float32),
        ],
        in_specs=[SMEM] + [VMEM] * 9,
        out_specs=[VMEM] * 3,
        scratch_shapes=[
            pltpu.VMEM((B, B), jnp.bfloat16),
            pltpu.VMEM((B, B), jnp.bfloat16),
            pltpu.VMEM((2, B, B), jnp.float32),
            pltpu.VMEM((2, B, B), jnp.bfloat16),
        ],
        compiler_params=PARAMS,
        name="roots",
    )(place, *pieces, left_all, right_all, left_rows, right_rows)


def place_kernel(owner, place, *refs):
    sources, out, position, sem = refs[:8], refs[8], refs[9], refs[10]
    fill_positions(owner, position)
    my_z, my_x, my_core = place[0], place[1], place[2]
    for wait in (False, True):
        for flip in range(2):
            for r in range(4):
                source = sources[flip * 4 + r]
                for a in range(4):
                    who = ((my_z ^ a) * 4 + (my_x ^ r)) * 2 + (my_core ^ flip)
                    block = position[who]
                    for slot in range(SLOTS):
                        copy = pltpu.make_async_copy(
                            source.at[pl.ds(a * 128 + slot * 64, 64), :],
                            out.at[:, pl.ds(aligned(jnp.minimum(block + slot * 32, 35), B), B)],
                            sem,
                        )
                        act = copy.wait if wait else copy.start
                        if slot == 0:
                            act()
                        else:
                            pl.when(block < 4)(act)


def put_blocks(owner, place, sources, blocks):
    return pl.pallas_call(
        place_kernel,
        out_shape=jax.ShapeDtypeStruct((64, blocks * B), jnp.bfloat16),
        in_specs=[SMEM, SMEM] + [ANY] * 8,
        out_specs=ANY,
        scratch_shapes=[pltpu.SMEM((32,), jnp.int32), pltpu.SemaphoreType.DMA],
        compiler_params=PARAMS,
        name="put_blocks",
    )(owner, place, *sources)


def shards(x_band, d_gate_up, owner, stat_left, stat_right):
    place = jnp.stack([lax.axis_index(a) for a in FINE]).astype(jnp.int32)
    bucket = d_gate_up.shape[1] // B
    me = lax.axis_index(("z_hi", "x", "core"))
    node_axes = ("y", "z_lo")

    left_all = lax.all_gather(stat_left[0].astype(jnp.bfloat16), node_axes, axis=1, tiled=True)
    right_all = lax.all_gather(stat_right[0].astype(jnp.bfloat16), node_axes, axis=1, tiled=True)

    own, core, x1c, x1s, x3c, x3s, y1c, y1s, y3c, y3s = pack(owner, place, d_gate_up, x_band)
    x1c, x3c = swap(x1c, "x", 1), swap(x3c, "x", 3)
    y1c, y3c = swap(y1c, "y", 1), swap(y3c, "y", 3)
    x1s, x3s = swap_core(x1s, "x", 1), swap_core(x3s, "x", 3)
    y1s, y3s = swap_core(y1s, "y", 1), swap_core(y3s, "y", 3)
    core = swap(core, "core", 1)
    f0 = swap(jnp.concatenate([x1c[:, X_FWD], x1s[:, X_FWD]]), "x", 3)
    f1 = swap(jnp.concatenate([x3c[:, X_FWD], x3s[:, X_FWD]]), "x", 1)
    f2 = swap(jnp.concatenate([y1c[:, Y_FWD], y1s[:, Y_FWD]]), "y", 3)
    f3 = swap(jnp.concatenate([y3c[:, Y_FWD], y3s[:, Y_FWD]]), "y", 1)
    py0, py1, py2, py3, px0, px1, px2, px3 = partials(
        place, (own, core, x1c, x1s, x3c, x3s, y1c, y1s, y3c, y3s, f0, f1, f2, f3)
    )
    ry2, rx2 = swap(py2, "y", 2), swap(px2, "x", 2)
    ry1, rx1 = swap(py1, "y", 1), swap(px1, "x", 1)
    ry3, rx3 = swap(py3, "y", 3), swap(px3, "x", 3)
    message = ring_sum((py0, ry1, ry2, ry3, px0, rx1, rx2, rx3))
    message = lax.all_to_all(message, ("z_hi", "z_lo"), 0, 0, tiled=True)
    summed = jnp.sum(message.reshape(8, PIECE, B).astype(jnp.float32), axis=0).astype(jnp.bfloat16)

    spread = jnp.broadcast_to(summed[64:, :256][None], (32, 16, 256)).reshape(512, 256)
    spread = lax.all_to_all(spread, ("z_hi", "x", "core"), 0, 0, tiled=True)
    mine = jnp.sum(jnp.where(owner[:32] == me, jnp.arange(32, dtype=jnp.int32), 0))
    extra = jnp.minimum(mine, bucket - 33)
    spread = spread.reshape(4, 2, 2, 2, 16, 2, 128)
    chosen = lax.dynamic_slice(spread, (0, extra % 2, 0, 0, 0, extra // 2, 0), (4, 1, 2, 2, 16, 1, 128))
    chosen = chosen.reshape(4, 2, 2, 16, 128).transpose(0, 3, 1, 2, 4).reshape(64, B)
    chosen = jnp.where(mine < bucket - 32, chosen, jnp.zeros_like(chosen))

    mine_rows = jnp.concatenate([summed[:64], chosen])
    far = swap(mine_rows, "z_lo", 1)
    both = jnp.concatenate([mine_rows, far])
    r2, r1, r3 = swap(both, "y", 2), swap(both, "y", 1), swap(both, "y", 3)
    directions, left_new, right_new = roots(
        place, (mine_rows, far, r1, r2, r3), left_all, right_all, stat_left[0], stat_right[0]
    )
    a2, a1, a3 = swap(directions, "z_hi", 2), swap(directions, "z_hi", 1), swap(directions, "z_hi", 3)
    plane = jnp.concatenate([directions, a1, a2, a3])
    b2, b1, b3 = swap(plane, "x", 2), swap(plane, "x", 1), swap(plane, "x", 3)
    near = (plane, b1, b2, b3)
    across = tuple(swap(v, "core", 1) for v in near)
    out = put_blocks(owner, place, near + across, bucket)
    return (out, left_new[None], right_new[None])


def solution(mesh):
    fine = Mesh(np.asarray(mesh.devices).reshape(FINE_SIZES), FINE)
    dp, node = FINE[:3], FINE[3:]
    placed = (P(dp + node, None), P(dp + node, None), P(), P(dp, None, node, None), P(dp, None, node, None))
    return jax.shard_map(
        shards,
        mesh=fine,
        in_specs=placed,
        out_specs=(P(node, None), P(dp, None, node, None), P(dp, None, node, None)),
        check_vma=False,
    )
```

```python
import functools
import math

import jax
import jax.numpy as jnp
import numpy as np
from jax import lax
from jax.experimental import pallas as pl
from jax.experimental.pallas import tpu as pltpu
from jax.sharding import Mesh, PartitionSpec as P

B = 512
SLOTS = 2
BETA = 0.9
EXTRA_CHUNK = 128
FLOW = B + EXTRA_CHUNK
HALF = B // 2

FINE = ("z_hi", "x", "core", "y", "z_lo")
FINE_SIZES = (4, 4, 2, 4, 2)
VMEM_LIMIT = 24 * 1024 * 1024

COEF = [6.25 / 4, -(1.25 + 1.25**5) / 4] + [
    -math.comb(5, k) * 1.25 ** (5 - k) * (-0.25) ** k / 4 for k in range(1, 6)
]

ANY = pl.BlockSpec(memory_space=pl.ANY)
SMEM = pl.BlockSpec(memory_space=pltpu.SMEM)
VMEM = pl.BlockSpec(memory_space=pltpu.VMEM)
PARAMS = pltpu.CompilerParams(vmem_limit_bytes=VMEM_LIMIT)


def swap(value, axis, mask):
    size = FINE_SIZES[FINE.index(axis)]
    return lax.ppermute(value, axis, [(i, i ^ mask) for i in range(size)])


def aligned(index, step):
    return pl.multiple_of(index * step, step)


def fill_positions(owner, position):
    for block in range(32):
        position[owner[block]] = block


X_DIRECT = 4 * FLOW
X_MSG = 6 * FLOW + B
Y_DIRECT = 4 * B
Y_MSG = 6 * B + B
OWN_MSG = 4 * FLOW + 4 * B
X_FWD = slice(X_DIRECT, 6 * FLOW + HALF)
Y_FWD = slice(Y_DIRECT, 6 * B + HALF)


class Packer:
    def __init__(self, owner, place, d, position, sem):
        fill_positions(owner, position)
        self.position, self.place, self.d, self.sem = position, place, d, sem
        self.cores = (place[2], 1 - place[2])
        self.copies = []

    def copy(self, source, first, width, target, at):
        self.copies.append(
            pltpu.make_async_copy(source.at[:, pl.ds(first, width)], target.at[:, pl.ds(at, width)], self.sem)
        )
        self.copies[-1].start()

    def flow_x(self, flow, r, core, target, at):
        to_x = self.place[1] ^ r
        block = self.position[(flow * 4 + to_x) * 2 + core]
        self.copy(self.d, aligned(block, B), B, target, at)
        chunk = 32 * B // EXTRA_CHUNK + flow * 8 + to_x * 2 + core
        self.copy(self.d, aligned(chunk, EXTRA_CHUNK), EXTRA_CHUNK, target, at + B)

    def flow_y(self, flow, r, core, target, at):
        to_y = self.place[3] ^ r
        for q in range(4):
            block = self.position[(flow * 4 + (self.place[1] ^ q)) * 2 + core]
            self.copy(self.d, pl.multiple_of(block * B + to_y * 128, 128), 128, target, at + q * 128)

    def finish(self):
        for c in self.copies:
            c.wait()


def pack_kernel(owner, place, d, xb, x1, x3, y1, y3, position, sem):
    packer = Packer(owner, place, d, position, sem)
    for near, through, on_x, on_y in ((1, 0, x1, y1), (3, 1, x3, y3)):
        for i, core in enumerate(packer.cores):
            packer.flow_x(0, near, core, on_x, i * 2 * FLOW)
            packer.flow_x(1, near, core, on_x, i * 2 * FLOW + FLOW)
            packer.flow_x(through, 2, core, on_x, X_DIRECT + i * FLOW)
            packer.flow_y(2, near, core, on_y, i * 2 * B)
            packer.flow_y(3, near, core, on_y, i * 2 * B + B)
            packer.flow_y(2 + through, 2, core, on_y, Y_DIRECT + i * B)
        for i, h in enumerate((through, 1 - through)):
            packer.copy(xb, h * HALF, HALF, on_x, 6 * FLOW + i * HALF)
            packer.copy(xb, h * HALF, HALF, on_y, 6 * B + i * HALF)
    packer.finish()


def pack_own_kernel(owner, place, d, out, position, sem):
    packer = Packer(owner, place, d, position, sem)
    for i, core in enumerate(packer.cores):
        for flow in range(2):
            packer.flow_x(flow, 0, core, out, (i * 2 + flow) * FLOW)
            packer.flow_y(2 + flow, 0, core, out, 4 * FLOW + (i * 2 + flow) * B)
    packer.finish()


def packed(kernel, name, widths, owner, place, d, *more):
    rows = d.shape[0]
    return pl.pallas_call(
        kernel,
        out_shape=[jax.ShapeDtypeStruct((rows, w), jnp.bfloat16) for w in widths],
        in_specs=[SMEM, SMEM, ANY] + [ANY] * len(more),
        out_specs=[VMEM] * len(widths),
        scratch_shapes=[pltpu.SMEM((32,), jnp.int32), pltpu.SemaphoreType.DMA],
        compiler_params=PARAMS,
        name=name,
    )(owner, place, d, *more)


def contract_rows(a, b):
    return lax.dot_general(a, b, (((0,), (0,)), ((), ())), preferred_element_type=jnp.float32)


def partial_kernel(which, own, xb, x1, x3, y1, y3, f0, f1, f2, f3, wide, tall, xs, ds, xt, dt):
    t = own.shape[0]
    wide_at = which * 2 * FLOW
    tall_at = which * 2 * B
    rows = pl.ds(0, t)
    xs[rows, :] = xb[...]
    xt[rows, :] = xb[...]
    ds[rows, :] = own[:, wide_at : wide_at + 2 * FLOW]
    dt[rows, :] = own[:, 4 * FLOW + tall_at : 4 * FLOW + tall_at + 2 * B]
    for i, (on_x, on_y) in enumerate(((x1, y1), (x3, y3))):
        rows = pl.ds((1 + i) * t, t)
        ds[rows, :] = on_x[:, wide_at : wide_at + 2 * FLOW]
        dt[rows, :] = on_y[:, tall_at : tall_at + 2 * B]
        for k, h in enumerate((i, 1 - i)):
            xs[rows, h * HALF : (h + 1) * HALF] = on_x[:, 6 * FLOW + k * HALF : 6 * FLOW + (k + 1) * HALF]
            xt[rows, h * HALF : (h + 1) * HALF] = on_y[:, 6 * B + k * HALF : 6 * B + (k + 1) * HALF]
    rows = pl.ds(3 * t, t)
    for i, (on_x, on_y) in enumerate(((f0, f2), (f1, f3))):
        ds[rows, i * FLOW : (i + 1) * FLOW] = on_x[:, which * FLOW : (which + 1) * FLOW]
        dt[rows, i * B : (i + 1) * B] = on_y[:, which * B : (which + 1) * B]
        xs[rows, i * HALF : (i + 1) * HALF] = on_x[:, 2 * FLOW :]
        xt[rows, i * HALF : (i + 1) * HALF] = on_y[:, 2 * B :]
    wide[...] = contract_rows(xs[...], ds[...]).astype(wide.dtype)
    tall[...] = contract_rows(xt[...], dt[...]).astype(tall.dtype)


def partials(which, pieces):
    t = pieces[0].shape[0]
    return pl.pallas_call(
        functools.partial(partial_kernel, which),
        out_shape=[
            jax.ShapeDtypeStruct((B, 2 * FLOW), jnp.bfloat16),
            jax.ShapeDtypeStruct((B, 2 * B), jnp.bfloat16),
        ],
        in_specs=[VMEM] * len(pieces),
        out_specs=[VMEM] * 2,
        scratch_shapes=[
            pltpu.VMEM((4 * t, B), jnp.bfloat16),
            pltpu.VMEM((4 * t, 2 * FLOW), jnp.bfloat16),
            pltpu.VMEM((4 * t, B), jnp.bfloat16),
            pltpu.VMEM((4 * t, 2 * B), jnp.bfloat16),
        ],
        compiler_params=PARAMS,
        name="partials",
    )(*pieces)


def chip_sum_kernel(place, wide, tall, far_wide, far_tall, py0, py1, py2, py3, px0, px1, px2, px3):
    my_y = place[3]
    for s, ref in enumerate((py0, py1, py2, py3)):
        rows = pl.ds(aligned(my_y ^ s, 128), 128)
        ref[...] = (wide[rows, :].astype(jnp.float32) + far_wide[rows, :].astype(jnp.float32)).astype(ref.dtype)
    for q, ref in enumerate((px0, px1, px2, px3)):
        for flow in range(2):
            at = flow * B + q * 128
            ref[:, flow * 128 : (flow + 1) * 128] = (
                tall[:, at : at + 128].astype(jnp.float32) + far_tall[:, at : at + 128].astype(jnp.float32)
            ).astype(ref.dtype)


def chip_sum(place, *parts):
    kinds = [jnp.float32] + [jnp.bfloat16] * 3
    return pl.pallas_call(
        chip_sum_kernel,
        out_shape=[jax.ShapeDtypeStruct((128, 2 * FLOW), k) for k in kinds]
        + [jax.ShapeDtypeStruct((B, 256), k) for k in kinds],
        in_specs=[SMEM] + [VMEM] * 4,
        out_specs=[VMEM] * 8,
        compiler_params=PARAMS,
        name="chip_sum",
    )(place, *parts)


PIECE = 80


def ring_sum_kernel(py0, ry1, ry2, ry3, px0, rx1, rx2, rx3, out):
    wide = py0[...] + ry1[...].astype(jnp.float32) + ry2[...].astype(jnp.float32) + ry3[...].astype(jnp.float32)
    tall = px0[...] + rx1[...].astype(jnp.float32) + rx2[...].astype(jnp.float32) + rx3[...].astype(jnp.float32)
    wide = wide.astype(jnp.bfloat16)
    tall = tall.astype(jnp.bfloat16)
    for z in range(4):
        for low in range(2):
            first = (z * 2 + low) * PIECE
            if z < 2:
                out[first : first + 64, :] = wide[low * 64 : low * 64 + 64, z * FLOW : z * FLOW + B]
            else:
                for g in range(4):
                    from_row = low * 256 + g * 64
                    out[first : first + 64, g * 128 : (g + 1) * 128] = tall[
                        from_row : from_row + 64, (z - 2) * 128 : (z - 1) * 128
                    ]
            k = (z * 2 + low) * 16
            for flow in range(2):
                out[first + 64 : first + PIECE, flow * 128 : (flow + 1) * 128] = wide[
                    k : k + 16, flow * FLOW + B : (flow + 1) * FLOW
                ]
            out[first + 64 : first + PIECE, 256:] = jnp.zeros((16, 256), jnp.bfloat16)


def ring_sum(parts):
    return pl.pallas_call(
        ring_sum_kernel,
        out_shape=jax.ShapeDtypeStruct((8 * PIECE, B), jnp.bfloat16),
        in_specs=[VMEM] * 8,
        out_specs=VMEM,
        compiler_params=PARAMS,
        name="ring_sum",
    )(*parts)


def line_sum_kernel(arrived, main, spread):
    total = arrived[0].astype(jnp.float32)
    for i in range(1, 8):
        total = total + arrived[i].astype(jnp.float32)
    total = total.astype(jnp.bfloat16)
    main[...] = total[:64]
    for i in range(64):
        spread[i * 16 : (i + 1) * 16, :] = total[64:, :256]


def line_sum(arrived):
    return pl.pallas_call(
        line_sum_kernel,
        out_shape=[jax.ShapeDtypeStruct((64, B), jnp.bfloat16), jax.ShapeDtypeStruct((64 * 16, 256), jnp.bfloat16)],
        in_specs=[VMEM],
        out_specs=[VMEM] * 2,
        compiler_params=PARAMS,
        name="line_sum",
    )(arrived)


def choose_kernel(owner, place, main, far, spread, out, position):
    fill_positions(owner, position)
    mine = position[(place[0] * 4 + place[1]) * 2 + place[2]]
    out[:64, :] = main[...]
    out[64:128, :] = far[...]

    @pl.when(mine >= 4)
    def _():
        out[128:, :] = jnp.zeros((128, B), jnp.bfloat16)

    @pl.when(mine < 4)
    def _():
        lanes = pl.ds(aligned(mine >> 1, 128), 128)
        for z in range(4):
            for xl in range(2):
                for core in range(2):
                    for low in range(2):
                        source = (((z * 4 + 2 * (mine & 1) + xl) * 2 + core) * 2 + low) * 16
                        to = 128 + low * 64 + z * 16
                        at = (xl * 2 + core) * 128
                        out[to : to + 16, at : at + 128] = spread[pl.ds(pl.multiple_of(source, 16), 16), lanes]


def choose(owner, place, main, far, spread):
    return pl.pallas_call(
        choose_kernel,
        out_shape=jax.ShapeDtypeStruct((256, B), jnp.bfloat16),
        in_specs=[SMEM, SMEM] + [VMEM] * 3,
        out_specs=VMEM,
        scratch_shapes=[pltpu.SMEM((32,), jnp.int32)],
        compiler_params=PARAMS,
        name="choose",
    )(owner, place, main, far, spread)


def root_kernel(place, r0, r1, r2, r3, statistics, left_rows, right_rows,
                directions, left_new, right_new, g0, g1, a_ref, m_ref):
    my_z, my_y, my_low = place[0], place[3], place[4]
    node = my_y * 2 + my_low
    first_row = aligned(node, 64)
    for r, piece in enumerate((r0, r1, r2, r3)):
        at_y = my_y ^ r
        for w in range(2):
            at_low = my_low ^ w
            base = w * 64

            @pl.when(my_z < 2)
            def _():
                g0[pl.ds(pl.multiple_of(at_y * 128 + at_low * 64, 64), 64), :] = piece[base : base + 64, :]

            @pl.when(my_z >= 2)
            def _():
                for g in range(4):
                    g0[
                        pl.ds(pl.multiple_of(at_low * 256 + g * 64, 64), 64),
                        pl.ds(aligned(at_y, 128), 128),
                    ] = piece[base : base + 64, g * 128 : (g + 1) * 128]

            for z in range(4):
                g1[pl.ds(pl.multiple_of(at_y * 128 + (z * 2 + w) * 16, 16), 16), :] = piece[
                    128 + w * 64 + z * 16 : 128 + w * 64 + (z + 1) * 16, :
                ]

    def scaled(gram, old_rows, new_rows, slot, which):
        a_ref[which] = gram
        rows = a_ref[which, pl.ds(first_row, 64), :]
        new_rows[slot] = BETA * old_rows[slot] + rows * (1.0 / B)
        full = BETA * statistics[which * SLOTS + slot].astype(jnp.float32) + gram * (1.0 / B)
        norm = B * jnp.sqrt(jnp.sum(full * full, keepdims=True) * (1.0 / (B * B)) + 1e-06)
        matrix = full / norm
        a_ref[which] = matrix
        m_ref[which] = matrix.astype(jnp.bfloat16)
        return lax.rsqrt(jnp.sqrt(norm))

    for slot, g_ref in enumerate((g0, g1)):
        g = g_ref[...]
        left_gram = lax.dot_general(g, g, (((1,), (1,)), ((), ())), preferred_element_type=jnp.float32)
        right_gram = contract_rows(g, g)
        left_scale = scaled(left_gram, left_rows, left_new, slot, 0)
        right_scale = scaled(right_gram, right_rows, right_new, slot, 1)
        power = a_ref[0, pl.ds(first_row, 64), :]
        column = lax.broadcasted_iota(jnp.int32, (64, B), 1)
        row = lax.broadcasted_iota(jnp.int32, (64, B), 0) + first_row
        total = jnp.where(row == column, COEF[0], 0.0) + COEF[1] * power
        for k in range(2, 7):
            power = jnp.dot(power.astype(jnp.bfloat16), m_ref[0], preferred_element_type=jnp.float32)
            total = total + COEF[k] * power
        root = (total * left_scale).astype(jnp.bfloat16)
        half = jnp.dot(root, g, preferred_element_type=jnp.float32).astype(jnp.bfloat16)
        power = half.astype(jnp.float32)
        total = COEF[0] * power
        for k in range(1, 7):
            power = jnp.dot(power.astype(jnp.bfloat16), m_ref[1], preferred_element_type=jnp.float32)
            total = total + COEF[k] * power
        directions[slot * 64 : (slot + 1) * 64, :] = (total * right_scale).astype(jnp.bfloat16)


def roots(place, pieces, statistics, left_rows, right_rows):
    return pl.pallas_call(
        root_kernel,
        out_shape=[
            jax.ShapeDtypeStruct((SLOTS * 64, B), jnp.bfloat16),
            jax.ShapeDtypeStruct((SLOTS, 64, B), jnp.float32),
            jax.ShapeDtypeStruct((SLOTS, 64, B), jnp.float32),
        ],
        in_specs=[SMEM] + [VMEM] * 7,
        out_specs=[VMEM] * 3,
        scratch_shapes=[
            pltpu.VMEM((B, B), jnp.bfloat16),
            pltpu.VMEM((B, B), jnp.bfloat16),
            pltpu.VMEM((2, B, B), jnp.float32),
            pltpu.VMEM((2, B, B), jnp.bfloat16),
        ],
        compiler_params=PARAMS,
        name="roots",
    )(place, *pieces, statistics, left_rows, right_rows)


def place_kernel(owner, place, *refs):
    sources, out, position, sem = refs[:8], refs[8], refs[9], refs[10]
    fill_positions(owner, position)
    my_z, my_x, my_core = place[0], place[1], place[2]
    for wait in (False, True):
        for flip in range(2):
            for r in range(4):
                source = sources[flip * 4 + r]
                for a in range(4):
                    who = ((my_z ^ a) * 4 + (my_x ^ r)) * 2 + (my_core ^ flip)
                    block = position[who]
                    for slot in range(SLOTS):
                        copy = pltpu.make_async_copy(
                            source.at[pl.ds(a * 128 + slot * 64, 64), :],
                            out.at[:, pl.ds(aligned(jnp.minimum(block + slot * 32, 35), B), B)],
                            sem,
                        )
                        act = copy.wait if wait else copy.start
                        if slot == 0:
                            act()
                        else:
                            pl.when(block < 4)(act)


def put_blocks(owner, place, sources, blocks):
    return pl.pallas_call(
        place_kernel,
        out_shape=jax.ShapeDtypeStruct((64, blocks * B), jnp.bfloat16),
        in_specs=[SMEM, SMEM] + [ANY] * 8,
        out_specs=ANY,
        scratch_shapes=[pltpu.SMEM((32,), jnp.int32), pltpu.SemaphoreType.DMA],
        compiler_params=PARAMS,
        name="put_blocks",
    )(owner, place, *sources)


def shards(x_band, d_gate_up, owner, stat_left, stat_right):
    place = jnp.stack([lax.axis_index(a) for a in FINE]).astype(jnp.int32)
    bucket = d_gate_up.shape[1] // B
    statistics = jnp.concatenate([stat_left[0], stat_right[0]]).astype(jnp.bfloat16)
    statistics = lax.all_gather(statistics, ("y", "z_lo"), axis=1, tiled=True)

    x1, x3, y1, y3 = packed(pack_kernel, "pack", [X_MSG] * 2 + [Y_MSG] * 2, owner, place, d_gate_up, x_band)
    x1, x3, y1, y3 = swap(x1, "x", 1), swap(x3, "x", 3), swap(y1, "y", 1), swap(y3, "y", 3)
    (own,) = packed(pack_own_kernel, "pack_own", [OWN_MSG], owner, place, d_gate_up)
    f0, f1 = swap(x1[:, X_FWD], "x", 3), swap(x3[:, X_FWD], "x", 1)
    f2, f3 = swap(y1[:, Y_FWD], "y", 3), swap(y3[:, Y_FWD], "y", 1)
    pieces = (own, x_band, x1, x3, y1, y3, f0, f1, f2, f3)
    wide, tall = partials(1, pieces)
    far_wide, far_tall = swap(wide, "core", 1), swap(tall, "core", 1)
    wide, tall = partials(0, pieces)
    py0, py1, py2, py3, px0, px1, px2, px3 = chip_sum(place, wide, tall, far_wide, far_tall)
    ry2, rx2 = swap(py2, "y", 2), swap(px2, "x", 2)
    ry1, rx1 = swap(py1, "y", 1), swap(px1, "x", 1)
    ry3, rx3 = swap(py3, "y", 3), swap(px3, "x", 3)
    message = ring_sum((py0, ry1, ry2, ry3, px0, rx1, rx2, rx3))
    message, statistics = lax.optimization_barrier((message, statistics))
    message = lax.all_to_all(message, ("z_hi", "z_lo"), 0, 0, tiled=True)
    main, spread = line_sum(message.reshape(8, PIECE, B))

    far = swap(main, "z_lo", 1)
    spread = lax.all_to_all(spread, ("z_hi", "x", "core", "z_lo"), 0, 0, tiled=True)
    both = choose(owner, place, main, far, spread)
    r2, r1, r3 = swap(both, "y", 2), swap(both, "y", 1), swap(both, "y", 3)
    directions, left_new, right_new = roots(place, (both, r1, r2, r3), statistics, stat_left[0], stat_right[0])
    a2, a1, a3 = swap(directions, "z_hi", 2), swap(directions, "z_hi", 1), swap(directions, "z_hi", 3)
    plane = jnp.concatenate([directions, a1, a2, a3])
    b2, b1, b3 = swap(plane, "x", 2), swap(plane, "x", 1), swap(plane, "x", 3)
    near = (plane, b1, b2, b3)
    across = tuple(swap(v, "core", 1) for v in near)
    out = put_blocks(owner, place, near + across, bucket)
    return (out, left_new[None], right_new[None])


def solution(mesh):
    fine = Mesh(np.asarray(mesh.devices).reshape(FINE_SIZES), FINE)
    dp, node = FINE[:3], FINE[3:]
    placed = (P(dp + node, None), P(dp + node, None), P(), P(dp, None, node, None), P(dp, None, node, None))
    return jax.shard_map(
        shards,
        mesh=fine,
        in_specs=placed,
        out_specs=(P(node, None), P(dp, None, node, None), P(dp, None, node, None)),
        check_vma=False,
    )
```

```python
import functools
import math

import jax
import jax.numpy as jnp
import numpy as np
from jax import lax
from jax.experimental import pallas as pl
from jax.experimental.pallas import tpu as pltpu
from jax.sharding import Mesh, PartitionSpec as P

B = 512
SLOTS = 2
BETA = 0.9
EXTRA_CHUNK = 128
FLOW = B + EXTRA_CHUNK
HALF = B // 2

FINE = ("z_hi", "x", "core", "y", "z_lo")
FINE_SIZES = (4, 4, 2, 4, 2)
VMEM_LIMIT = 24 * 1024 * 1024

COEF = [6.25 / 4, -(1.25 + 1.25**5) / 4] + [
    -math.comb(5, k) * 1.25 ** (5 - k) * (-0.25) ** k / 4 for k in range(1, 6)
]

ANY = pl.BlockSpec(memory_space=pl.ANY)
HBM = pl.BlockSpec(memory_space=pltpu.HBM)
SMEM = pl.BlockSpec(memory_space=pltpu.SMEM)
VMEM = pl.BlockSpec(memory_space=pltpu.VMEM)
PARAMS = pltpu.CompilerParams(vmem_limit_bytes=VMEM_LIMIT)


def swap(value, axis, mask):
    size = FINE_SIZES[FINE.index(axis)]
    return lax.ppermute(value, axis, [(i, i ^ mask) for i in range(size)])


def aligned(index, step):
    return pl.multiple_of(index * step, step)


def fill_positions(owner, position):
    for block in range(32):
        position[owner[block]] = block


X_DIRECT = 4 * FLOW
X_MSG = 6 * FLOW + B
Y_DIRECT = 4 * B
Y_MSG = 6 * B + B
OWN_MSG = 4 * FLOW + 4 * B
X_FWD = slice(X_DIRECT, 6 * FLOW + HALF)
Y_FWD = slice(Y_DIRECT, 6 * B + HALF)


class Packer:
    def __init__(self, owner, place, d, position, sem):
        fill_positions(owner, position)
        self.position, self.place, self.d, self.sem = position, place, d, sem
        self.cores = (place[2], 1 - place[2])
        self.copies = []

    def copy(self, source, first, width, target, at):
        self.copies.append(
            pltpu.make_async_copy(source.at[:, pl.ds(first, width)], target.at[:, pl.ds(at, width)], self.sem)
        )
        self.copies[-1].start()

    def flow_x(self, flow, r, core, target, at):
        to_x = self.place[1] ^ r
        block = self.position[(flow * 4 + to_x) * 2 + core]
        self.copy(self.d, aligned(block, B), B, target, at)
        chunk = 32 * B // EXTRA_CHUNK + flow * 8 + to_x * 2 + core
        self.copy(self.d, aligned(chunk, EXTRA_CHUNK), EXTRA_CHUNK, target, at + B)

    def flow_y(self, flow, r, core, target, at):
        to_y = self.place[3] ^ r
        for q in range(4):
            block = self.position[(flow * 4 + (self.place[1] ^ q)) * 2 + core]
            self.copy(self.d, pl.multiple_of(block * B + to_y * 128, 128), 128, target, at + q * 128)

    def finish(self):
        for c in self.copies:
            c.wait()


def pack_kernel(owner, place, d, xb, x1, x3, y1, y3, position, sem):
    packer = Packer(owner, place, d, position, sem)
    for near, through, on_x, on_y in ((1, 0, x1, y1), (3, 1, x3, y3)):
        for i, core in enumerate(packer.cores):
            packer.flow_x(0, near, core, on_x, i * 2 * FLOW)
            packer.flow_x(1, near, core, on_x, i * 2 * FLOW + FLOW)
            packer.flow_x(through, 2, core, on_x, X_DIRECT + i * FLOW)
            packer.flow_y(2, near, core, on_y, i * 2 * B)
            packer.flow_y(3, near, core, on_y, i * 2 * B + B)
            packer.flow_y(2 + through, 2, core, on_y, Y_DIRECT + i * B)
        for i, h in enumerate((through, 1 - through)):
            packer.copy(xb, h * HALF, HALF, on_x, 6 * FLOW + i * HALF)
            packer.copy(xb, h * HALF, HALF, on_y, 6 * B + i * HALF)
    packer.finish()


def pack_own_kernel(owner, place, d, out, position, sem):
    packer = Packer(owner, place, d, position, sem)
    for i, core in enumerate(packer.cores):
        for flow in range(2):
            packer.flow_x(flow, 0, core, out, (i * 2 + flow) * FLOW)
            packer.flow_y(2 + flow, 0, core, out, 4 * FLOW + (i * 2 + flow) * B)
    packer.finish()


def packed(kernel, name, widths, owner, place, d, *more):
    rows = d.shape[0]
    return pl.pallas_call(
        kernel,
        out_shape=[jax.ShapeDtypeStruct((rows, w), jnp.bfloat16) for w in widths],
        in_specs=[SMEM, SMEM, HBM] + [ANY] * len(more),
        out_specs=[VMEM] * len(widths),
        scratch_shapes=[pltpu.SMEM((32,), jnp.int32), pltpu.SemaphoreType.DMA],
        compiler_params=PARAMS,
        name=name,
    )(owner, place, d, *more)


def contract_rows(a, b):
    return lax.dot_general(a, b, (((0,), (0,)), ((), ())), preferred_element_type=jnp.float32)


def partial_kernel(which, own, xb, x1, x3, y1, y3, f0, f1, f2, f3, wide, tall, xs, ds, xt, dt):
    t = own.shape[0]
    wide_at = which * 2 * FLOW
    tall_at = which * 2 * B
    rows = pl.ds(0, t)
    xs[rows, :] = xb[...]
    xt[rows, :] = xb[...]
    ds[rows, :] = own[:, wide_at : wide_at + 2 * FLOW]
    dt[rows, :] = own[:, 4 * FLOW + tall_at : 4 * FLOW + tall_at + 2 * B]
    for i, (on_x, on_y) in enumerate(((x1, y1), (x3, y3))):
        rows = pl.ds((1 + i) * t, t)
        ds[rows, :] = on_x[:, wide_at : wide_at + 2 * FLOW]
        dt[rows, :] = on_y[:, tall_at : tall_at + 2 * B]
        for k, h in enumerate((i, 1 - i)):
            xs[rows, h * HALF : (h + 1) * HALF] = on_x[:, 6 * FLOW + k * HALF : 6 * FLOW + (k + 1) * HALF]
            xt[rows, h * HALF : (h + 1) * HALF] = on_y[:, 6 * B + k * HALF : 6 * B + (k + 1) * HALF]
    rows = pl.ds(3 * t, t)
    for i, (on_x, on_y) in enumerate(((f0, f2), (f1, f3))):
        ds[rows, i * FLOW : (i + 1) * FLOW] = on_x[:, which * FLOW : (which + 1) * FLOW]
        dt[rows, i * B : (i + 1) * B] = on_y[:, which * B : (which + 1) * B]
        xs[rows, i * HALF : (i + 1) * HALF] = on_x[:, 2 * FLOW :]
        xt[rows, i * HALF : (i + 1) * HALF] = on_y[:, 2 * B :]
    wide[...] = contract_rows(xs[...], ds[...]).astype(wide.dtype)
    tall[...] = contract_rows(xt[...], dt[...]).astype(tall.dtype)


def partials(which, pieces):
    t = pieces[0].shape[0]
    return pl.pallas_call(
        functools.partial(partial_kernel, which),
        out_shape=[
            jax.ShapeDtypeStruct((B, 2 * FLOW), jnp.bfloat16),
            jax.ShapeDtypeStruct((B, 2 * B), jnp.bfloat16),
        ],
        in_specs=[VMEM] * len(pieces),
        out_specs=[VMEM] * 2,
        scratch_shapes=[
            pltpu.VMEM((4 * t, B), jnp.bfloat16),
            pltpu.VMEM((4 * t, 2 * FLOW), jnp.bfloat16),
            pltpu.VMEM((4 * t, B), jnp.bfloat16),
            pltpu.VMEM((4 * t, 2 * B), jnp.bfloat16),
        ],
        compiler_params=PARAMS,
        name="partials",
    )(*pieces)


def chip_sum_kernel(place, wide, tall, far_wide, far_tall, py0, py1, py2, py3, px0, px1, px2, px3):
    my_y = place[3]
    for s, ref in enumerate((py0, py1, py2, py3)):
        rows = pl.ds(aligned(my_y ^ s, 128), 128)
        ref[...] = (wide[rows, :].astype(jnp.float32) + far_wide[rows, :].astype(jnp.float32)).astype(ref.dtype)
    for q, ref in enumerate((px0, px1, px2, px3)):
        for flow in range(2):
            at = flow * B + q * 128
            ref[:, flow * 128 : (flow + 1) * 128] = (
                tall[:, at : at + 128].astype(jnp.float32) + far_tall[:, at : at + 128].astype(jnp.float32)
            ).astype(ref.dtype)


def chip_sum(place, *parts):
    kinds = [jnp.float32] + [jnp.bfloat16] * 3
    return pl.pallas_call(
        chip_sum_kernel,
        out_shape=[jax.ShapeDtypeStruct((128, 2 * FLOW), k) for k in kinds]
        + [jax.ShapeDtypeStruct((B, 256), k) for k in kinds],
        in_specs=[SMEM] + [VMEM] * 4,
        out_specs=[VMEM] * 8,
        compiler_params=PARAMS,
        name="chip_sum",
    )(place, *parts)


PIECE = 96


def ring_sum_kernel(py0, ry1, ry2, ry3, px0, rx1, rx2, rx3, out):
    wide = py0[...] + ry1[...].astype(jnp.float32) + ry2[...].astype(jnp.float32) + ry3[...].astype(jnp.float32)
    tall = px0[...] + rx1[...].astype(jnp.float32) + rx2[...].astype(jnp.float32) + rx3[...].astype(jnp.float32)
    wide = wide.astype(jnp.bfloat16)
    tall = tall.astype(jnp.bfloat16)
    for z in range(4):
        for low in range(2):
            first = (z * 2 + low) * PIECE
            if z < 2:
                out[first : first + 64, :] = wide[low * 64 : low * 64 + 64, z * FLOW : z * FLOW + B]
            else:
                for g in range(4):
                    from_row = low * 256 + g * 64
                    out[first : first + 64, g * 128 : (g + 1) * 128] = tall[
                        from_row : from_row + 64, (z - 2) * 128 : (z - 1) * 128
                    ]
            for h in range(2):
                for flow in range(2):
                    k = low * 64 + h * 32
                    at = h * 256 + flow * 128
                    out[first + 64 : first + PIECE, at : at + 128] = wide[
                        k : k + 32, flow * FLOW + B : (flow + 1) * FLOW
                    ]


def ring_sum(parts):
    return pl.pallas_call(
        ring_sum_kernel,
        out_shape=jax.ShapeDtypeStruct((8 * PIECE, B), jnp.bfloat16),
        in_specs=[VMEM] * 8,
        out_specs=VMEM,
        compiler_params=PARAMS,
        name="ring_sum",
    )(*parts)


def line_sum_kernel(arrived, out):
    total = arrived[0].astype(jnp.float32)
    for i in range(1, 8):
        total = total + arrived[i].astype(jnp.float32)
    out[...] = total.astype(jnp.bfloat16)


def line_sum(arrived):
    return pl.pallas_call(
        line_sum_kernel,
        out_shape=jax.ShapeDtypeStruct((PIECE, B), jnp.bfloat16),
        in_specs=[VMEM],
        out_specs=VMEM,
        compiler_params=PARAMS,
        name="line_sum",
    )(arrived)


def choose_kernel(owner, place, q0, q1, q2, q3, out, position, held):
    fill_positions(owner, position)
    my_x, my_core, my_low = place[1], place[2], place[4]
    mine = position[(place[0] * 4 + my_x) * 2 + my_core]

    @pl.when(mine >= 4)
    def _():
        out[...] = jnp.zeros(out.shape, jnp.bfloat16)

    @pl.when(mine < 4)
    def _():
        for r, ref in enumerate((q0, q1, q2, q3)):
            held[my_x ^ r] = ref[...]
        flow = mine >> 1
        for xl in range(2):
            at_x = 2 * (mine & 1) + xl
            for flip in range(2):
                to = aligned(xl * 2 + (my_core ^ flip), 128)
                for w in range(2):
                    for h in range(2):
                        rows = pl.ds(pl.multiple_of((my_low ^ w) * 64 + h * 32, 32), 32)
                        from_row = (flip * 2 + w) * 32
                        out[rows, pl.ds(to, 128)] = held[
                            at_x, from_row : from_row + 32, pl.ds(aligned(h * 2 + flow, 128), 128)
                        ]


def choose(owner, place, pieces):
    return pl.pallas_call(
        choose_kernel,
        out_shape=jax.ShapeDtypeStruct((128, B), jnp.bfloat16),
        in_specs=[SMEM, SMEM] + [VMEM] * 4,
        out_specs=VMEM,
        scratch_shapes=[pltpu.SMEM((32,), jnp.int32), pltpu.VMEM((4, 128, B), jnp.bfloat16)],
        compiler_params=PARAMS,
        name="choose",
    )(owner, place, *pieces)


def cast_kernel(left, right, out):
    out[:SLOTS] = left[...].astype(jnp.bfloat16)
    out[SLOTS:] = right[...].astype(jnp.bfloat16)


def cast_rows(left, right):
    return pl.pallas_call(
        cast_kernel,
        out_shape=jax.ShapeDtypeStruct((2 * SLOTS, 64, B), jnp.bfloat16),
        in_specs=[VMEM] * 2,
        out_specs=VMEM,
        compiler_params=PARAMS,
        name="cast_rows",
    )(left, right)


def whole_kernel(place, s0, s1, s2, s3, out):
    for r, piece in enumerate((s0, s1, s2, s3)):
        for w in range(2):
            rows = pl.ds(aligned((place[3] ^ r) * 2 + (place[4] ^ w), 64), 64)
            for k in range(2 * SLOTS):
                out[k, rows, :] = piece[w * 2 * SLOTS + k]


def whole(place, pieces):
    return pl.pallas_call(
        whole_kernel,
        out_shape=jax.ShapeDtypeStruct((2 * SLOTS, B, B), jnp.bfloat16),
        in_specs=[SMEM] + [VMEM] * 4,
        out_specs=VMEM,
        compiler_params=PARAMS,
        name="whole",
    )(place, *pieces)


def root_kernel(slot, place, r0, r1, r2, r3, statistics, left_rows, right_rows, *refs):
    if slot:
        left_first, right_first, directions, left_new, right_new, g_ref, a_ref, m_ref = refs
        left_new[0] = left_first[...]
        right_new[0] = right_first[...]
    else:
        directions, left_new, right_new, g_ref, a_ref, m_ref = refs
    my_z, my_y, my_low = place[0], place[3], place[4]
    node = my_y * 2 + my_low
    first_row = aligned(node, 64)
    for r, piece in enumerate((r0, r1, r2, r3)):
        at_y = my_y ^ r
        if slot:
            g_ref[pl.ds(aligned(at_y, 128), 128), :] = piece[...]
            continue
        for w in range(2):
            at_low = my_low ^ w
            base = w * 64

            @pl.when(my_z < 2)
            def _():
                g_ref[pl.ds(pl.multiple_of(at_y * 128 + at_low * 64, 64), 64), :] = piece[base : base + 64, :]

            @pl.when(my_z >= 2)
            def _():
                for g in range(4):
                    g_ref[
                        pl.ds(pl.multiple_of(at_low * 256 + g * 64, 64), 64),
                        pl.ds(aligned(at_y, 128), 128),
                    ] = piece[base : base + 64, g * 128 : (g + 1) * 128]

    def scaled(gram, old_rows, new_rows, which):
        a_ref[which] = gram
        rows = BETA * old_rows[slot] + a_ref[which, pl.ds(first_row, 64), :] * (1.0 / B)
        if slot:
            new_rows[slot] = rows
        else:
            new_rows[...] = rows
        full = BETA * statistics[which * SLOTS + slot].astype(jnp.float32) + gram * (1.0 / B)
        norm = B * jnp.sqrt(jnp.sum(full * full, keepdims=True) * (1.0 / (B * B)) + 1e-06)
        matrix = full / norm
        a_ref[which] = matrix
        m_ref[which] = matrix.astype(jnp.bfloat16)
        return lax.rsqrt(jnp.sqrt(norm))

    g = g_ref[...]
    left_gram = lax.dot_general(g, g, (((1,), (1,)), ((), ())), preferred_element_type=jnp.float32)
    right_gram = contract_rows(g, g)
    left_scale = scaled(left_gram, left_rows, left_new, 0)
    right_scale = scaled(right_gram, right_rows, right_new, 1)
    power = a_ref[0, pl.ds(first_row, 64), :]
    column = lax.broadcasted_iota(jnp.int32, (64, B), 1)
    row = lax.broadcasted_iota(jnp.int32, (64, B), 0) + first_row
    total = jnp.where(row == column, COEF[0], 0.0) + COEF[1] * power
    for k in range(2, 7):
        power = jnp.dot(power.astype(jnp.bfloat16), m_ref[0], preferred_element_type=jnp.float32)
        total = total + COEF[k] * power
    root = (total * left_scale).astype(jnp.bfloat16)
    half = jnp.dot(root, g, preferred_element_type=jnp.float32).astype(jnp.bfloat16)
    power = half.astype(jnp.float32)
    total = COEF[0] * power
    for k in range(1, 7):
        power = jnp.dot(power.astype(jnp.bfloat16), m_ref[1], preferred_element_type=jnp.float32)
        total = total + COEF[k] * power
    directions[...] = (total * right_scale).astype(jnp.bfloat16)


def roots(slot, place, pieces, statistics, left_rows, right_rows, *first):
    new = jax.ShapeDtypeStruct((SLOTS, 64, B) if slot else (64, B), jnp.float32)
    return pl.pallas_call(
        functools.partial(root_kernel, slot),
        out_shape=[jax.ShapeDtypeStruct((64, B), jnp.bfloat16), new, new],
        in_specs=[SMEM] + [VMEM] * (7 + len(first)),
        out_specs=[VMEM] * 3,
        scratch_shapes=[
            pltpu.VMEM((B, B), jnp.bfloat16),
            pltpu.VMEM((2, B, B), jnp.float32),
            pltpu.VMEM((2, B, B), jnp.bfloat16),
        ],
        compiler_params=PARAMS,
        name="roots",
    )(place, *pieces, statistics, left_rows, right_rows, *first)


def place_kernel(owner, place, *refs):
    sources, out, position, sem = refs[:16], refs[16], refs[17], refs[18]
    fill_positions(owner, position)
    my_z, my_x, my_core = place[0], place[1], place[2]
    for wait in (False, True):
        for slot in range(SLOTS):
            for flip in range(2):
                for r in range(4):
                    source = sources[(slot * 2 + flip) * 4 + r]
                    for a in range(4):
                        block = position[((my_z ^ a) * 4 + (my_x ^ r)) * 2 + (my_core ^ flip)]
                        copy = pltpu.make_async_copy(
                            source.at[pl.ds(a * 64, 64), :],
                            out.at[:, pl.ds(aligned(jnp.minimum(block + slot * 32, 35), B), B)],
                            sem,
                        )
                        act = copy.wait if wait else copy.start
                        if slot == 0:
                            act()
                        else:
                            pl.when(block < 4)(act)


def put_blocks(owner, place, sources, blocks):
    return pl.pallas_call(
        place_kernel,
        out_shape=jax.ShapeDtypeStruct((64, blocks * B), jnp.bfloat16),
        in_specs=[SMEM, SMEM] + [ANY] * 16,
        out_specs=ANY,
        scratch_shapes=[pltpu.SMEM((32,), jnp.int32), pltpu.SemaphoreType.DMA],
        compiler_params=PARAMS,
        name="put_blocks",
    )(owner, place, *sources)


def around_z_and_x(rows):
    a2, a1, a3 = swap(rows, "z_hi", 2), swap(rows, "z_hi", 1), swap(rows, "z_hi", 3)
    plane = jnp.concatenate([rows, a1, a2, a3])
    b2, b1, b3 = swap(plane, "x", 2), swap(plane, "x", 1), swap(plane, "x", 3)
    near = (plane, b1, b2, b3)
    return near + tuple(swap(v, "core", 1) for v in near)


def shards(x_band, d_gate_up, owner, stat_left, stat_right):
    place = jnp.stack([lax.axis_index(a) for a in FINE]).astype(jnp.int32)
    bucket = d_gate_up.shape[1] // B

    x1, x3, y1, y3 = packed(pack_kernel, "pack", [X_MSG] * 2 + [Y_MSG] * 2, owner, place, d_gate_up, x_band)
    x1, x3, y1, y3 = swap(x1, "x", 1), swap(x3, "x", 3), swap(y1, "y", 1), swap(y3, "y", 3)
    (own,) = packed(pack_own_kernel, "pack_own", [OWN_MSG], owner, place, d_gate_up)
    statistics = cast_rows(stat_left[0], stat_right[0])
    statistics = jnp.concatenate([statistics, swap(statistics, "z_lo", 1)])
    f0, f1 = swap(x1[:, X_FWD], "x", 3), swap(x3[:, X_FWD], "x", 1)
    f2, f3 = swap(y1[:, Y_FWD], "y", 3), swap(y3[:, Y_FWD], "y", 1)
    pieces = (own, x_band, x1, x3, y1, y3, f0, f1, f2, f3)
    wide, tall = partials(1, pieces)
    far_wide, far_tall = swap(wide, "core", 1), swap(tall, "core", 1)
    wide, tall = partials(0, pieces)
    py0, py1, py2, py3, px0, px1, px2, px3 = chip_sum(place, wide, tall, far_wide, far_tall)
    ry2, rx2 = swap(py2, "y", 2), swap(px2, "x", 2)
    ry1, rx1 = swap(py1, "y", 1), swap(px1, "x", 1)
    ry3, rx3 = swap(py3, "y", 3), swap(px3, "x", 3)
    message = ring_sum((py0, ry1, ry2, ry3, px0, rx1, rx2, rx3))

    message, statistics = lax.optimization_barrier((message, statistics))
    s2, s1, s3 = swap(statistics, "y", 2), swap(statistics, "y", 1), swap(statistics, "y", 3)
    message = lax.all_to_all(message, ("z_hi", "z_lo"), 0, 0, tiled=True)
    line = line_sum(message.reshape(8, PIECE, B))
    line, s1, s2, s3 = lax.optimization_barrier((line, s1, s2, s3))
    statistics = whole(place, (statistics, s1, s2, s3))

    main, extra = line[:64], line[64:]
    far = swap(line, "z_lo", 1)
    extra_core = swap(extra, "core", 1)
    diagonal = [(c * 2 + w, 3 - (c * 2 + w)) for c in range(2) for w in range(2)]
    extra_far = lax.ppermute(extra, ("core", "z_lo"), diagonal)
    m0 = jnp.concatenate([main, far[:64]])
    m2, m1, m3 = swap(m0, "y", 2), swap(m0, "y", 1), swap(m0, "y", 3)
    q0 = jnp.concatenate([extra, far[64:], extra_core, extra_far])
    q2, q1, q3 = swap(q0, "x", 2), swap(q0, "x", 1), swap(q0, "x", 3)
    first, left_first, right_first = roots(0, place, (m0, m1, m2, m3), statistics, stat_left[0], stat_right[0])
    e0 = choose(owner, place, (q0, q1, q2, q3))
    e2, e1, e3 = swap(e0, "y", 2), swap(e0, "y", 1), swap(e0, "y", 3)
    second, left_new, right_new = roots(
        1, place, (e0, e1, e2, e3), statistics, stat_left[0], stat_right[0], left_first, right_first
    )
    blocks = around_z_and_x(first) + around_z_and_x(second)
    out = put_blocks(owner, place, blocks, bucket)
    return (out, left_new[None], right_new[None])


def solution(mesh):
    fine = Mesh(np.asarray(mesh.devices).reshape(FINE_SIZES), FINE)
    dp, node = FINE[:3], FINE[3:]
    placed = (P(dp + node, None), P(dp + node, None), P(), P(dp, None, node, None), P(dp, None, node, None))
    return jax.shard_map(
        shards,
        mesh=fine,
        in_specs=placed,
        out_specs=(P(node, None), P(dp, None, node, None), P(dp, None, node, None)),
        check_vma=False,
    )
```

```python
import functools
import math

import jax
import jax.numpy as jnp
import numpy as np
from jax import lax
from jax.experimental import pallas as pl
from jax.experimental.pallas import tpu as pltpu
from jax.sharding import Mesh, PartitionSpec as P

B = 512
SLOTS = 2
BETA = 0.9
EXTRA_CHUNK = 128
FLOW = B + EXTRA_CHUNK
HALF = B // 2

FINE = ("z_hi", "x", "core", "y", "z_lo")
FINE_SIZES = (4, 4, 2, 4, 2)
VMEM_LIMIT = 24 * 1024 * 1024

COEF = [6.25 / 4, -(1.25 + 1.25**5) / 4] + [
    -math.comb(5, k) * 1.25 ** (5 - k) * (-0.25) ** k / 4 for k in range(1, 6)
]

ANY = pl.BlockSpec(memory_space=pl.ANY)
HBM = pl.BlockSpec(memory_space=pltpu.HBM)
SMEM = pl.BlockSpec(memory_space=pltpu.SMEM)
VMEM = pl.BlockSpec(memory_space=pltpu.VMEM)
PARAMS = pltpu.CompilerParams(vmem_limit_bytes=VMEM_LIMIT)


def swap(value, axis, mask):
    size = FINE_SIZES[FINE.index(axis)]
    return lax.ppermute(value, axis, [(i, i ^ mask) for i in range(size)])


def aligned(index, step):
    return pl.multiple_of(index * step, step)


def fill_positions(owner, position):
    for block in range(32):
        position[owner[block]] = block


X_DIRECT = 4 * FLOW
X_MSG = 6 * FLOW + B
Y_DIRECT = 4 * B
Y_MSG = 6 * B + B
OWN_MSG = 4 * FLOW + 4 * B
X_FWD = slice(X_DIRECT, 6 * FLOW + HALF)
Y_FWD = slice(Y_DIRECT, 6 * B + HALF)


class Packer:
    def __init__(self, owner, place, d, position, sem):
        fill_positions(owner, position)
        self.position, self.place, self.d, self.sem = position, place, d, sem
        self.cores = (place[2], 1 - place[2])
        self.copies = []

    def copy(self, source, first, width, target, at):
        self.copies.append(
            pltpu.make_async_copy(source.at[:, pl.ds(first, width)], target.at[:, pl.ds(at, width)], self.sem)
        )
        self.copies[-1].start()

    def flow_x(self, flow, r, core, target, at):
        to_x = self.place[1] ^ r
        block = self.position[(flow * 4 + to_x) * 2 + core]
        self.copy(self.d, aligned(block, B), B, target, at)
        chunk = 32 * B // EXTRA_CHUNK + flow * 8 + to_x * 2 + core
        self.copy(self.d, aligned(chunk, EXTRA_CHUNK), EXTRA_CHUNK, target, at + B)

    def flow_y(self, flow, r, core, target, at):
        to_y = self.place[3] ^ r
        for q in range(4):
            block = self.position[(flow * 4 + (self.place[1] ^ q)) * 2 + core]
            self.copy(self.d, pl.multiple_of(block * B + to_y * 128, 128), 128, target, at + q * 128)

    def finish(self):
        for c in self.copies:
            c.wait()


def pack_kernel(owner, place, d, xb, x1, x3, y1, y3, position, sem):
    packer = Packer(owner, place, d, position, sem)
    for near, through, on_x, on_y in ((1, 0, x1, y1), (3, 1, x3, y3)):
        for i, core in enumerate(packer.cores):
            packer.flow_x(0, near, core, on_x, i * 2 * FLOW)
            packer.flow_x(1, near, core, on_x, i * 2 * FLOW + FLOW)
            packer.flow_x(through, 2, core, on_x, X_DIRECT + i * FLOW)
            packer.flow_y(2, near, core, on_y, i * 2 * B)
            packer.flow_y(3, near, core, on_y, i * 2 * B + B)
            packer.flow_y(2 + through, 2, core, on_y, Y_DIRECT + i * B)
        for i, h in enumerate((through, 1 - through)):
            packer.copy(xb, h * HALF, HALF, on_x, 6 * FLOW + i * HALF)
            packer.copy(xb, h * HALF, HALF, on_y, 6 * B + i * HALF)
    packer.finish()


def pack_own_kernel(owner, place, d, out, position, sem):
    packer = Packer(owner, place, d, position, sem)
    for i, core in enumerate(packer.cores):
        for flow in range(2):
            packer.flow_x(flow, 0, core, out, (i * 2 + flow) * FLOW)
            packer.flow_y(2 + flow, 0, core, out, 4 * FLOW + (i * 2 + flow) * B)
    packer.finish()


def packed(kernel, name, widths, owner, place, d, *more):
    rows = d.shape[0]
    return pl.pallas_call(
        kernel,
        out_shape=[jax.ShapeDtypeStruct((rows, w), jnp.bfloat16) for w in widths],
        in_specs=[SMEM, SMEM, HBM] + [ANY] * len(more),
        out_specs=[VMEM] * len(widths),
        scratch_shapes=[pltpu.SMEM((32,), jnp.int32), pltpu.SemaphoreType.DMA],
        compiler_params=PARAMS,
        name=name,
    )(owner, place, d, *more)


def contract_rows(a, b):
    return lax.dot_general(a, b, (((0,), (0,)), ((), ())), preferred_element_type=jnp.float32)


def partial_kernel(which, own, xb, x1, x3, y1, y3, f0, f1, f2, f3, out, xs, ds, xt, dt):
    t = own.shape[0]
    wide_at = which * 2 * FLOW
    tall_at = which * 2 * B
    rows = pl.ds(0, t)
    xs[rows, :] = xb[...]
    xt[rows, :] = xb[...]
    ds[rows, :] = own[:, wide_at : wide_at + 2 * FLOW]
    dt[rows, :] = own[:, 4 * FLOW + tall_at : 4 * FLOW + tall_at + 2 * B]
    for i, (on_x, on_y) in enumerate(((x1, y1), (x3, y3))):
        rows = pl.ds((1 + i) * t, t)
        ds[rows, :] = on_x[:, wide_at : wide_at + 2 * FLOW]
        dt[rows, :] = on_y[:, tall_at : tall_at + 2 * B]
        for k, h in enumerate((i, 1 - i)):
            xs[rows, h * HALF : (h + 1) * HALF] = on_x[:, 6 * FLOW + k * HALF : 6 * FLOW + (k + 1) * HALF]
            xt[rows, h * HALF : (h + 1) * HALF] = on_y[:, 6 * B + k * HALF : 6 * B + (k + 1) * HALF]
    rows = pl.ds(3 * t, t)
    for i, (on_x, on_y) in enumerate(((f0, f2), (f1, f3))):
        ds[rows, i * FLOW : (i + 1) * FLOW] = on_x[:, which * FLOW : (which + 1) * FLOW]
        dt[rows, i * B : (i + 1) * B] = on_y[:, which * B : (which + 1) * B]
        xs[rows, i * HALF : (i + 1) * HALF] = on_x[:, 2 * FLOW :]
        xt[rows, i * HALF : (i + 1) * HALF] = on_y[:, 2 * B :]
    out[:, : 2 * FLOW] = contract_rows(xs[...], ds[...]).astype(out.dtype)
    out[:, 2 * FLOW :] = contract_rows(xt[...], dt[...]).astype(out.dtype)


def partials(which, pieces):
    t = pieces[0].shape[0]
    return pl.pallas_call(
        functools.partial(partial_kernel, which),
        out_shape=jax.ShapeDtypeStruct((B, 2 * FLOW + 2 * B), jnp.bfloat16),
        in_specs=[VMEM] * len(pieces),
        out_specs=VMEM,
        scratch_shapes=[
            pltpu.VMEM((4 * t, B), jnp.bfloat16),
            pltpu.VMEM((4 * t, 2 * FLOW), jnp.bfloat16),
            pltpu.VMEM((4 * t, B), jnp.bfloat16),
            pltpu.VMEM((4 * t, 2 * B), jnp.bfloat16),
        ],
        compiler_params=PARAMS,
        name="partials",
    )(*pieces)


def chip_sum_kernel(place, near, far, py0, py1, py2, py3, px0, px1, px2, px3):
    my_y = place[3]
    wide = slice(0, 2 * FLOW)
    for s, ref in enumerate((py0, py1, py2, py3)):
        rows = pl.ds(aligned(my_y ^ s, 128), 128)
        ref[...] = (near[rows, wide].astype(jnp.float32) + far[rows, wide].astype(jnp.float32)).astype(ref.dtype)
    for q, ref in enumerate((px0, px1, px2, px3)):
        for flow in range(2):
            at = slice(2 * FLOW + flow * B + q * 128, 2 * FLOW + flow * B + (q + 1) * 128)
            ref[:, flow * 128 : (flow + 1) * 128] = (
                near[:, at].astype(jnp.float32) + far[:, at].astype(jnp.float32)
            ).astype(ref.dtype)


def chip_sum(place, *parts):
    kinds = [jnp.float32] + [jnp.bfloat16] * 3
    return pl.pallas_call(
        chip_sum_kernel,
        out_shape=[jax.ShapeDtypeStruct((128, 2 * FLOW), k) for k in kinds]
        + [jax.ShapeDtypeStruct((B, 256), k) for k in kinds],
        in_specs=[SMEM] + [VMEM] * 2,
        out_specs=[VMEM] * 8,
        compiler_params=PARAMS,
        name="chip_sum",
    )(place, *parts)


PIECE = 96


def ring_sum_kernel(py0, ry1, ry2, ry3, px0, rx1, rx2, rx3, out):
    wide = py0[...] + ry1[...].astype(jnp.float32) + ry2[...].astype(jnp.float32) + ry3[...].astype(jnp.float32)
    tall = px0[...] + rx1[...].astype(jnp.float32) + rx2[...].astype(jnp.float32) + rx3[...].astype(jnp.float32)
    wide = wide.astype(jnp.bfloat16)
    tall = tall.astype(jnp.bfloat16)
    for z in range(4):
        for low in range(2):
            first = (z * 2 + low) * PIECE
            if z < 2:
                out[first : first + 64, :] = wide[low * 64 : low * 64 + 64, z * FLOW : z * FLOW + B]
            else:
                for g in range(4):
                    from_row = low * 256 + g * 64
                    out[first : first + 64, g * 128 : (g + 1) * 128] = tall[
                        from_row : from_row + 64, (z - 2) * 128 : (z - 1) * 128
                    ]
            for h in range(2):
                for flow in range(2):
                    k = low * 64 + h * 32
                    at = h * 256 + flow * 128
                    out[first + 64 : first + PIECE, at : at + 128] = wide[
                        k : k + 32, flow * FLOW + B : (flow + 1) * FLOW
                    ]


def ring_sum(parts):
    return pl.pallas_call(
        ring_sum_kernel,
        out_shape=jax.ShapeDtypeStruct((8 * PIECE, B), jnp.bfloat16),
        in_specs=[VMEM] * 8,
        out_specs=VMEM,
        compiler_params=PARAMS,
        name="ring_sum",
    )(*parts)


def line_sum_kernel(arrived, out):
    total = arrived[0].astype(jnp.float32)
    for i in range(1, 8):
        total = total + arrived[i].astype(jnp.float32)
    out[...] = total.astype(jnp.bfloat16)


def line_sum(arrived):
    return pl.pallas_call(
        line_sum_kernel,
        out_shape=jax.ShapeDtypeStruct((PIECE, B), jnp.bfloat16),
        in_specs=[VMEM],
        out_specs=VMEM,
        compiler_params=PARAMS,
        name="line_sum",
    )(arrived)


def choose_kernel(owner, place, q0, q1, q2, q3, out, position, held):
    fill_positions(owner, position)
    my_x, my_core, my_low = place[1], place[2], place[4]
    mine = position[(place[0] * 4 + my_x) * 2 + my_core]

    @pl.when(mine >= 4)
    def _():
        out[...] = jnp.zeros(out.shape, jnp.bfloat16)

    @pl.when(mine < 4)
    def _():
        for r, ref in enumerate((q0, q1, q2, q3)):
            held[my_x ^ r] = ref[...]
        flow = mine >> 1
        for xl in range(2):
            at_x = 2 * (mine & 1) + xl
            for flip in range(2):
                to = aligned(xl * 2 + (my_core ^ flip), 128)
                for w in range(2):
                    for h in range(2):
                        rows = pl.ds(pl.multiple_of((my_low ^ w) * 64 + h * 32, 32), 32)
                        from_row = (flip * 2 + w) * 32
                        out[rows, pl.ds(to, 128)] = held[
                            at_x, from_row : from_row + 32, pl.ds(aligned(h * 2 + flow, 128), 128)
                        ]


def choose(owner, place, pieces):
    return pl.pallas_call(
        choose_kernel,
        out_shape=jax.ShapeDtypeStruct((128, B), jnp.bfloat16),
        in_specs=[SMEM, SMEM] + [VMEM] * 4,
        out_specs=VMEM,
        scratch_shapes=[pltpu.SMEM((32,), jnp.int32), pltpu.VMEM((4, 128, B), jnp.bfloat16)],
        compiler_params=PARAMS,
        name="choose",
    )(owner, place, *pieces)


def cast_kernel(left, right, out):
    out[:SLOTS] = left[...].astype(jnp.bfloat16)
    out[SLOTS:] = right[...].astype(jnp.bfloat16)


def cast_rows(left, right):
    return pl.pallas_call(
        cast_kernel,
        out_shape=jax.ShapeDtypeStruct((2 * SLOTS, 64, B), jnp.bfloat16),
        in_specs=[VMEM] * 2,
        out_specs=VMEM,
        compiler_params=PARAMS,
        name="cast_rows",
    )(left, right)


def whole_kernel(place, s0, s1, s2, s3, out):
    for r, piece in enumerate((s0, s1, s2, s3)):
        for w in range(2):
            rows = pl.ds(aligned((place[3] ^ r) * 2 + (place[4] ^ w), 64), 64)
            for k in range(2 * SLOTS):
                out[k, rows, :] = piece[w * 2 * SLOTS + k]


def whole(place, pieces):
    return pl.pallas_call(
        whole_kernel,
        out_shape=jax.ShapeDtypeStruct((2 * SLOTS, B, B), jnp.bfloat16),
        in_specs=[SMEM] + [VMEM] * 4,
        out_specs=VMEM,
        compiler_params=PARAMS,
        name="whole",
    )(place, *pieces)


def root_kernel(slot, place, r0, r1, r2, r3, statistics, left_rows, right_rows, *refs):
    if slot:
        left_first, right_first, directions, left_new, right_new, g_ref, a_ref, m_ref = refs
        left_new[0] = left_first[...]
        right_new[0] = right_first[...]
    else:
        directions, left_new, right_new, g_ref, a_ref, m_ref = refs
    my_z, my_y, my_low = place[0], place[3], place[4]
    node = my_y * 2 + my_low
    first_row = aligned(node, 64)
    for r, piece in enumerate((r0, r1, r2, r3)):
        at_y = my_y ^ r
        if slot:
            g_ref[pl.ds(aligned(at_y, 128), 128), :] = piece[...]
            continue
        for w in range(2):
            at_low = my_low ^ w
            base = w * 64

            @pl.when(my_z < 2)
            def _():
                g_ref[pl.ds(pl.multiple_of(at_y * 128 + at_low * 64, 64), 64), :] = piece[base : base + 64, :]

            @pl.when(my_z >= 2)
            def _():
                for g in range(4):
                    g_ref[
                        pl.ds(pl.multiple_of(at_low * 256 + g * 64, 64), 64),
                        pl.ds(aligned(at_y, 128), 128),
                    ] = piece[base : base + 64, g * 128 : (g + 1) * 128]

    def scaled(gram, old_rows, new_rows, which):
        a_ref[which] = gram
        rows = BETA * old_rows[slot] + a_ref[which, pl.ds(first_row, 64), :] * (1.0 / B)
        if slot:
            new_rows[slot] = rows
        else:
            new_rows[...] = rows
        full = BETA * statistics[which * SLOTS + slot].astype(jnp.float32) + gram * (1.0 / B)
        norm = B * jnp.sqrt(jnp.sum(full * full, keepdims=True) * (1.0 / (B * B)) + 1e-06)
        matrix = full / norm
        a_ref[which] = matrix
        m_ref[which] = matrix.astype(jnp.bfloat16)
        return lax.rsqrt(jnp.sqrt(norm))

    g = g_ref[...]
    left_gram = lax.dot_general(g, g, (((1,), (1,)), ((), ())), preferred_element_type=jnp.float32)
    right_gram = contract_rows(g, g)
    left_scale = scaled(left_gram, left_rows, left_new, 0)
    right_scale = scaled(right_gram, right_rows, right_new, 1)
    power = a_ref[0, pl.ds(first_row, 64), :]
    column = lax.broadcasted_iota(jnp.int32, (64, B), 1)
    row = lax.broadcasted_iota(jnp.int32, (64, B), 0) + first_row
    total = jnp.where(row == column, COEF[0], 0.0) + COEF[1] * power
    for k in range(2, 7):
        power = jnp.dot(power.astype(jnp.bfloat16), m_ref[0], preferred_element_type=jnp.float32)
        total = total + COEF[k] * power
    root = (total * left_scale).astype(jnp.bfloat16)
    half = jnp.dot(root, g, preferred_element_type=jnp.float32).astype(jnp.bfloat16)
    power = half.astype(jnp.float32)
    total = COEF[0] * power
    for k in range(1, 7):
        power = jnp.dot(power.astype(jnp.bfloat16), m_ref[1], preferred_element_type=jnp.float32)
        total = total + COEF[k] * power
    directions[...] = (total * right_scale).astype(jnp.bfloat16)


def roots(slot, place, pieces, statistics, left_rows, right_rows, *first):
    new = jax.ShapeDtypeStruct((SLOTS, 64, B) if slot else (64, B), jnp.float32)
    return pl.pallas_call(
        functools.partial(root_kernel, slot),
        out_shape=[jax.ShapeDtypeStruct((64, B), jnp.bfloat16), new, new],
        in_specs=[SMEM] + [VMEM] * (7 + len(first)),
        out_specs=[VMEM] * 3,
        scratch_shapes=[
            pltpu.VMEM((B, B), jnp.bfloat16),
            pltpu.VMEM((2, B, B), jnp.float32),
            pltpu.VMEM((2, B, B), jnp.bfloat16),
        ],
        compiler_params=PARAMS,
        name="roots",
    )(place, *pieces, statistics, left_rows, right_rows, *first)


def place_kernel(owner, place, *refs):
    sources, out, position, sem = refs[:16], refs[16], refs[17], refs[18]
    fill_positions(owner, position)
    my_z, my_x, my_core = place[0], place[1], place[2]
    for wait in (False, True):
        for slot in range(SLOTS):
            for flip in range(2):
                for r in range(4):
                    source = sources[(slot * 2 + flip) * 4 + r]
                    for a in range(4):
                        block = position[((my_z ^ a) * 4 + (my_x ^ r)) * 2 + (my_core ^ flip)]
                        copy = pltpu.make_async_copy(
                            source.at[pl.ds(a * 64, 64), :],
                            out.at[:, pl.ds(aligned(jnp.minimum(block + slot * 32, 35), B), B)],
                            sem,
                        )
                        act = copy.wait if wait else copy.start
                        if slot == 0:
                            act()
                        else:
                            pl.when(block < 4)(act)


def put_blocks(owner, place, sources, blocks):
    return pl.pallas_call(
        place_kernel,
        out_shape=jax.ShapeDtypeStruct((64, blocks * B), jnp.bfloat16),
        in_specs=[SMEM, SMEM] + [ANY] * 16,
        out_specs=ANY,
        scratch_shapes=[pltpu.SMEM((32,), jnp.int32), pltpu.SemaphoreType.DMA],
        compiler_params=PARAMS,
        name="put_blocks",
    )(owner, place, *sources)


def around_z(rows):
    a2, a1, a3 = swap(rows, "z_hi", 2), swap(rows, "z_hi", 1), swap(rows, "z_hi", 3)
    return jnp.concatenate([rows, a1, a2, a3])


def around_x(plane):
    b2, b1, b3 = swap(plane, "x", 2), swap(plane, "x", 1), swap(plane, "x", 3)
    return plane, b1, b2, b3


def shards(x_band, d_gate_up, owner, stat_left, stat_right):
    place = jnp.stack([lax.axis_index(a) for a in FINE]).astype(jnp.int32)
    bucket = d_gate_up.shape[1] // B

    x1, x3, y1, y3 = packed(pack_kernel, "pack", [X_MSG] * 2 + [Y_MSG] * 2, owner, place, d_gate_up, x_band)
    x1, x3, y1, y3 = swap(x1, "x", 1), swap(x3, "x", 3), swap(y1, "y", 1), swap(y3, "y", 3)
    (own,) = packed(pack_own_kernel, "pack_own", [OWN_MSG], owner, place, d_gate_up)
    statistics = cast_rows(stat_left[0], stat_right[0])
    statistics = jnp.concatenate([statistics, swap(statistics, "z_lo", 1)])
    f0, f1 = swap(x1[:, X_FWD], "x", 3), swap(x3[:, X_FWD], "x", 1)
    y1_on, y3_on, statistics = lax.optimization_barrier((y1[:, Y_FWD], y3[:, Y_FWD], statistics))
    f2, f3 = swap(y1_on, "y", 3), swap(y3_on, "y", 1)
    pieces = (own, x_band, x1, x3, y1, y3, f0, f1, f2, f3)
    far_sum = swap(partials(1, pieces), "core", 1)
    py0, py1, py2, py3, px0, px1, px2, px3 = chip_sum(place, partials(0, pieces), far_sum)
    ry2, rx2 = swap(py2, "y", 2), swap(px2, "x", 2)
    ry1, rx1 = swap(py1, "y", 1), swap(px1, "x", 1)
    ry3, rx3 = swap(py3, "y", 3), swap(px3, "x", 3)
    message = ring_sum((py0, ry1, ry2, ry3, px0, rx1, rx2, rx3))

    message, statistics = lax.optimization_barrier((message, statistics))
    s2, s1, s3 = swap(statistics, "y", 2), swap(statistics, "y", 1), swap(statistics, "y", 3)
    message = lax.all_to_all(message, ("z_hi", "z_lo"), 0, 0, tiled=True)
    line = line_sum(message.reshape(8, PIECE, B))

    main, extra = line[:64], line[64:]
    far = swap(line, "z_lo", 1)
    extra_core = swap(extra, "core", 1)
    diagonal = [(c * 2 + w, 3 - (c * 2 + w)) for c in range(2) for w in range(2)]
    extra_far = lax.ppermute(extra, ("core", "z_lo"), diagonal)
    m0 = jnp.concatenate([main, far[:64]])
    m0, s1, s2, s3 = lax.optimization_barrier((m0, s1, s2, s3))
    statistics = whole(place, (statistics, s1, s2, s3))
    m2, m1, m3 = swap(m0, "y", 2), swap(m0, "y", 1), swap(m0, "y", 3)
    q0 = jnp.concatenate([extra, far[64:], extra_core, extra_far])
    q2, q1, q3 = swap(q0, "x", 2), swap(q0, "x", 1), swap(q0, "x", 3)
    first, left_first, right_first = roots(0, place, (m0, m1, m2, m3), statistics, stat_left[0], stat_right[0])
    e0 = choose(owner, place, (q0, q1, q2, q3))
    e2, e1, e3 = swap(e0, "y", 2), swap(e0, "y", 1), swap(e0, "y", 3)
    second, left_new, right_new = roots(
        1, place, (e0, e1, e2, e3), statistics, stat_left[0], stat_right[0], left_first, right_first
    )
    first = around_x(around_z(first))
    plane = around_z(second)
    first, _ = lax.optimization_barrier((first, plane))
    second = around_x(plane)
    blocks = [swap(v, "core", mask) if mask else v for part in (first, second) for mask in range(2) for v in part]
    out = put_blocks(owner, place, blocks, bucket)
    return (out, left_new[None], right_new[None])


def solution(mesh):
    fine = Mesh(np.asarray(mesh.devices).reshape(FINE_SIZES), FINE)
    dp, node = FINE[:3], FINE[3:]
    placed = (P(dp + node, None), P(dp + node, None), P(), P(dp, None, node, None), P(dp, None, node, None))
    return jax.shard_map(
        shards,
        mesh=fine,
        in_specs=placed,
        out_specs=(P(node, None), P(dp, None, node, None), P(dp, None, node, None)),
        check_vma=False,
    )
```

```python
import functools
import math

import jax
import jax.numpy as jnp
import numpy as np
from jax import lax
from jax.experimental import pallas as pl
from jax.experimental.pallas import tpu as pltpu
from jax.sharding import Mesh, PartitionSpec as P

B = 512
SLOTS = 2
BETA = 0.9
EXTRA_CHUNK = 128
FLOW = B + EXTRA_CHUNK
HALF = B // 2

FINE = ("z_hi", "x", "core", "y", "z_lo")
FINE_SIZES = (4, 4, 2, 4, 2)
VMEM_LIMIT = 24 * 1024 * 1024

COEF = [6.25 / 4, -(1.25 + 1.25**5) / 4] + [
    -math.comb(5, k) * 1.25 ** (5 - k) * (-0.25) ** k / 4 for k in range(1, 6)
]

ANY = pl.BlockSpec(memory_space=pl.ANY)
HBM = pl.BlockSpec(memory_space=pltpu.HBM)
SMEM = pl.BlockSpec(memory_space=pltpu.SMEM)
VMEM = pl.BlockSpec(memory_space=pltpu.VMEM)
PARAMS = pltpu.CompilerParams(vmem_limit_bytes=VMEM_LIMIT)


def swap(value, axis, mask):
    size = FINE_SIZES[FINE.index(axis)]
    return lax.ppermute(value, axis, [(i, i ^ mask) for i in range(size)])


def aligned(index, step):
    return pl.multiple_of(index * step, step)


def fill_positions(place, position):
    for block in range(32):
        position[place[len(FINE) + block]] = block


X_DIRECT = 4 * FLOW
X_MSG = 6 * FLOW + B
Y_DIRECT = 4 * B
Y_MSG = 6 * B + B
OWN_MSG = 4 * FLOW + 4 * B
X_FWD = slice(X_DIRECT, 6 * FLOW + HALF)
Y_FWD = slice(Y_DIRECT, 6 * B + HALF)


class Packer:
    def __init__(self, place, d, position, sem):
        fill_positions(place, position)
        self.position, self.place, self.d, self.sem = position, place, d, sem
        self.cores = (place[2], 1 - place[2])
        self.copies = []

    def copy(self, source, first, width, target, at):
        self.copies.append(
            pltpu.make_async_copy(source.at[:, pl.ds(first, width)], target.at[:, pl.ds(at, width)], self.sem)
        )
        self.copies[-1].start()

    def flow_x(self, flow, r, core, target, at):
        to_x = self.place[1] ^ r
        block = self.position[(flow * 4 + to_x) * 2 + core]
        self.copy(self.d, aligned(block, B), B, target, at)
        chunk = 32 * B // EXTRA_CHUNK + flow * 8 + to_x * 2 + core
        self.copy(self.d, aligned(chunk, EXTRA_CHUNK), EXTRA_CHUNK, target, at + B)

    def flow_y(self, flow, r, core, target, at):
        to_y = self.place[3] ^ r
        for q in range(4):
            block = self.position[(flow * 4 + (self.place[1] ^ q)) * 2 + core]
            self.copy(self.d, pl.multiple_of(block * B + to_y * 128, 128), 128, target, at + q * 128)

    def finish(self):
        for c in self.copies:
            c.wait()


def pack_kernel(place, d, xb, x1, x3, y1, y3, position, sem):
    packer = Packer(place, d, position, sem)
    for near, through, on_x, on_y in ((1, 0, x1, y1), (3, 1, x3, y3)):
        for i, core in enumerate(packer.cores):
            packer.flow_x(0, near, core, on_x, i * 2 * FLOW)
            packer.flow_x(1, near, core, on_x, i * 2 * FLOW + FLOW)
            packer.flow_x(through, 2, core, on_x, X_DIRECT + i * FLOW)
            packer.flow_y(2, near, core, on_y, i * 2 * B)
            packer.flow_y(3, near, core, on_y, i * 2 * B + B)
            packer.flow_y(2 + through, 2, core, on_y, Y_DIRECT + i * B)
        for i, h in enumerate((through, 1 - through)):
            packer.copy(xb, h * HALF, HALF, on_x, 6 * FLOW + i * HALF)
            packer.copy(xb, h * HALF, HALF, on_y, 6 * B + i * HALF)
    packer.finish()


def pack_own_kernel(place, d, out, position, sem):
    packer = Packer(place, d, position, sem)
    for i, core in enumerate(packer.cores):
        for flow in range(2):
            packer.flow_x(flow, 0, core, out, (i * 2 + flow) * FLOW)
            packer.flow_y(2 + flow, 0, core, out, 4 * FLOW + (i * 2 + flow) * B)
    packer.finish()


def packed(kernel, name, widths, place, d, *more):
    rows = d.shape[0]
    return pl.pallas_call(
        kernel,
        out_shape=[jax.ShapeDtypeStruct((rows, w), jnp.bfloat16) for w in widths],
        in_specs=[SMEM, HBM] + [ANY] * len(more),
        out_specs=[VMEM] * len(widths),
        scratch_shapes=[pltpu.SMEM((32,), jnp.int32), pltpu.SemaphoreType.DMA],
        compiler_params=PARAMS,
        name=name,
    )(place, d, *more)


def contract_rows(a, b):
    return lax.dot_general(a, b, (((0,), (0,)), ((), ())), preferred_element_type=jnp.float32)


def partial_kernel(which, own, xb, x1, x3, y1, y3, f0, f1, f2, f3, out, xs, ds, xt, dt):
    t = own.shape[0]
    wide_at = which * 2 * FLOW
    tall_at = which * 2 * B
    rows = pl.ds(0, t)
    xs[rows, :] = xb[...]
    xt[rows, :] = xb[...]
    ds[rows, :] = own[:, wide_at : wide_at + 2 * FLOW]
    dt[rows, :] = own[:, 4 * FLOW + tall_at : 4 * FLOW + tall_at + 2 * B]
    for i, (on_x, on_y) in enumerate(((x1, y1), (x3, y3))):
        rows = pl.ds((1 + i) * t, t)
        ds[rows, :] = on_x[:, wide_at : wide_at + 2 * FLOW]
        dt[rows, :] = on_y[:, tall_at : tall_at + 2 * B]
        for k, h in enumerate((i, 1 - i)):
            xs[rows, h * HALF : (h + 1) * HALF] = on_x[:, 6 * FLOW + k * HALF : 6 * FLOW + (k + 1) * HALF]
            xt[rows, h * HALF : (h + 1) * HALF] = on_y[:, 6 * B + k * HALF : 6 * B + (k + 1) * HALF]
    rows = pl.ds(3 * t, t)
    for i, (on_x, on_y) in enumerate(((f0, f2), (f1, f3))):
        ds[rows, i * FLOW : (i + 1) * FLOW] = on_x[:, which * FLOW : (which + 1) * FLOW]
        dt[rows, i * B : (i + 1) * B] = on_y[:, which * B : (which + 1) * B]
        xs[rows, i * HALF : (i + 1) * HALF] = on_x[:, 2 * FLOW :]
        xt[rows, i * HALF : (i + 1) * HALF] = on_y[:, 2 * B :]
    out[:, : 2 * FLOW] = contract_rows(xs[...], ds[...]).astype(out.dtype)
    out[:, 2 * FLOW :] = contract_rows(xt[...], dt[...]).astype(out.dtype)


def partials(which, pieces):
    t = pieces[0].shape[0]
    return pl.pallas_call(
        functools.partial(partial_kernel, which),
        out_shape=jax.ShapeDtypeStruct((B, 2 * FLOW + 2 * B), jnp.bfloat16),
        in_specs=[VMEM] * len(pieces),
        out_specs=VMEM,
        scratch_shapes=[
            pltpu.VMEM((4 * t, B), jnp.bfloat16),
            pltpu.VMEM((4 * t, 2 * FLOW), jnp.bfloat16),
            pltpu.VMEM((4 * t, B), jnp.bfloat16),
            pltpu.VMEM((4 * t, 2 * B), jnp.bfloat16),
        ],
        compiler_params=PARAMS,
        name="partials",
    )(*pieces)


def chip_sum_kernel(place, near, far, py0, py1, py2, py3, px0, px1, px2, px3):
    my_y = place[3]
    wide = slice(0, 2 * FLOW)
    for s, ref in enumerate((py0, py1, py2, py3)):
        rows = pl.ds(aligned(my_y ^ s, 128), 128)
        ref[...] = (near[rows, wide].astype(jnp.float32) + far[rows, wide].astype(jnp.float32)).astype(ref.dtype)
    for q, ref in enumerate((px0, px1, px2, px3)):
        for flow in range(2):
            at = slice(2 * FLOW + flow * B + q * 128, 2 * FLOW + flow * B + (q + 1) * 128)
            ref[:, flow * 128 : (flow + 1) * 128] = (
                near[:, at].astype(jnp.float32) + far[:, at].astype(jnp.float32)
            ).astype(ref.dtype)


def chip_sum(place, *parts):
    kinds = [jnp.float32] + [jnp.bfloat16] * 3
    return pl.pallas_call(
        chip_sum_kernel,
        out_shape=[jax.ShapeDtypeStruct((128, 2 * FLOW), k) for k in kinds]
        + [jax.ShapeDtypeStruct((B, 256), k) for k in kinds],
        in_specs=[SMEM] + [VMEM] * 2,
        out_specs=[VMEM] * 8,
        compiler_params=PARAMS,
        name="chip_sum",
    )(place, *parts)


PIECE = 96


def ring_sum_kernel(py0, ry1, ry2, ry3, px0, rx1, rx2, rx3, out):
    wide = py0[...] + ry1[...].astype(jnp.float32) + ry2[...].astype(jnp.float32) + ry3[...].astype(jnp.float32)
    tall = px0[...] + rx1[...].astype(jnp.float32) + rx2[...].astype(jnp.float32) + rx3[...].astype(jnp.float32)
    wide = wide.astype(jnp.bfloat16)
    tall = tall.astype(jnp.bfloat16)
    for z in range(4):
        for low in range(2):
            first = (z * 2 + low) * PIECE
            if z < 2:
                out[first : first + 64, :] = wide[low * 64 : low * 64 + 64, z * FLOW : z * FLOW + B]
            else:
                for g in range(4):
                    from_row = low * 256 + g * 64
                    out[first : first + 64, g * 128 : (g + 1) * 128] = tall[
                        from_row : from_row + 64, (z - 2) * 128 : (z - 1) * 128
                    ]
            for h in range(2):
                for flow in range(2):
                    k = low * 64 + h * 32
                    at = h * 256 + flow * 128
                    out[first + 64 : first + PIECE, at : at + 128] = wide[
                        k : k + 32, flow * FLOW + B : (flow + 1) * FLOW
                    ]


def ring_sum(parts):
    return pl.pallas_call(
        ring_sum_kernel,
        out_shape=jax.ShapeDtypeStruct((8 * PIECE, B), jnp.bfloat16),
        in_specs=[VMEM] * 8,
        out_specs=VMEM,
        compiler_params=PARAMS,
        name="ring_sum",
    )(*parts)


def line_sum_kernel(arrived, out):
    total = arrived[0].astype(jnp.float32)
    for i in range(1, 8):
        total = total + arrived[i].astype(jnp.float32)
    out[...] = total.astype(jnp.bfloat16)


def line_sum(arrived):
    return pl.pallas_call(
        line_sum_kernel,
        out_shape=jax.ShapeDtypeStruct((PIECE, B), jnp.bfloat16),
        in_specs=[VMEM],
        out_specs=VMEM,
        compiler_params=PARAMS,
        name="line_sum",
    )(arrived)


def choose_kernel(place, q0, q1, q2, q3, out, position, held):
    fill_positions(place, position)
    my_x, my_core, my_low = place[1], place[2], place[4]
    mine = position[(place[0] * 4 + my_x) * 2 + my_core]

    @pl.when(mine >= 4)
    def _():
        out[...] = jnp.zeros(out.shape, jnp.bfloat16)

    @pl.when(mine < 4)
    def _():
        for r, ref in enumerate((q0, q1, q2, q3)):
            held[my_x ^ r] = ref[...]
        flow = mine >> 1
        for xl in range(2):
            at_x = 2 * (mine & 1) + xl
            for flip in range(2):
                to = aligned(xl * 2 + (my_core ^ flip), 128)
                for w in range(2):
                    for h in range(2):
                        rows = pl.ds(pl.multiple_of((my_low ^ w) * 64 + h * 32, 32), 32)
                        from_row = (flip * 2 + w) * 32
                        out[rows, pl.ds(to, 128)] = held[
                            at_x, from_row : from_row + 32, pl.ds(aligned(h * 2 + flow, 128), 128)
                        ]


def choose(place, pieces):
    return pl.pallas_call(
        choose_kernel,
        out_shape=jax.ShapeDtypeStruct((128, B), jnp.bfloat16),
        in_specs=[SMEM] + [VMEM] * 4,
        out_specs=VMEM,
        scratch_shapes=[pltpu.SMEM((32,), jnp.int32), pltpu.VMEM((4, 128, B), jnp.bfloat16)],
        compiler_params=PARAMS,
        name="choose",
    )(place, *pieces)


def cast_kernel(left, right, out):
    out[:SLOTS] = left[...].astype(jnp.bfloat16)
    out[SLOTS:] = right[...].astype(jnp.bfloat16)


def cast_rows(left, right):
    return pl.pallas_call(
        cast_kernel,
        out_shape=jax.ShapeDtypeStruct((2 * SLOTS, 64, B), jnp.bfloat16),
        in_specs=[VMEM] * 2,
        out_specs=VMEM,
        compiler_params=PARAMS,
        name="cast_rows",
    )(left, right)


def whole_kernel(place, s0, s1, s2, s3, out):
    for r, piece in enumerate((s0, s1, s2, s3)):
        for w in range(2):
            rows = pl.ds(aligned((place[3] ^ r) * 2 + (place[4] ^ w), 64), 64)
            for k in range(2 * SLOTS):
                out[k, rows, :] = piece[w * 2 * SLOTS + k]


def whole(place, pieces):
    return pl.pallas_call(
        whole_kernel,
        out_shape=jax.ShapeDtypeStruct((2 * SLOTS, B, B), jnp.bfloat16),
        in_specs=[SMEM] + [VMEM] * 4,
        out_specs=VMEM,
        compiler_params=PARAMS,
        name="whole",
    )(place, *pieces)


def root_kernel(slot, place, r0, r1, r2, r3, statistics, left_rows, right_rows, *refs):
    if slot:
        left_first, right_first, directions, left_new, right_new, g_ref, a_ref, m_ref = refs
        left_new[0] = left_first[...]
        right_new[0] = right_first[...]
    else:
        directions, left_new, right_new, g_ref, a_ref, m_ref = refs
    my_z, my_y, my_low = place[0], place[3], place[4]
    node = my_y * 2 + my_low
    first_row = aligned(node, 64)
    for r, piece in enumerate((r0, r1, r2, r3)):
        at_y = my_y ^ r
        if slot:
            g_ref[pl.ds(aligned(at_y, 128), 128), :] = piece[...]
            continue
        for w in range(2):
            at_low = my_low ^ w
            base = w * 64

            @pl.when(my_z < 2)
            def _():
                g_ref[pl.ds(pl.multiple_of(at_y * 128 + at_low * 64, 64), 64), :] = piece[base : base + 64, :]

            @pl.when(my_z >= 2)
            def _():
                for g in range(4):
                    g_ref[
                        pl.ds(pl.multiple_of(at_low * 256 + g * 64, 64), 64),
                        pl.ds(aligned(at_y, 128), 128),
                    ] = piece[base : base + 64, g * 128 : (g + 1) * 128]

    def scaled(gram, old_rows, new_rows, which):
        a_ref[which] = gram
        rows = BETA * old_rows[slot] + a_ref[which, pl.ds(first_row, 64), :] * (1.0 / B)
        if slot:
            new_rows[slot] = rows
        else:
            new_rows[...] = rows
        full = BETA * statistics[which * SLOTS + slot].astype(jnp.float32) + gram * (1.0 / B)
        norm = B * jnp.sqrt(jnp.sum(full * full, keepdims=True) * (1.0 / (B * B)) + 1e-06)
        matrix = full / norm
        a_ref[which] = matrix
        m_ref[which] = matrix.astype(jnp.bfloat16)
        return lax.rsqrt(jnp.sqrt(norm))

    g = g_ref[...]
    left_gram = lax.dot_general(g, g, (((1,), (1,)), ((), ())), preferred_element_type=jnp.float32)
    right_gram = contract_rows(g, g)
    left_scale = scaled(left_gram, left_rows, left_new, 0)
    right_scale = scaled(right_gram, right_rows, right_new, 1)
    power = a_ref[0, pl.ds(first_row, 64), :]
    column = lax.broadcasted_iota(jnp.int32, (64, B), 1)
    row = lax.broadcasted_iota(jnp.int32, (64, B), 0) + first_row
    total = jnp.where(row == column, COEF[0], 0.0) + COEF[1] * power
    for k in range(2, 7):
        power = jnp.dot(power.astype(jnp.bfloat16), m_ref[0], preferred_element_type=jnp.float32)
        total = total + COEF[k] * power
    root = (total * left_scale).astype(jnp.bfloat16)
    half = jnp.dot(root, g, preferred_element_type=jnp.float32).astype(jnp.bfloat16)
    power = half.astype(jnp.float32)
    total = COEF[0] * power
    for k in range(1, 7):
        power = jnp.dot(power.astype(jnp.bfloat16), m_ref[1], preferred_element_type=jnp.float32)
        total = total + COEF[k] * power
    directions[...] = (total * right_scale).astype(jnp.bfloat16)


def roots(slot, place, pieces, statistics, left_rows, right_rows, *first):
    new = jax.ShapeDtypeStruct((SLOTS, 64, B) if slot else (64, B), jnp.float32)
    return pl.pallas_call(
        functools.partial(root_kernel, slot),
        out_shape=[jax.ShapeDtypeStruct((64, B), jnp.bfloat16), new, new],
        in_specs=[SMEM] + [VMEM] * (7 + len(first)),
        out_specs=[VMEM] * 3,
        scratch_shapes=[
            pltpu.VMEM((B, B), jnp.bfloat16),
            pltpu.VMEM((2, B, B), jnp.float32),
            pltpu.VMEM((2, B, B), jnp.bfloat16),
        ],
        compiler_params=PARAMS,
        name="roots",
    )(place, *pieces, statistics, left_rows, right_rows, *first)


def place_kernel(place, *refs):
    sources, out, position, sem = refs[:16], refs[16], refs[17], refs[18]
    fill_positions(place, position)
    my_z, my_x, my_core = place[0], place[1], place[2]
    for wait in (False, True):
        for slot in range(SLOTS):
            for flip in range(2):
                for r in range(4):
                    source = sources[(slot * 2 + flip) * 4 + r]
                    for a in range(4):
                        block = position[((my_z ^ a) * 4 + (my_x ^ r)) * 2 + (my_core ^ flip)]
                        copy = pltpu.make_async_copy(
                            source.at[pl.ds(a * 64, 64), :],
                            out.at[:, pl.ds(aligned(jnp.minimum(block + slot * 32, 35), B), B)],
                            sem,
                        )
                        act = copy.wait if wait else copy.start
                        if slot == 0:
                            act()
                        else:
                            pl.when(block < 4)(act)


def put_blocks(place, sources, blocks):
    return pl.pallas_call(
        place_kernel,
        out_shape=jax.ShapeDtypeStruct((64, blocks * B), jnp.bfloat16),
        in_specs=[SMEM] + [ANY] * 16,
        out_specs=ANY,
        scratch_shapes=[pltpu.SMEM((32,), jnp.int32), pltpu.SemaphoreType.DMA],
        compiler_params=PARAMS,
        name="put_blocks",
    )(place, *sources)


def around_z(rows):
    a2, a1, a3 = swap(rows, "z_hi", 2), swap(rows, "z_hi", 1), swap(rows, "z_hi", 3)
    return jnp.concatenate([rows, a1, a2, a3])


def around_x(plane):
    b2, b1, b3 = swap(plane, "x", 2), swap(plane, "x", 1), swap(plane, "x", 3)
    return plane, b1, b2, b3


def shards(x_band, d_gate_up, owner, stat_left, stat_right):
    place = jnp.concatenate([jnp.stack([lax.axis_index(a) for a in FINE]).astype(jnp.int32), owner])
    bucket = d_gate_up.shape[1] // B

    x1, x3, y1, y3 = packed(pack_kernel, "pack", [X_MSG] * 2 + [Y_MSG] * 2, place, d_gate_up, x_band)
    x1, x3, y1, y3 = swap(x1, "x", 1), swap(x3, "x", 3), swap(y1, "y", 1), swap(y3, "y", 3)
    (own,) = packed(pack_own_kernel, "pack_own", [OWN_MSG], place, d_gate_up)
    statistics = cast_rows(stat_left[0], stat_right[0])
    statistics = jnp.concatenate([statistics, swap(statistics, "z_lo", 1)])
    f0, f1 = swap(x1[:, X_FWD], "x", 3), swap(x3[:, X_FWD], "x", 1)
    y1_on, y3_on, statistics = lax.optimization_barrier((y1[:, Y_FWD], y3[:, Y_FWD], statistics))
    f2, f3 = swap(y1_on, "y", 3), swap(y3_on, "y", 1)
    pieces = (own, x_band, x1, x3, y1, y3, f0, f1, f2, f3)
    far_sum = swap(partials(1, pieces), "core", 1)
    py0, py1, py2, py3, px0, px1, px2, px3 = chip_sum(place, partials(0, pieces), far_sum)
    ry2, rx2 = swap(py2, "y", 2), swap(px2, "x", 2)
    ry1, rx1 = swap(py1, "y", 1), swap(px1, "x", 1)
    ry3, rx3 = swap(py3, "y", 3), swap(px3, "x", 3)
    message = ring_sum((py0, ry1, ry2, ry3, px0, rx1, rx2, rx3))

    message, statistics = lax.optimization_barrier((message, statistics))
    s2, s1, s3 = swap(statistics, "y", 2), swap(statistics, "y", 1), swap(statistics, "y", 3)
    message = lax.all_to_all(message, ("z_hi", "z_lo"), 0, 0, tiled=True)
    line = line_sum(message.reshape(8, PIECE, B))

    main, extra = line[:64], line[64:]
    far = swap(line, "z_lo", 1)
    extra_core = swap(extra, "core", 1)
    diagonal = [(c * 2 + w, 3 - (c * 2 + w)) for c in range(2) for w in range(2)]
    extra_far = lax.ppermute(extra, ("core", "z_lo"), diagonal)
    m0 = jnp.concatenate([main, far[:64]])
    m0, s1, s2, s3 = lax.optimization_barrier((m0, s1, s2, s3))
    statistics = whole(place, (statistics, s1, s2, s3))
    m2, m1, m3 = swap(m0, "y", 2), swap(m0, "y", 1), swap(m0, "y", 3)
    q0 = jnp.concatenate([extra, far[64:], extra_core, extra_far])
    q2, q1, q3 = swap(q0, "x", 2), swap(q0, "x", 1), swap(q0, "x", 3)
    first, left_first, right_first = roots(0, place, (m0, m1, m2, m3), statistics, stat_left[0], stat_right[0])
    e0 = choose(place, (q0, q1, q2, q3))
    e2, e1, e3 = swap(e0, "y", 2), swap(e0, "y", 1), swap(e0, "y", 3)
    first, e1, e2, e3 = lax.optimization_barrier((first, e1, e2, e3))
    second, left_new, right_new = roots(
        1, place, (e0, e1, e2, e3), statistics, stat_left[0], stat_right[0], left_first, right_first
    )
    plane = around_z(first)
    _, second = lax.optimization_barrier((plane, second))
    first = around_x(plane)
    plane = around_z(second)
    first, _ = lax.optimization_barrier((first, plane))
    second = around_x(plane)
    blocks = [swap(v, "core", mask) if mask else v for part in (first, second) for mask in range(2) for v in part]
    out = put_blocks(place, blocks, bucket)
    return (out, left_new[None], right_new[None])


def solution(mesh):
    fine = Mesh(np.asarray(mesh.devices).reshape(FINE_SIZES), FINE)
    dp, node = FINE[:3], FINE[3:]
    placed = (P(dp + node, None), P(dp + node, None), P(), P(dp, None, node, None), P(dp, None, node, None))
    return jax.shard_map(
        shards,
        mesh=fine,
        in_specs=placed,
        out_specs=(P(node, None), P(dp, None, node, None), P(dp, None, node, None)),
        check_vma=False,
    )
```

```python
import functools
import math

import jax
import jax.numpy as jnp
import numpy as np
from jax import lax
from jax.experimental import pallas as pl
from jax.experimental.pallas import tpu as pltpu
from jax.sharding import Mesh, PartitionSpec as P

B = 512
SLOTS = 2
BETA = 0.9
EXTRA_CHUNK = 128
FLOW = B + EXTRA_CHUNK
HALF = B // 2

FINE = ("z_hi", "x", "core", "y", "z_lo")
FINE_SIZES = (4, 4, 2, 4, 2)
VMEM_LIMIT = 24 * 1024 * 1024

COEF = [6.25 / 4, -(1.25 + 1.25**5) / 4] + [
    -math.comb(5, k) * 1.25 ** (5 - k) * (-0.25) ** k / 4 for k in range(1, 6)
]

ANY = pl.BlockSpec(memory_space=pl.ANY)
HBM = pl.BlockSpec(memory_space=pltpu.HBM)
SMEM = pl.BlockSpec(memory_space=pltpu.SMEM)
VMEM = pl.BlockSpec(memory_space=pltpu.VMEM)
PARAMS = pltpu.CompilerParams(vmem_limit_bytes=VMEM_LIMIT)


def swap(value, axis, mask):
    size = FINE_SIZES[FINE.index(axis)]
    return lax.ppermute(value, axis, [(i, i ^ mask) for i in range(size)])


def aligned(index, step):
    return pl.multiple_of(index * step, step)


def fill_positions(place, position):
    for block in range(32):
        position[place[len(FINE) + block]] = block


X_DIRECT = 4 * FLOW
X_MSG = 6 * FLOW + B
Y_DIRECT = 4 * B
Y_MSG = 6 * B + B
OWN_MSG = 4 * FLOW + 4 * B
X_FWD = slice(X_DIRECT, 6 * FLOW + HALF)
Y_FWD = slice(Y_DIRECT, 6 * B + HALF)


class Packer:
    def __init__(self, place, d, position, sem):
        fill_positions(place, position)
        self.position, self.place, self.d, self.sem = position, place, d, sem
        self.cores = (place[2], 1 - place[2])
        self.copies = []

    def copy(self, source, first, width, target, at):
        self.copies.append(
            pltpu.make_async_copy(source.at[:, pl.ds(first, width)], target.at[:, pl.ds(at, width)], self.sem)
        )
        self.copies[-1].start()

    def flow_x(self, flow, r, core, target, at):
        to_x = self.place[1] ^ r
        block = self.position[(flow * 4 + to_x) * 2 + core]
        self.copy(self.d, aligned(block, B), B, target, at)
        chunk = 32 * B // EXTRA_CHUNK + flow * 8 + to_x * 2 + core
        self.copy(self.d, aligned(chunk, EXTRA_CHUNK), EXTRA_CHUNK, target, at + B)

    def flow_y(self, flow, r, core, target, at):
        to_y = self.place[3] ^ r
        for q in range(4):
            block = self.position[(flow * 4 + (self.place[1] ^ q)) * 2 + core]
            self.copy(self.d, pl.multiple_of(block * B + to_y * 128, 128), 128, target, at + q * 128)

    def finish(self):
        for c in self.copies:
            c.wait()


NEIGHBOURS = ((1, 0), (3, 1))


def pack_x_kernel(place, d, xb, x1, x3, position, sem):
    packer = Packer(place, d, position, sem)
    for (near, through), out in zip(NEIGHBOURS, (x1, x3)):
        for i, core in enumerate(packer.cores):
            packer.flow_x(0, near, core, out, i * 2 * FLOW)
            packer.flow_x(1, near, core, out, i * 2 * FLOW + FLOW)
            packer.flow_x(through, 2, core, out, X_DIRECT + i * FLOW)
        for i, h in enumerate((through, 1 - through)):
            packer.copy(xb, h * HALF, HALF, out, 6 * FLOW + i * HALF)
    packer.finish()


def pack_y_kernel(place, d, xb, y1, y3, position, sem):
    packer = Packer(place, d, position, sem)
    for (near, through), out in zip(NEIGHBOURS, (y1, y3)):
        for i, core in enumerate(packer.cores):
            packer.flow_y(2, near, core, out, i * 2 * B)
            packer.flow_y(3, near, core, out, i * 2 * B + B)
            packer.flow_y(2 + through, 2, core, out, Y_DIRECT + i * B)
        for i, h in enumerate((through, 1 - through)):
            packer.copy(xb, h * HALF, HALF, out, 6 * B + i * HALF)
    packer.finish()


def pack_own_kernel(place, d, out, position, sem):
    packer = Packer(place, d, position, sem)
    for i, core in enumerate(packer.cores):
        for flow in range(2):
            packer.flow_x(flow, 0, core, out, (i * 2 + flow) * FLOW)
            packer.flow_y(2 + flow, 0, core, out, 4 * FLOW + (i * 2 + flow) * B)
    packer.finish()


def packed(kernel, name, widths, place, d, *more):
    rows = d.shape[0]
    return pl.pallas_call(
        kernel,
        out_shape=[jax.ShapeDtypeStruct((rows, w), jnp.bfloat16) for w in widths],
        in_specs=[SMEM, HBM] + [ANY] * len(more),
        out_specs=[VMEM] * len(widths),
        scratch_shapes=[pltpu.SMEM((32,), jnp.int32), pltpu.SemaphoreType.DMA],
        compiler_params=PARAMS,
        name=name,
    )(place, d, *more)


def contract_rows(a, b):
    return lax.dot_general(a, b, (((0,), (0,)), ((), ())), preferred_element_type=jnp.float32)


def partial_kernel(which, width, own_at, own, xb, near1, near3, far1, far3, out, xs, ds):
    t = own.shape[0]
    keep = 2 * width
    at = which * keep
    rows = pl.ds(0, t)
    xs[rows, :] = xb[...]
    ds[rows, :] = own[:, own_at + at : own_at + at + keep]
    for i, ref in enumerate((near1, near3)):
        rows = pl.ds((1 + i) * t, t)
        ds[rows, :] = ref[:, at : at + keep]
        for k, h in enumerate((i, 1 - i)):
            xs[rows, h * HALF : (h + 1) * HALF] = ref[:, 6 * width + k * HALF : 6 * width + (k + 1) * HALF]
    rows = pl.ds(3 * t, t)
    for i, ref in enumerate((far1, far3)):
        ds[rows, i * width : (i + 1) * width] = ref[:, which * width : (which + 1) * width]
        xs[rows, i * HALF : (i + 1) * HALF] = ref[:, 2 * width :]
    out[...] = contract_rows(xs[...], ds[...]).astype(out.dtype)


def partials(which, width, own_at, pieces):
    t = pieces[0].shape[0]
    return pl.pallas_call(
        functools.partial(partial_kernel, which, width, own_at),
        out_shape=jax.ShapeDtypeStruct((B, 2 * width), jnp.bfloat16),
        in_specs=[VMEM] * len(pieces),
        out_specs=VMEM,
        scratch_shapes=[pltpu.VMEM((4 * t, B), jnp.bfloat16), pltpu.VMEM((4 * t, 2 * width), jnp.bfloat16)],
        compiler_params=PARAMS,
        name="partials",
    )(*pieces)


def wide_sum_kernel(place, near, far, *outs):
    for s, ref in enumerate(outs):
        rows = pl.ds(aligned(place[3] ^ s, 128), 128)
        ref[...] = (near[rows, :].astype(jnp.float32) + far[rows, :].astype(jnp.float32)).astype(ref.dtype)


def tall_sum_kernel(place, near, far, *outs):
    for q, ref in enumerate(outs):
        for flow in range(2):
            at = slice(flow * B + q * 128, flow * B + (q + 1) * 128)
            ref[:, flow * 128 : (flow + 1) * 128] = (
                near[:, at].astype(jnp.float32) + far[:, at].astype(jnp.float32)
            ).astype(ref.dtype)


def chip_sum(kernel, name, shape, place, near, far):
    return pl.pallas_call(
        kernel,
        out_shape=[jax.ShapeDtypeStruct(shape, k) for k in [jnp.float32] + [jnp.bfloat16] * 3],
        in_specs=[SMEM] + [VMEM] * 2,
        out_specs=[VMEM] * 4,
        compiler_params=PARAMS,
        name=name,
    )(place, near, far)


PIECE = 96


def ring_sum_kernel(ry1, rx1, ry3, rx3, ry2, rx2, py0, px0, out):
    wide = py0[...] + ry1[...].astype(jnp.float32) + ry2[...].astype(jnp.float32) + ry3[...].astype(jnp.float32)
    tall = px0[...] + rx1[...].astype(jnp.float32) + rx2[...].astype(jnp.float32) + rx3[...].astype(jnp.float32)
    wide = wide.astype(jnp.bfloat16)
    tall = tall.astype(jnp.bfloat16)
    for z in range(4):
        for low in range(2):
            first = (z * 2 + low) * PIECE
            if z < 2:
                out[first : first + 64, :] = wide[low * 64 : low * 64 + 64, z * FLOW : z * FLOW + B]
            else:
                for g in range(4):
                    from_row = low * 256 + g * 64
                    out[first : first + 64, g * 128 : (g + 1) * 128] = tall[
                        from_row : from_row + 64, (z - 2) * 128 : (z - 1) * 128
                    ]
            for h in range(2):
                for flow in range(2):
                    k = low * 64 + h * 32
                    at = h * 256 + flow * 128
                    out[first + 64 : first + PIECE, at : at + 128] = wide[
                        k : k + 32, flow * FLOW + B : (flow + 1) * FLOW
                    ]


def ring_sum(parts):
    return pl.pallas_call(
        ring_sum_kernel,
        out_shape=jax.ShapeDtypeStruct((8 * PIECE, B), jnp.bfloat16),
        in_specs=[VMEM] * 8,
        out_specs=VMEM,
        compiler_params=PARAMS,
        name="ring_sum",
    )(*parts)


def line_sum_kernel(arrived, out):
    total = arrived[0].astype(jnp.float32)
    for i in range(1, 8):
        total = total + arrived[i].astype(jnp.float32)
    out[...] = total.astype(jnp.bfloat16)


def line_sum(arrived):
    return pl.pallas_call(
        line_sum_kernel,
        out_shape=jax.ShapeDtypeStruct((PIECE, B), jnp.bfloat16),
        in_specs=[VMEM],
        out_specs=VMEM,
        compiler_params=PARAMS,
        name="line_sum",
    )(arrived)


def choose_kernel(place, q0, q1, q2, q3, out, position, held):
    fill_positions(place, position)
    my_x, my_core, my_low = place[1], place[2], place[4]
    mine = position[(place[0] * 4 + my_x) * 2 + my_core]

    @pl.when(mine >= 4)
    def _():
        out[...] = jnp.zeros(out.shape, jnp.bfloat16)

    @pl.when(mine < 4)
    def _():
        for r, ref in enumerate((q0, q1, q2, q3)):
            held[my_x ^ r] = ref[...]
        flow = mine >> 1
        for xl in range(2):
            at_x = 2 * (mine & 1) + xl
            for flip in range(2):
                to = aligned(xl * 2 + (my_core ^ flip), 128)
                for w in range(2):
                    for h in range(2):
                        rows = pl.ds(pl.multiple_of((my_low ^ w) * 64 + h * 32, 32), 32)
                        from_row = (flip * 2 + w) * 32
                        out[rows, pl.ds(to, 128)] = held[
                            at_x, from_row : from_row + 32, pl.ds(aligned(h * 2 + flow, 128), 128)
                        ]


def choose(place, pieces):
    return pl.pallas_call(
        choose_kernel,
        out_shape=jax.ShapeDtypeStruct((128, B), jnp.bfloat16),
        in_specs=[SMEM] + [VMEM] * 4,
        out_specs=VMEM,
        scratch_shapes=[pltpu.SMEM((32,), jnp.int32), pltpu.VMEM((4, 128, B), jnp.bfloat16)],
        compiler_params=PARAMS,
        name="choose",
    )(place, *pieces)


def cast_kernel(left, right, out):
    out[:SLOTS] = left[...].astype(jnp.bfloat16)
    out[SLOTS:] = right[...].astype(jnp.bfloat16)


def cast_rows(left, right):
    return pl.pallas_call(
        cast_kernel,
        out_shape=jax.ShapeDtypeStruct((2 * SLOTS, 64, B), jnp.bfloat16),
        in_specs=[VMEM] * 2,
        out_specs=VMEM,
        compiler_params=PARAMS,
        name="cast_rows",
    )(left, right)


def whole_kernel(place, s0, s1, s2, s3, out):
    for r, piece in enumerate((s0, s1, s2, s3)):
        for w in range(2):
            rows = pl.ds(aligned((place[3] ^ r) * 2 + (place[4] ^ w), 64), 64)
            for k in range(2 * SLOTS):
                out[k, rows, :] = piece[w * 2 * SLOTS + k]


def whole(place, pieces):
    return pl.pallas_call(
        whole_kernel,
        out_shape=jax.ShapeDtypeStruct((2 * SLOTS, B, B), jnp.bfloat16),
        in_specs=[SMEM] + [VMEM] * 4,
        out_specs=VMEM,
        compiler_params=PARAMS,
        name="whole",
    )(place, *pieces)


def root_kernel(slot, place, r0, r1, r2, r3, statistics, left_rows, right_rows, *refs):
    if slot:
        left_first, right_first, directions, left_new, right_new, g_ref, a_ref, m_ref = refs
        left_new[0] = left_first[...]
        right_new[0] = right_first[...]
    else:
        directions, left_new, right_new, g_ref, a_ref, m_ref = refs
    my_z, my_y, my_low = place[0], place[3], place[4]
    node = my_y * 2 + my_low
    first_row = aligned(node, 64)
    for r, piece in enumerate((r0, r1, r2, r3)):
        at_y = my_y ^ r
        if slot:
            g_ref[pl.ds(aligned(at_y, 128), 128), :] = piece[...]
            continue
        for w in range(2):
            at_low = my_low ^ w
            base = w * 64

            @pl.when(my_z < 2)
            def _():
                g_ref[pl.ds(pl.multiple_of(at_y * 128 + at_low * 64, 64), 64), :] = piece[base : base + 64, :]

            @pl.when(my_z >= 2)
            def _():
                for g in range(4):
                    g_ref[
                        pl.ds(pl.multiple_of(at_low * 256 + g * 64, 64), 64),
                        pl.ds(aligned(at_y, 128), 128),
                    ] = piece[base : base + 64, g * 128 : (g + 1) * 128]

    def scaled(gram, old_rows, new_rows, which):
        a_ref[which] = gram
        rows = BETA * old_rows[slot] + a_ref[which, pl.ds(first_row, 64), :] * (1.0 / B)
        if slot:
            new_rows[slot] = rows
        else:
            new_rows[...] = rows
        full = BETA * statistics[which * SLOTS + slot].astype(jnp.float32) + gram * (1.0 / B)
        norm = B * jnp.sqrt(jnp.sum(full * full, keepdims=True) * (1.0 / (B * B)) + 1e-06)
        matrix = full / norm
        a_ref[which] = matrix
        m_ref[which] = matrix.astype(jnp.bfloat16)
        return lax.rsqrt(jnp.sqrt(norm))

    g = g_ref[...]
    left_gram = lax.dot_general(g, g, (((1,), (1,)), ((), ())), preferred_element_type=jnp.float32)
    right_gram = contract_rows(g, g)
    left_scale = scaled(left_gram, left_rows, left_new, 0)
    right_scale = scaled(right_gram, right_rows, right_new, 1)
    power = a_ref[0, pl.ds(first_row, 64), :]
    column = lax.broadcasted_iota(jnp.int32, (64, B), 1)
    row = lax.broadcasted_iota(jnp.int32, (64, B), 0) + first_row
    total = jnp.where(row == column, COEF[0], 0.0) + COEF[1] * power
    for k in range(2, 7):
        power = jnp.dot(power.astype(jnp.bfloat16), m_ref[0], preferred_element_type=jnp.float32)
        total = total + COEF[k] * power
    root = (total * left_scale).astype(jnp.bfloat16)
    half = jnp.dot(root, g, preferred_element_type=jnp.float32).astype(jnp.bfloat16)
    power = half.astype(jnp.float32)
    total = COEF[0] * power
    for k in range(1, 7):
        power = jnp.dot(power.astype(jnp.bfloat16), m_ref[1], preferred_element_type=jnp.float32)
        total = total + COEF[k] * power
    directions[...] = (total * right_scale).astype(jnp.bfloat16)


def roots(slot, place, pieces, statistics, left_rows, right_rows, *first):
    new = jax.ShapeDtypeStruct((SLOTS, 64, B) if slot else (64, B), jnp.float32)
    return pl.pallas_call(
        functools.partial(root_kernel, slot),
        out_shape=[jax.ShapeDtypeStruct((64, B), jnp.bfloat16), new, new],
        in_specs=[SMEM] + [VMEM] * (7 + len(first)),
        out_specs=[VMEM] * 3,
        scratch_shapes=[
            pltpu.VMEM((B, B), jnp.bfloat16),
            pltpu.VMEM((2, B, B), jnp.float32),
            pltpu.VMEM((2, B, B), jnp.bfloat16),
        ],
        compiler_params=PARAMS,
        name="roots",
    )(place, *pieces, statistics, left_rows, right_rows, *first)


def place_kernel(place, *refs):
    sources, out, position, sem = refs[:16], refs[16], refs[17], refs[18]
    fill_positions(place, position)
    my_z, my_x, my_core = place[0], place[1], place[2]
    for wait in (False, True):
        for slot in range(SLOTS):
            for flip in range(2):
                for r in range(4):
                    source = sources[(slot * 2 + flip) * 4 + r]
                    for a in range(4):
                        block = position[((my_z ^ a) * 4 + (my_x ^ r)) * 2 + (my_core ^ flip)]
                        copy = pltpu.make_async_copy(
                            source.at[pl.ds(a * 64, 64), :],
                            out.at[:, pl.ds(aligned(jnp.minimum(block + slot * 32, 35), B), B)],
                            sem,
                        )
                        act = copy.wait if wait else copy.start
                        if slot == 0:
                            act()
                        else:
                            pl.when(block < 4)(act)


def put_blocks(place, sources, blocks):
    return pl.pallas_call(
        place_kernel,
        out_shape=jax.ShapeDtypeStruct((64, blocks * B), jnp.bfloat16),
        in_specs=[SMEM] + [ANY] * 16,
        out_specs=ANY,
        scratch_shapes=[pltpu.SMEM((32,), jnp.int32), pltpu.SemaphoreType.DMA],
        compiler_params=PARAMS,
        name="put_blocks",
    )(place, *sources)


def around_z(rows):
    a2, a1, a3 = swap(rows, "z_hi", 2), swap(rows, "z_hi", 1), swap(rows, "z_hi", 3)
    return jnp.concatenate([rows, a1, a2, a3])


def around_x(plane):
    b2, b1, b3 = swap(plane, "x", 2), swap(plane, "x", 1), swap(plane, "x", 3)
    return plane, b1, b2, b3


def shards(x_band, d_gate_up, owner, stat_left, stat_right):
    place = jnp.concatenate([jnp.stack([lax.axis_index(a) for a in FINE]).astype(jnp.int32), owner])
    bucket = d_gate_up.shape[1] // B

    x1, x3 = packed(pack_x_kernel, "pack_x", [X_MSG] * 2, place, d_gate_up, x_band)
    x1, x3 = swap(x1, "x", 1), swap(x3, "x", 3)
    y1, y3 = packed(pack_y_kernel, "pack_y", [Y_MSG] * 2, place, d_gate_up, x_band)
    y1, y3 = swap(y1, "y", 1), swap(y3, "y", 3)
    (own,) = packed(pack_own_kernel, "pack_own", [OWN_MSG], place, d_gate_up)
    statistics = cast_rows(stat_left[0], stat_right[0])
    statistics = jnp.concatenate([statistics, swap(statistics, "z_lo", 1)])
    f0, f1 = swap(x1[:, X_FWD], "x", 3), swap(x3[:, X_FWD], "x", 1)
    y1_on, y3_on, statistics = lax.optimization_barrier((y1[:, Y_FWD], y3[:, Y_FWD], statistics))
    f2, f3 = swap(y1_on, "y", 3), swap(y3_on, "y", 1)
    on_x, on_y = (own, x_band, x1, x3, f0, f1), (own, x_band, y1, y3, f2, f3)
    far_wide = swap(partials(1, FLOW, 0, on_x), "core", 1)
    far_tall = swap(partials(1, B, 4 * FLOW, on_y), "core", 1)
    wide, tall = partials(0, FLOW, 0, on_x), partials(0, B, 4 * FLOW, on_y)
    py0, py1, py2, py3 = chip_sum(wide_sum_kernel, "wide_sum", (128, 2 * FLOW), place, wide, far_wide)
    px0, px1, px2, px3 = chip_sum(tall_sum_kernel, "tall_sum", (B, 256), place, tall, far_tall)
    ry1, rx1 = swap(py1, "y", 1), swap(px1, "x", 1)
    ry3, rx3 = swap(py3, "y", 3), swap(px3, "x", 3)
    ry2, rx2 = swap(py2, "y", 2), swap(px2, "x", 2)
    message = ring_sum((ry1, rx1, ry3, rx3, ry2, rx2, py0, px0))

    message, statistics = lax.optimization_barrier((message, statistics))
    s2, s1, s3 = swap(statistics, "y", 2), swap(statistics, "y", 1), swap(statistics, "y", 3)
    message = lax.all_to_all(message, ("z_hi", "z_lo"), 0, 0, tiled=True)
    line = line_sum(message.reshape(8, PIECE, B))

    main, extra = line[:64], line[64:]
    far = swap(line, "z_lo", 1)
    extra_core = swap(extra, "core", 1)
    diagonal = [(c * 2 + w, 3 - (c * 2 + w)) for c in range(2) for w in range(2)]
    extra_far = lax.ppermute(extra, ("core", "z_lo"), diagonal)
    m0 = jnp.concatenate([main, far[:64]])
    m0, s1, s2, s3 = lax.optimization_barrier((m0, s1, s2, s3))
    statistics = whole(place, (statistics, s1, s2, s3))
    m2, m1, m3 = swap(m0, "y", 2), swap(m0, "y", 1), swap(m0, "y", 3)
    q0 = jnp.concatenate([extra, far[64:], extra_core, extra_far])
    q2, q1, q3 = swap(q0, "x", 2), swap(q0, "x", 1), swap(q0, "x", 3)
    first, left_first, right_first = roots(0, place, (m0, m1, m2, m3), statistics, stat_left[0], stat_right[0])
    e0 = choose(place, (q0, q1, q2, q3))
    e2, e1, e3 = swap(e0, "y", 2), swap(e0, "y", 1), swap(e0, "y", 3)
    first, e1, e2, e3 = lax.optimization_barrier((first, e1, e2, e3))
    second, left_new, right_new = roots(
        1, place, (e0, e1, e2, e3), statistics, stat_left[0], stat_right[0], left_first, right_first
    )
    plane = around_z(first)
    _, second = lax.optimization_barrier((plane, second))
    first = around_x(plane)
    plane = around_z(second)
    first, _ = lax.optimization_barrier((first, plane))
    second = around_x(plane)
    blocks = [swap(v, "core", mask) if mask else v for part in (first, second) for mask in range(2) for v in part]
    out = put_blocks(place, blocks, bucket)
    return (out, left_new[None], right_new[None])


def solution(mesh):
    fine = Mesh(np.asarray(mesh.devices).reshape(FINE_SIZES), FINE)
    dp, node = FINE[:3], FINE[3:]
    placed = (P(dp + node, None), P(dp + node, None), P(), P(dp, None, node, None), P(dp, None, node, None))
    return jax.shard_map(
        shards,
        mesh=fine,
        in_specs=placed,
        out_specs=(P(node, None), P(dp, None, node, None), P(dp, None, node, None)),
        check_vma=False,
    )
```

```python
import functools
import math

import jax
import jax.numpy as jnp
import numpy as np
from jax import lax
from jax.experimental import pallas as pl
from jax.experimental.pallas import tpu as pltpu
from jax.sharding import Mesh, PartitionSpec as P

B = 512
SLOTS = 2
BETA = 0.9
EXTRA_CHUNK = 128
FLOW = B + EXTRA_CHUNK
HALF = B // 2

FINE = ("z_hi", "x", "core", "y", "z_lo")
FINE_SIZES = (4, 4, 2, 4, 2)
VMEM_LIMIT = 24 * 1024 * 1024

COEF = [6.25 / 4, -(1.25 + 1.25**5) / 4] + [
    -math.comb(5, k) * 1.25 ** (5 - k) * (-0.25) ** k / 4 for k in range(1, 6)
]

ANY = pl.BlockSpec(memory_space=pl.ANY)
HBM = pl.BlockSpec(memory_space=pltpu.HBM)
SMEM = pl.BlockSpec(memory_space=pltpu.SMEM)
VMEM = pl.BlockSpec(memory_space=pltpu.VMEM)
PARAMS = pltpu.CompilerParams(vmem_limit_bytes=VMEM_LIMIT)


def swap(value, axis, mask):
    size = FINE_SIZES[FINE.index(axis)]
    return lax.ppermute(value, axis, [(i, i ^ mask) for i in range(size)])


def aligned(index, step):
    return pl.multiple_of(index * step, step)


def fill_positions(place, position):
    for block in range(32):
        position[place[len(FINE) + block]] = block


X_DIRECT = 4 * FLOW
X_MSG = 6 * FLOW + B
Y_DIRECT = 4 * B
Y_MSG = 6 * B + B
OWN_MSG = 4 * FLOW + 4 * B
X_FWD = slice(X_DIRECT, 6 * FLOW + HALF)
Y_FWD = slice(Y_DIRECT, 6 * B + HALF)


class Packer:
    def __init__(self, place, d, position, sem):
        fill_positions(place, position)
        self.position, self.place, self.d, self.sem = position, place, d, sem
        self.cores = (place[2], 1 - place[2])
        self.copies = []

    def copy(self, source, first, width, target, at):
        self.copies.append(
            pltpu.make_async_copy(source.at[:, pl.ds(first, width)], target.at[:, pl.ds(at, width)], self.sem)
        )
        self.copies[-1].start()

    def flow_x(self, flow, r, core, target, at):
        to_x = self.place[1] ^ r
        block = self.position[(flow * 4 + to_x) * 2 + core]
        self.copy(self.d, aligned(block, B), B, target, at)
        chunk = 32 * B // EXTRA_CHUNK + flow * 8 + to_x * 2 + core
        self.copy(self.d, aligned(chunk, EXTRA_CHUNK), EXTRA_CHUNK, target, at + B)

    def flow_y(self, flow, r, core, target, at):
        to_y = self.place[3] ^ r
        for q in range(4):
            block = self.position[(flow * 4 + (self.place[1] ^ q)) * 2 + core]
            self.copy(self.d, pl.multiple_of(block * B + to_y * 128, 128), 128, target, at + q * 128)

    def finish(self):
        for c in self.copies:
            c.wait()


NEIGHBOURS = ((1, 0), (3, 1))


def pack_x_kernel(place, d, xb, x1, x3, position, sem):
    packer = Packer(place, d, position, sem)
    for (near, through), out in zip(NEIGHBOURS, (x1, x3)):
        for i, core in enumerate(packer.cores):
            packer.flow_x(0, near, core, out, i * 2 * FLOW)
            packer.flow_x(1, near, core, out, i * 2 * FLOW + FLOW)
            packer.flow_x(through, 2, core, out, X_DIRECT + i * FLOW)
        for i, h in enumerate((through, 1 - through)):
            packer.copy(xb, h * HALF, HALF, out, 6 * FLOW + i * HALF)
    packer.finish()


def pack_y_kernel(place, d, xb, y1, y3, position, sem):
    packer = Packer(place, d, position, sem)
    for (near, through), out in zip(NEIGHBOURS, (y1, y3)):
        for i, core in enumerate(packer.cores):
            packer.flow_y(2, near, core, out, i * 2 * B)
            packer.flow_y(3, near, core, out, i * 2 * B + B)
            packer.flow_y(2 + through, 2, core, out, Y_DIRECT + i * B)
        for i, h in enumerate((through, 1 - through)):
            packer.copy(xb, h * HALF, HALF, out, 6 * B + i * HALF)
    packer.finish()


def pack_own_kernel(place, d, out, position, sem):
    packer = Packer(place, d, position, sem)
    for i, core in enumerate(packer.cores):
        for flow in range(2):
            packer.flow_x(flow, 0, core, out, (i * 2 + flow) * FLOW)
            packer.flow_y(2 + flow, 0, core, out, 4 * FLOW + (i * 2 + flow) * B)
    packer.finish()


PACK_PARAMS = pltpu.CompilerParams(vmem_limit_bytes=50 * 1024 * 1024)


def packed(kernel, name, widths, place, d, *more):
    rows = d.shape[0]
    return pl.pallas_call(
        kernel,
        out_shape=[jax.ShapeDtypeStruct((rows, w), jnp.bfloat16) for w in widths],
        in_specs=[SMEM, HBM] + [ANY] * len(more),
        out_specs=[VMEM] * len(widths),
        scratch_shapes=[pltpu.SMEM((32,), jnp.int32), pltpu.SemaphoreType.DMA],
        compiler_params=PACK_PARAMS,
        name=name,
    )(place, d, *more)


def contract_rows(a, b):
    return lax.dot_general(a, b, (((0,), (0,)), ((), ())), preferred_element_type=jnp.float32)


def partial_kernel(which, width, own_at, own, xb, near1, near3, far1, far3, out, xs, ds):
    t = own.shape[0]
    keep = 2 * width
    at = which * keep
    rows = pl.ds(0, t)
    xs[rows, :] = xb[...]
    ds[rows, :] = own[:, own_at + at : own_at + at + keep]
    for i, ref in enumerate((near1, near3)):
        rows = pl.ds((1 + i) * t, t)
        ds[rows, :] = ref[:, at : at + keep]
        for k, h in enumerate((i, 1 - i)):
            xs[rows, h * HALF : (h + 1) * HALF] = ref[:, 6 * width + k * HALF : 6 * width + (k + 1) * HALF]
    rows = pl.ds(3 * t, t)
    for i, ref in enumerate((far1, far3)):
        ds[rows, i * width : (i + 1) * width] = ref[:, which * width : (which + 1) * width]
        xs[rows, i * HALF : (i + 1) * HALF] = ref[:, 2 * width :]
    out[...] = contract_rows(xs[...], ds[...]).astype(out.dtype)


def partials(which, width, own_at, pieces):
    t = pieces[0].shape[0]
    return pl.pallas_call(
        functools.partial(partial_kernel, which, width, own_at),
        out_shape=jax.ShapeDtypeStruct((B, 2 * width), jnp.bfloat16),
        in_specs=[VMEM] * len(pieces),
        out_specs=VMEM,
        scratch_shapes=[pltpu.VMEM((4 * t, B), jnp.bfloat16), pltpu.VMEM((4 * t, 2 * width), jnp.bfloat16)],
        compiler_params=PARAMS,
        name="partials",
    )(*pieces)


def wide_sum_kernel(place, near, far, *outs):
    for s, ref in enumerate(outs):
        rows = pl.ds(aligned(place[3] ^ s, 128), 128)
        ref[...] = (near[rows, :].astype(jnp.float32) + far[rows, :].astype(jnp.float32)).astype(ref.dtype)


def tall_sum_kernel(place, near, far, *outs):
    for q, ref in enumerate(outs):
        for flow in range(2):
            at = slice(flow * B + q * 128, flow * B + (q + 1) * 128)
            ref[:, flow * 128 : (flow + 1) * 128] = (
                near[:, at].astype(jnp.float32) + far[:, at].astype(jnp.float32)
            ).astype(ref.dtype)


def chip_sum(kernel, name, shape, place, near, far):
    return pl.pallas_call(
        kernel,
        out_shape=[jax.ShapeDtypeStruct(shape, k) for k in [jnp.float32] + [jnp.bfloat16] * 3],
        in_specs=[SMEM] + [VMEM] * 2,
        out_specs=[VMEM] * 4,
        compiler_params=PARAMS,
        name=name,
    )(place, near, far)


PIECE = 96


def ring_sum_kernel(ry1, rx1, ry3, rx3, ry2, rx2, py0, px0, out):
    wide = py0[...] + ry1[...].astype(jnp.float32) + ry2[...].astype(jnp.float32) + ry3[...].astype(jnp.float32)
    tall = px0[...] + rx1[...].astype(jnp.float32) + rx2[...].astype(jnp.float32) + rx3[...].astype(jnp.float32)
    wide = wide.astype(jnp.bfloat16)
    tall = tall.astype(jnp.bfloat16)
    for z in range(4):
        for low in range(2):
            first = (z * 2 + low) * PIECE
            if z < 2:
                out[first : first + 64, :] = wide[low * 64 : low * 64 + 64, z * FLOW : z * FLOW + B]
            else:
                for g in range(4):
                    from_row = low * 256 + g * 64
                    out[first : first + 64, g * 128 : (g + 1) * 128] = tall[
                        from_row : from_row + 64, (z - 2) * 128 : (z - 1) * 128
                    ]
            for h in range(2):
                for flow in range(2):
                    k = low * 64 + h * 32
                    at = h * 256 + flow * 128
                    out[first + 64 : first + PIECE, at : at + 128] = wide[
                        k : k + 32, flow * FLOW + B : (flow + 1) * FLOW
                    ]


def ring_sum(parts):
    return pl.pallas_call(
        ring_sum_kernel,
        out_shape=jax.ShapeDtypeStruct((8 * PIECE, B), jnp.bfloat16),
        in_specs=[VMEM] * 8,
        out_specs=VMEM,
        compiler_params=PARAMS,
        name="ring_sum",
    )(*parts)


def line_sum_kernel(arrived, out):
    total = arrived[0].astype(jnp.float32)
    for i in range(1, 8):
        total = total + arrived[i].astype(jnp.float32)
    out[...] = total.astype(jnp.bfloat16)


def line_sum(arrived):
    return pl.pallas_call(
        line_sum_kernel,
        out_shape=jax.ShapeDtypeStruct((PIECE, B), jnp.bfloat16),
        in_specs=[VMEM],
        out_specs=VMEM,
        compiler_params=PARAMS,
        name="line_sum",
    )(arrived)


def choose_kernel(place, q0, q1, q2, q3, out, position, held):
    fill_positions(place, position)
    my_x, my_core, my_low = place[1], place[2], place[4]
    mine = position[(place[0] * 4 + my_x) * 2 + my_core]

    @pl.when(mine >= 4)
    def _():
        out[...] = jnp.zeros(out.shape, jnp.bfloat16)

    @pl.when(mine < 4)
    def _():
        for r, ref in enumerate((q0, q1, q2, q3)):
            held[my_x ^ r] = ref[...]
        flow = mine >> 1
        for xl in range(2):
            at_x = 2 * (mine & 1) + xl
            for flip in range(2):
                to = aligned(xl * 2 + (my_core ^ flip), 128)
                for w in range(2):
                    for h in range(2):
                        rows = pl.ds(pl.multiple_of((my_low ^ w) * 64 + h * 32, 32), 32)
                        from_row = (flip * 2 + w) * 32
                        out[rows, pl.ds(to, 128)] = held[
                            at_x, from_row : from_row + 32, pl.ds(aligned(h * 2 + flow, 128), 128)
                        ]


def choose(place, pieces):
    return pl.pallas_call(
        choose_kernel,
        out_shape=jax.ShapeDtypeStruct((128, B), jnp.bfloat16),
        in_specs=[SMEM] + [VMEM] * 4,
        out_specs=VMEM,
        scratch_shapes=[pltpu.SMEM((32,), jnp.int32), pltpu.VMEM((4, 128, B), jnp.bfloat16)],
        compiler_params=PARAMS,
        name="choose",
    )(place, *pieces)


def cast_kernel(left, right, out):
    out[:SLOTS] = left[...].astype(jnp.bfloat16)
    out[SLOTS:] = right[...].astype(jnp.bfloat16)


def cast_rows(left, right):
    return pl.pallas_call(
        cast_kernel,
        out_shape=jax.ShapeDtypeStruct((2 * SLOTS, 64, B), jnp.bfloat16),
        in_specs=[VMEM] * 2,
        out_specs=VMEM,
        compiler_params=PARAMS,
        name="cast_rows",
    )(left, right)


def whole_kernel(place, s0, s1, s2, s3, out):
    for r, piece in enumerate((s0, s1, s2, s3)):
        for w in range(2):
            rows = pl.ds(aligned((place[3] ^ r) * 2 + (place[4] ^ w), 64), 64)
            for k in range(2 * SLOTS):
                out[k, rows, :] = piece[w * 2 * SLOTS + k]


def whole(place, pieces):
    return pl.pallas_call(
        whole_kernel,
        out_shape=jax.ShapeDtypeStruct((2 * SLOTS, B, B), jnp.bfloat16),
        in_specs=[SMEM] + [VMEM] * 4,
        out_specs=VMEM,
        compiler_params=PARAMS,
        name="whole",
    )(place, *pieces)


def root_kernel(slot, place, r0, r1, r2, r3, statistics, left_rows, right_rows, *refs):
    if slot:
        first, left_first, right_first, directions, left_new, right_new, g_ref, a_ref, m_ref = refs
        directions[:64, :] = first[...]
        left_new[0] = left_first[...]
        right_new[0] = right_first[...]
    else:
        directions, left_new, right_new, g_ref, a_ref, m_ref = refs
    my_z, my_y, my_low = place[0], place[3], place[4]
    node = my_y * 2 + my_low
    first_row = aligned(node, 64)
    for r, piece in enumerate((r0, r1, r2, r3)):
        at_y = my_y ^ r
        if slot:
            g_ref[pl.ds(aligned(at_y, 128), 128), :] = piece[...]
            continue
        for w in range(2):
            at_low = my_low ^ w
            base = w * 64

            @pl.when(my_z < 2)
            def _():
                g_ref[pl.ds(pl.multiple_of(at_y * 128 + at_low * 64, 64), 64), :] = piece[base : base + 64, :]

            @pl.when(my_z >= 2)
            def _():
                for g in range(4):
                    g_ref[
                        pl.ds(pl.multiple_of(at_low * 256 + g * 64, 64), 64),
                        pl.ds(aligned(at_y, 128), 128),
                    ] = piece[base : base + 64, g * 128 : (g + 1) * 128]

    def scaled(gram, old_rows, new_rows, which):
        a_ref[which] = gram
        rows = BETA * old_rows[slot] + a_ref[which, pl.ds(first_row, 64), :] * (1.0 / B)
        if slot:
            new_rows[slot] = rows
        else:
            new_rows[...] = rows
        full = BETA * statistics[which * SLOTS + slot].astype(jnp.float32) + gram * (1.0 / B)
        norm = B * jnp.sqrt(jnp.sum(full * full, keepdims=True) * (1.0 / (B * B)) + 1e-06)
        matrix = full / norm
        a_ref[which] = matrix
        m_ref[which] = matrix.astype(jnp.bfloat16)
        return lax.rsqrt(jnp.sqrt(norm))

    g = g_ref[...]
    left_gram = lax.dot_general(g, g, (((1,), (1,)), ((), ())), preferred_element_type=jnp.float32)
    right_gram = contract_rows(g, g)
    left_scale = scaled(left_gram, left_rows, left_new, 0)
    right_scale = scaled(right_gram, right_rows, right_new, 1)
    power = a_ref[0, pl.ds(first_row, 64), :]
    column = lax.broadcasted_iota(jnp.int32, (64, B), 1)
    row = lax.broadcasted_iota(jnp.int32, (64, B), 0) + first_row
    total = jnp.where(row == column, COEF[0], 0.0) + COEF[1] * power
    for k in range(2, 7):
        power = jnp.dot(power.astype(jnp.bfloat16), m_ref[0], preferred_element_type=jnp.float32)
        total = total + COEF[k] * power
    root = (total * left_scale).astype(jnp.bfloat16)
    half = jnp.dot(root, g, preferred_element_type=jnp.float32).astype(jnp.bfloat16)
    power = half.astype(jnp.float32)
    total = COEF[0] * power
    for k in range(1, 7):
        power = jnp.dot(power.astype(jnp.bfloat16), m_ref[1], preferred_element_type=jnp.float32)
        total = total + COEF[k] * power
    directions[64 * slot : 64 * (slot + 1), :] = (total * right_scale).astype(jnp.bfloat16)


def roots(slot, place, pieces, statistics, left_rows, right_rows, *first):
    new = jax.ShapeDtypeStruct((SLOTS, 64, B) if slot else (64, B), jnp.float32)
    return pl.pallas_call(
        functools.partial(root_kernel, slot),
        out_shape=[jax.ShapeDtypeStruct((64 * (slot + 1), B), jnp.bfloat16), new, new],
        in_specs=[SMEM] + [VMEM] * (7 + len(first)),
        out_specs=[VMEM] * 3,
        scratch_shapes=[
            pltpu.VMEM((B, B), jnp.bfloat16),
            pltpu.VMEM((2, B, B), jnp.float32),
            pltpu.VMEM((2, B, B), jnp.bfloat16),
        ],
        compiler_params=PARAMS,
        name="roots",
    )(place, *pieces, statistics, left_rows, right_rows, *first)


def place_kernel(place, *refs):
    sources, out, position, sem = refs[:10], refs[10], refs[11], refs[12]
    fill_positions(place, position)
    my_z, my_x, my_core = place[0], place[1], place[2]
    for wait in (False, True):
        for flip in range(2):
            plane, near1, near3, far_low, far_high = sources[flip * 5 : flip * 5 + 5]
            for r in range(4):
                for a in range(4):
                    source, row = (plane, near1, (far_low, far_high)[a // 2], near3)[r], a * 128
                    if r == 2:
                        row = (a % 2) * 128
                    block = position[((my_z ^ a) * 4 + (my_x ^ r)) * 2 + (my_core ^ flip)]
                    for slot in range(SLOTS):
                        copy = pltpu.make_async_copy(
                            source.at[pl.ds(row + slot * 64, 64), :],
                            out.at[:, pl.ds(aligned(jnp.minimum(block + slot * 32, 35), B), B)],
                            sem,
                        )
                        act = copy.wait if wait else copy.start
                        if slot == 0:
                            act()
                        else:
                            pl.when(block < 4)(act)


def put_blocks(place, sources, blocks):
    return pl.pallas_call(
        place_kernel,
        out_shape=jax.ShapeDtypeStruct((64, blocks * B), jnp.bfloat16),
        in_specs=[SMEM] + [ANY] * 10,
        out_specs=ANY,
        scratch_shapes=[pltpu.SMEM((32,), jnp.int32), pltpu.SemaphoreType.DMA],
        compiler_params=PARAMS,
        name="put_blocks",
    )(place, *sources)


def shards(x_band, d_gate_up, owner, stat_left, stat_right):
    place = jnp.concatenate([jnp.stack([lax.axis_index(a) for a in FINE]).astype(jnp.int32), owner])
    bucket = d_gate_up.shape[1] // B

    x1, x3 = packed(pack_x_kernel, "pack_x", [X_MSG] * 2, place, d_gate_up, x_band)
    x1, x3 = swap(x1, "x", 1), swap(x3, "x", 3)
    y1, y3 = packed(pack_y_kernel, "pack_y", [Y_MSG] * 2, place, d_gate_up, x_band)
    y1, y3 = swap(y1, "y", 1), swap(y3, "y", 3)
    (own,) = packed(pack_own_kernel, "pack_own", [OWN_MSG], place, d_gate_up)
    statistics = cast_rows(stat_left[0], stat_right[0])
    statistics = jnp.concatenate([statistics, swap(statistics, "z_lo", 1)])
    f0, f1 = swap(x1[:, X_FWD], "x", 3), swap(x3[:, X_FWD], "x", 1)
    y1_on, y3_on, statistics = lax.optimization_barrier((y1[:, Y_FWD], y3[:, Y_FWD], statistics))
    f2, f3 = swap(y1_on, "y", 3), swap(y3_on, "y", 1)
    on_x, on_y = (own, x_band, x1, x3, f0, f1), (own, x_band, y1, y3, f2, f3)
    far_wide = swap(partials(1, FLOW, 0, on_x), "core", 1)
    far_tall = swap(partials(1, B, 4 * FLOW, on_y), "core", 1)
    wide, tall = partials(0, FLOW, 0, on_x), partials(0, B, 4 * FLOW, on_y)
    py0, py1, py2, py3 = chip_sum(wide_sum_kernel, "wide_sum", (128, 2 * FLOW), place, wide, far_wide)
    px0, px1, px2, px3 = chip_sum(tall_sum_kernel, "tall_sum", (B, 256), place, tall, far_tall)
    ry1, rx1 = swap(py1, "y", 1), swap(px1, "x", 1)
    ry3, rx3 = swap(py3, "y", 3), swap(px3, "x", 3)
    ry2, rx2 = swap(py2, "y", 2), swap(px2, "x", 2)
    message = ring_sum((ry1, rx1, ry3, rx3, ry2, rx2, py0, px0))

    message, statistics = lax.optimization_barrier((message, statistics))
    s2, s1, s3 = swap(statistics, "y", 2), swap(statistics, "y", 1), swap(statistics, "y", 3)
    message = lax.all_to_all(message, ("z_hi", "z_lo"), 0, 0, tiled=True)
    line = line_sum(message.reshape(8, PIECE, B))

    main, extra = line[:64], line[64:]
    far = swap(line, "z_lo", 1)
    extra_core = swap(extra, "core", 1)
    diagonal = [(c * 2 + w, 3 - (c * 2 + w)) for c in range(2) for w in range(2)]
    extra_far = lax.ppermute(extra, ("core", "z_lo"), diagonal)
    m0 = jnp.concatenate([main, far[:64]])
    m0, s1, s2, s3 = lax.optimization_barrier((m0, s1, s2, s3))
    statistics = whole(place, (statistics, s1, s2, s3))
    m2, m1, m3 = swap(m0, "y", 2), swap(m0, "y", 1), swap(m0, "y", 3)
    q0 = jnp.concatenate([extra, far[64:], extra_core, extra_far])
    q2, q1, q3 = swap(q0, "x", 2), swap(q0, "x", 1), swap(q0, "x", 3)
    first, left_first, right_first = roots(0, place, (m0, m1, m2, m3), statistics, stat_left[0], stat_right[0])
    e0 = choose(place, (q0, q1, q2, q3))
    e2, e1, e3 = swap(e0, "y", 2), swap(e0, "y", 1), swap(e0, "y", 3)
    directions, left_new, right_new = roots(
        1, place, (e0, e1, e2, e3), statistics, stat_left[0], stat_right[0], first, left_first, right_first
    )
    a2, a1, a3 = swap(directions, "z_hi", 2), swap(directions, "z_hi", 1), swap(directions, "z_hi", 3)
    plane = jnp.concatenate([directions, a1, a2, a3])
    b1, b3 = swap(plane, "x", 1), swap(plane, "x", 3)
    near = (plane, b1, b3, swap(b1[:256], "x", 3), swap(b3[256:], "x", 1))
    out = put_blocks(place, near + tuple(swap(v, "core", 1) for v in near), bucket)
    return (out, left_new[None], right_new[None])


def solution(mesh):
    fine = Mesh(np.asarray(mesh.devices).reshape(FINE_SIZES), FINE)
    dp, node = FINE[:3], FINE[3:]
    placed = (P(dp + node, None), P(dp + node, None), P(), P(dp, None, node, None), P(dp, None, node, None))
    return jax.shard_map(
        shards,
        mesh=fine,
        in_specs=placed,
        out_specs=(P(node, None), P(dp, None, node, None), P(dp, None, node, None)),
        check_vma=False,
    )
```

```python
import functools
import math

import jax
import jax.numpy as jnp
import numpy as np
from jax import lax
from jax.experimental import pallas as pl
from jax.experimental.pallas import tpu as pltpu
from jax.sharding import Mesh, PartitionSpec as P

B = 512
SLOTS = 2
BETA = 0.9
EXTRA_CHUNK = 128
FLOW = B + EXTRA_CHUNK
HALF = B // 2

FINE = ("z_hi", "x", "core", "y", "z_lo")
FINE_SIZES = (4, 4, 2, 4, 2)
VMEM_LIMIT = 24 * 1024 * 1024

COEF = [6.25 / 4, -(1.25 + 1.25**5) / 4] + [
    -math.comb(5, k) * 1.25 ** (5 - k) * (-0.25) ** k / 4 for k in range(1, 6)
]

ANY = pl.BlockSpec(memory_space=pl.ANY)
HBM = pl.BlockSpec(memory_space=pltpu.HBM)
SMEM = pl.BlockSpec(memory_space=pltpu.SMEM)
VMEM = pl.BlockSpec(memory_space=pltpu.VMEM)
PARAMS = pltpu.CompilerParams(vmem_limit_bytes=VMEM_LIMIT)


def swap(value, axis, mask):
    size = FINE_SIZES[FINE.index(axis)]
    return lax.ppermute(value, axis, [(i, i ^ mask) for i in range(size)])


def aligned(index, step):
    return pl.multiple_of(index * step, step)


def fill_positions(place, position):
    for block in range(32):
        position[place[len(FINE) + block]] = block


X_DIRECT = 4 * FLOW
X_MSG = 6 * FLOW + B
Y_DIRECT = 4 * B
Y_MSG = 6 * B + B
OWN_MSG = 4 * FLOW + 4 * B
X_FWD = slice(X_DIRECT, 6 * FLOW + HALF)
Y_FWD = slice(Y_DIRECT, 6 * B + HALF)


class Packer:
    def __init__(self, place, d, position, sem):
        fill_positions(place, position)
        self.position, self.place, self.d, self.sem = position, place, d, sem
        self.cores = (place[2], 1 - place[2])
        self.copies = []

    def copy(self, source, first, width, target, at):
        self.copies.append(
            pltpu.make_async_copy(source.at[:, pl.ds(first, width)], target.at[:, pl.ds(at, width)], self.sem)
        )
        self.copies[-1].start()

    def flow_x(self, flow, r, core, target, at):
        to_x = self.place[1] ^ r
        block = self.position[(flow * 4 + to_x) * 2 + core]
        self.copy(self.d, aligned(block, B), B, target, at)
        chunk = 32 * B // EXTRA_CHUNK + flow * 8 + to_x * 2 + core
        self.copy(self.d, aligned(chunk, EXTRA_CHUNK), EXTRA_CHUNK, target, at + B)

    def flow_y(self, flow, r, core, target, at):
        to_y = self.place[3] ^ r
        for q in range(4):
            block = self.position[(flow * 4 + (self.place[1] ^ q)) * 2 + core]
            self.copy(self.d, pl.multiple_of(block * B + to_y * 128, 128), 128, target, at + q * 128)

    def finish(self):
        for c in self.copies:
            c.wait()


NEIGHBOURS = ((1, 0), (3, 1))


def pack_x_kernel(place, d, xb, x1, x3, position, sem):
    packer = Packer(place, d, position, sem)
    for (near, through), out in zip(NEIGHBOURS, (x1, x3)):
        for i, core in enumerate(packer.cores):
            packer.flow_x(0, near, core, out, i * 2 * FLOW)
            packer.flow_x(1, near, core, out, i * 2 * FLOW + FLOW)
            packer.flow_x(through, 2, core, out, X_DIRECT + i * FLOW)
        for i, h in enumerate((through, 1 - through)):
            packer.copy(xb, h * HALF, HALF, out, 6 * FLOW + i * HALF)
    packer.finish()


def pack_y_kernel(place, d, xb, y1, y3, position, sem):
    packer = Packer(place, d, position, sem)
    for (near, through), out in zip(NEIGHBOURS, (y1, y3)):
        for i, core in enumerate(packer.cores):
            packer.flow_y(2, near, core, out, i * 2 * B)
            packer.flow_y(3, near, core, out, i * 2 * B + B)
            packer.flow_y(2 + through, 2, core, out, Y_DIRECT + i * B)
        for i, h in enumerate((through, 1 - through)):
            packer.copy(xb, h * HALF, HALF, out, 6 * B + i * HALF)
    packer.finish()


def pack_own_kernel(place, d, out, position, sem):
    packer = Packer(place, d, position, sem)
    for i, core in enumerate(packer.cores):
        for flow in range(2):
            packer.flow_x(flow, 0, core, out, (i * 2 + flow) * FLOW)
            packer.flow_y(2 + flow, 0, core, out, 4 * FLOW + (i * 2 + flow) * B)
    packer.finish()


PACK_PARAMS = pltpu.CompilerParams(vmem_limit_bytes=50 * 1024 * 1024)


def packed(kernel, name, widths, place, d, *more):
    rows = d.shape[0]
    return pl.pallas_call(
        kernel,
        out_shape=[jax.ShapeDtypeStruct((rows, w), jnp.bfloat16) for w in widths],
        in_specs=[SMEM, HBM] + [ANY] * len(more),
        out_specs=[VMEM] * len(widths),
        scratch_shapes=[pltpu.SMEM((32,), jnp.int32), pltpu.SemaphoreType.DMA],
        compiler_params=PACK_PARAMS,
        name=name,
    )(place, d, *more)


def contract_rows(a, b):
    return lax.dot_general(a, b, (((0,), (0,)), ((), ())), preferred_element_type=jnp.float32)


def partial_kernel(which, width, own_at, own, xb, near1, near3, far1, far3, out, xs, ds):
    t = own.shape[0]
    keep = 2 * width
    at = which * keep
    rows = pl.ds(0, t)
    xs[rows, :] = xb[...]
    ds[rows, :] = own[:, own_at + at : own_at + at + keep]
    for i, ref in enumerate((near1, near3)):
        rows = pl.ds((1 + i) * t, t)
        ds[rows, :] = ref[:, at : at + keep]
        for k, h in enumerate((i, 1 - i)):
            xs[rows, h * HALF : (h + 1) * HALF] = ref[:, 6 * width + k * HALF : 6 * width + (k + 1) * HALF]
    rows = pl.ds(3 * t, t)
    for i, ref in enumerate((far1, far3)):
        ds[rows, i * width : (i + 1) * width] = ref[:, which * width : (which + 1) * width]
        xs[rows, i * HALF : (i + 1) * HALF] = ref[:, 2 * width :]
    out[...] = contract_rows(xs[...], ds[...]).astype(out.dtype)


def partials(which, width, own_at, pieces):
    t = pieces[0].shape[0]
    return pl.pallas_call(
        functools.partial(partial_kernel, which, width, own_at),
        out_shape=jax.ShapeDtypeStruct((B, 2 * width), jnp.bfloat16),
        in_specs=[VMEM] * len(pieces),
        out_specs=VMEM,
        scratch_shapes=[pltpu.VMEM((4 * t, B), jnp.bfloat16), pltpu.VMEM((4 * t, 2 * width), jnp.bfloat16)],
        compiler_params=PARAMS,
        name="partials",
    )(*pieces)


def wide_sum_kernel(place, near, far, *outs):
    for s, ref in enumerate(outs):
        rows = pl.ds(aligned(place[3] ^ s, 128), 128)
        ref[...] = (near[rows, :].astype(jnp.float32) + far[rows, :].astype(jnp.float32)).astype(ref.dtype)


def tall_sum_kernel(place, near, far, *outs):
    for q, ref in enumerate(outs):
        for flow in range(2):
            at = slice(flow * B + q * 128, flow * B + (q + 1) * 128)
            ref[:, flow * 128 : (flow + 1) * 128] = (
                near[:, at].astype(jnp.float32) + far[:, at].astype(jnp.float32)
            ).astype(ref.dtype)


def chip_sum(kernel, name, shape, place, near, far):
    return pl.pallas_call(
        kernel,
        out_shape=[jax.ShapeDtypeStruct(shape, k) for k in [jnp.float32] + [jnp.bfloat16] * 3],
        in_specs=[SMEM] + [VMEM] * 2,
        out_specs=[VMEM] * 4,
        compiler_params=PARAMS,
        name=name,
    )(place, near, far)


PIECE = 96


def ring_sum_kernel(ry1, rx1, ry3, rx3, ry2, rx2, py0, px0, out):
    wide = py0[...] + ry1[...].astype(jnp.float32) + ry2[...].astype(jnp.float32) + ry3[...].astype(jnp.float32)
    tall = px0[...] + rx1[...].astype(jnp.float32) + rx2[...].astype(jnp.float32) + rx3[...].astype(jnp.float32)
    wide = wide.astype(jnp.bfloat16)
    tall = tall.astype(jnp.bfloat16)
    for z in range(4):
        for low in range(2):
            first = (z * 2 + low) * PIECE
            if z < 2:
                out[first : first + 64, :] = wide[low * 64 : low * 64 + 64, z * FLOW : z * FLOW + B]
            else:
                for g in range(4):
                    from_row = low * 256 + g * 64
                    out[first : first + 64, g * 128 : (g + 1) * 128] = tall[
                        from_row : from_row + 64, (z - 2) * 128 : (z - 1) * 128
                    ]
            for h in range(2):
                for flow in range(2):
                    k = low * 64 + h * 32
                    at = h * 256 + flow * 128
                    out[first + 64 : first + PIECE, at : at + 128] = wide[
                        k : k + 32, flow * FLOW + B : (flow + 1) * FLOW
                    ]


def ring_sum(parts):
    return pl.pallas_call(
        ring_sum_kernel,
        out_shape=jax.ShapeDtypeStruct((8 * PIECE, B), jnp.bfloat16),
        in_specs=[VMEM] * 8,
        out_specs=VMEM,
        compiler_params=PARAMS,
        name="ring_sum",
    )(*parts)


def line_sum_kernel(arrived, out):
    total = arrived[0].astype(jnp.float32)
    for i in range(1, 8):
        total = total + arrived[i].astype(jnp.float32)
    out[...] = total.astype(jnp.bfloat16)


def line_sum(arrived):
    return pl.pallas_call(
        line_sum_kernel,
        out_shape=jax.ShapeDtypeStruct((PIECE, B), jnp.bfloat16),
        in_specs=[VMEM],
        out_specs=VMEM,
        compiler_params=PARAMS,
        name="line_sum",
    )(arrived)


def choose_kernel(place, q0, q1, q2, q3, out, position, held):
    fill_positions(place, position)
    my_x, my_core, my_low = place[1], place[2], place[4]
    mine = position[(place[0] * 4 + my_x) * 2 + my_core]

    @pl.when(mine >= 4)
    def _():
        out[...] = jnp.zeros(out.shape, jnp.bfloat16)

    @pl.when(mine < 4)
    def _():
        for r, ref in enumerate((q0, q1, q2, q3)):
            held[my_x ^ r] = ref[...]
        flow = mine >> 1
        for xl in range(2):
            at_x = 2 * (mine & 1) + xl
            for flip in range(2):
                to = aligned(xl * 2 + (my_core ^ flip), 128)
                for w in range(2):
                    for h in range(2):
                        rows = pl.ds(pl.multiple_of((my_low ^ w) * 64 + h * 32, 32), 32)
                        from_row = (flip * 2 + w) * 32
                        out[rows, pl.ds(to, 128)] = held[
                            at_x, from_row : from_row + 32, pl.ds(aligned(h * 2 + flow, 128), 128)
                        ]


def choose(place, pieces):
    return pl.pallas_call(
        choose_kernel,
        out_shape=jax.ShapeDtypeStruct((128, B), jnp.bfloat16),
        in_specs=[SMEM] + [VMEM] * 4,
        out_specs=VMEM,
        scratch_shapes=[pltpu.SMEM((32,), jnp.int32), pltpu.VMEM((4, 128, B), jnp.bfloat16)],
        compiler_params=PARAMS,
        name="choose",
    )(place, *pieces)


def cast_kernel(left, right, out):
    out[:SLOTS] = left[...].astype(jnp.bfloat16)
    out[SLOTS:] = right[...].astype(jnp.bfloat16)


def cast_rows(left, right):
    return pl.pallas_call(
        cast_kernel,
        out_shape=jax.ShapeDtypeStruct((2 * SLOTS, 64, B), jnp.bfloat16),
        in_specs=[VMEM] * 2,
        out_specs=VMEM,
        compiler_params=PARAMS,
        name="cast_rows",
    )(left, right)


def whole_kernel(place, s0, s1, s2, s3, out):
    for r, piece in enumerate((s0, s1, s2, s3)):
        for w in range(2):
            rows = pl.ds(aligned((place[3] ^ r) * 2 + (place[4] ^ w), 64), 64)
            for k in range(2 * SLOTS):
                out[k, rows, :] = piece[w * 2 * SLOTS + k]


def whole(place, pieces):
    return pl.pallas_call(
        whole_kernel,
        out_shape=jax.ShapeDtypeStruct((2 * SLOTS, B, B), jnp.bfloat16),
        in_specs=[SMEM] + [VMEM] * 4,
        out_specs=VMEM,
        compiler_params=PARAMS,
        name="whole",
    )(place, *pieces)


def root_kernel(slot, place, r0, r1, r2, r3, statistics, left_rows, right_rows, *refs):
    if slot:
        left_first, right_first, directions, left_new, right_new, g_ref, a_ref, m_ref = refs
        left_new[0] = left_first[...]
        right_new[0] = right_first[...]
    else:
        directions, left_new, right_new, g_ref, a_ref, m_ref = refs
    my_z, my_y, my_low = place[0], place[3], place[4]
    node = my_y * 2 + my_low
    first_row = aligned(node, 64)
    for r, piece in enumerate((r0, r1, r2, r3)):
        at_y = my_y ^ r
        if slot:
            g_ref[pl.ds(aligned(at_y, 128), 128), :] = piece[...]
            continue
        for w in range(2):
            at_low = my_low ^ w
            base = w * 64

            @pl.when(my_z < 2)
            def _():
                g_ref[pl.ds(pl.multiple_of(at_y * 128 + at_low * 64, 64), 64), :] = piece[base : base + 64, :]

            @pl.when(my_z >= 2)
            def _():
                for g in range(4):
                    g_ref[
                        pl.ds(pl.multiple_of(at_low * 256 + g * 64, 64), 64),
                        pl.ds(aligned(at_y, 128), 128),
                    ] = piece[base : base + 64, g * 128 : (g + 1) * 128]

    def scaled(gram, old_rows, new_rows, which):
        a_ref[which] = gram
        rows = BETA * old_rows[slot] + a_ref[which, pl.ds(first_row, 64), :] * (1.0 / B)
        if slot:
            new_rows[slot] = rows
        else:
            new_rows[...] = rows
        full = BETA * statistics[which * SLOTS + slot].astype(jnp.float32) + gram * (1.0 / B)
        norm = B * jnp.sqrt(jnp.sum(full * full, keepdims=True) * (1.0 / (B * B)) + 1e-06)
        matrix = full / norm
        a_ref[which] = matrix
        m_ref[which] = matrix.astype(jnp.bfloat16)
        return lax.rsqrt(jnp.sqrt(norm))

    g = g_ref[...]
    left_gram = lax.dot_general(g, g, (((1,), (1,)), ((), ())), preferred_element_type=jnp.float32)
    right_gram = contract_rows(g, g)
    left_scale = scaled(left_gram, left_rows, left_new, 0)
    right_scale = scaled(right_gram, right_rows, right_new, 1)
    power = a_ref[0, pl.ds(first_row, 64), :]
    column = lax.broadcasted_iota(jnp.int32, (64, B), 1)
    row = lax.broadcasted_iota(jnp.int32, (64, B), 0) + first_row
    total = jnp.where(row == column, COEF[0], 0.0) + COEF[1] * power
    for k in range(2, 7):
        power = jnp.dot(power.astype(jnp.bfloat16), m_ref[0], preferred_element_type=jnp.float32)
        total = total + COEF[k] * power
    root = (total * left_scale).astype(jnp.bfloat16)
    half = jnp.dot(root, g, preferred_element_type=jnp.float32).astype(jnp.bfloat16)
    power = half.astype(jnp.float32)
    total = COEF[0] * power
    for k in range(1, 7):
        power = jnp.dot(power.astype(jnp.bfloat16), m_ref[1], preferred_element_type=jnp.float32)
        total = total + COEF[k] * power
    directions[...] = (total * right_scale).astype(jnp.bfloat16)


def roots(slot, place, pieces, statistics, left_rows, right_rows, *first):
    new = jax.ShapeDtypeStruct((SLOTS, 64, B) if slot else (64, B), jnp.float32)
    return pl.pallas_call(
        functools.partial(root_kernel, slot),
        out_shape=[jax.ShapeDtypeStruct((64, B), jnp.bfloat16), new, new],
        in_specs=[SMEM] + [VMEM] * (7 + len(first)),
        out_specs=[VMEM] * 3,
        scratch_shapes=[
            pltpu.VMEM((B, B), jnp.bfloat16),
            pltpu.VMEM((2, B, B), jnp.float32),
            pltpu.VMEM((2, B, B), jnp.bfloat16),
        ],
        compiler_params=PARAMS,
        name="roots",
    )(place, *pieces, statistics, left_rows, right_rows, *first)


def place_kernel(place, *refs):
    sources, out, position, sem = refs[:10], refs[10], refs[11], refs[12]
    fill_positions(place, position)
    my_z, my_x, my_core = place[0], place[1], place[2]

    def find(slot, r, a, held, near1, near3, low, high):
        if r == 0:
            return held, slot * 3 * 4 + a
        if slot == 0 and r == 2:
            return (near3, 4 + a) if a < 2 else (near1, 2 + a)
        if slot == 0:
            return held, (1 if r == 1 else 2) * 4 + a
        if r == 2:
            return (low, a) if a < 2 else (high, a - 2)
        return (near1 if r == 1 else near3), a

    for wait in (False, True):
        for slot in range(SLOTS):
            for flip in range(2):
                for r in range(4):
                    for a in range(4):
                        source, row = find(slot, r, a, *sources[flip * 5 : flip * 5 + 5])
                        block = position[((my_z ^ a) * 4 + (my_x ^ r)) * 2 + (my_core ^ flip)]
                        copy = pltpu.make_async_copy(
                            source.at[pl.ds(row * 64, 64), :],
                            out.at[:, pl.ds(aligned(jnp.minimum(block + slot * 32, 35), B), B)],
                            sem,
                        )
                        act = copy.wait if wait else copy.start
                        if slot == 0:
                            act()
                        else:
                            pl.when(block < 4)(act)


def put_blocks(place, sources, blocks):
    return pl.pallas_call(
        place_kernel,
        out_shape=jax.ShapeDtypeStruct((64, blocks * B), jnp.bfloat16),
        in_specs=[SMEM] + [ANY] * 10,
        out_specs=ANY,
        scratch_shapes=[pltpu.SMEM((32,), jnp.int32), pltpu.SemaphoreType.DMA],
        compiler_params=PARAMS,
        name="put_blocks",
    )(place, *sources)


def around_z(rows):
    a2, a1, a3 = swap(rows, "z_hi", 2), swap(rows, "z_hi", 1), swap(rows, "z_hi", 3)
    return jnp.concatenate([rows, a1, a2, a3])


def shards(x_band, d_gate_up, owner, stat_left, stat_right):
    place = jnp.concatenate([jnp.stack([lax.axis_index(a) for a in FINE]).astype(jnp.int32), owner])
    bucket = d_gate_up.shape[1] // B

    x1, x3 = packed(pack_x_kernel, "pack_x", [X_MSG] * 2, place, d_gate_up, x_band)
    x1, x3 = swap(x1, "x", 1), swap(x3, "x", 3)
    y1, y3 = packed(pack_y_kernel, "pack_y", [Y_MSG] * 2, place, d_gate_up, x_band)
    y1, y3 = swap(y1, "y", 1), swap(y3, "y", 3)
    (own,) = packed(pack_own_kernel, "pack_own", [OWN_MSG], place, d_gate_up)
    statistics = cast_rows(stat_left[0], stat_right[0])
    statistics = jnp.concatenate([statistics, swap(statistics, "z_lo", 1)])
    f0, f1 = swap(x1[:, X_FWD], "x", 3), swap(x3[:, X_FWD], "x", 1)
    y1_on, y3_on, statistics = lax.optimization_barrier((y1[:, Y_FWD], y3[:, Y_FWD], statistics))
    f2, f3 = swap(y1_on, "y", 3), swap(y3_on, "y", 1)
    on_x, on_y = (own, x_band, x1, x3, f0, f1), (own, x_band, y1, y3, f2, f3)
    far_wide = swap(partials(1, FLOW, 0, on_x), "core", 1)
    far_tall = swap(partials(1, B, 4 * FLOW, on_y), "core", 1)
    wide, tall = partials(0, FLOW, 0, on_x), partials(0, B, 4 * FLOW, on_y)
    py0, py1, py2, py3 = chip_sum(wide_sum_kernel, "wide_sum", (128, 2 * FLOW), place, wide, far_wide)
    px0, px1, px2, px3 = chip_sum(tall_sum_kernel, "tall_sum", (B, 256), place, tall, far_tall)
    ry1, rx1 = swap(py1, "y", 1), swap(px1, "x", 1)
    ry3, rx3 = swap(py3, "y", 3), swap(px3, "x", 3)
    ry2, rx2 = swap(py2, "y", 2), swap(px2, "x", 2)
    message = ring_sum((ry1, rx1, ry3, rx3, ry2, rx2, py0, px0))

    message, statistics = lax.optimization_barrier((message, statistics))
    s2, s1, s3 = swap(statistics, "y", 2), swap(statistics, "y", 1), swap(statistics, "y", 3)
    message = lax.all_to_all(message, ("z_hi", "z_lo"), 0, 0, tiled=True)
    line = line_sum(message.reshape(8, PIECE, B))

    main, extra = line[:64], line[64:]
    far = swap(line, "z_lo", 1)
    extra_core = swap(extra, "core", 1)
    diagonal = [(c * 2 + w, 3 - (c * 2 + w)) for c in range(2) for w in range(2)]
    extra_far = lax.ppermute(extra, ("core", "z_lo"), diagonal)
    far, s1, s2, s3 = lax.optimization_barrier((far, s1, s2, s3))
    statistics = whole(place, (statistics, s1, s2, s3))
    m0 = jnp.concatenate([main, far[:64]])
    m2, m1, m3 = swap(m0, "y", 2), swap(m0, "y", 1), swap(m0, "y", 3)
    q0 = jnp.concatenate([extra, far[64:], extra_core, extra_far])
    q2, q1, q3 = swap(q0, "x", 2), swap(q0, "x", 1), swap(q0, "x", 3)
    first, left_first, right_first = roots(0, place, (m0, m1, m2, m3), statistics, stat_left[0], stat_right[0])
    e0 = choose(place, (q0, q1, q2, q3))
    e2, e1, e3 = swap(e0, "y", 2), swap(e0, "y", 1), swap(e0, "y", 3)
    plane, e1, e2, e3 = lax.optimization_barrier((around_z(first), e1, e2, e3))
    second, left_new, right_new = roots(
        1, place, (e0, e1, e2, e3), statistics, stat_left[0], stat_right[0], left_first, right_first
    )
    _, second = lax.optimization_barrier((plane, second))
    first1, first3 = swap(plane, "x", 1), swap(plane, "x", 3)
    second = around_z(second)
    near1 = swap(jnp.concatenate([second, first3[128:]]), "x", 1)
    near3 = swap(jnp.concatenate([second, first1[:128]]), "x", 3)
    held = jnp.concatenate([plane, first1, first3, second])
    sources = (held, near1, near3, swap(near1[:128], "x", 3), swap(near3[128:256], "x", 1))
    out = put_blocks(place, sources + tuple(swap(v, "core", 1) for v in sources), bucket)
    return (out, left_new[None], right_new[None])


def solution(mesh):
    fine = Mesh(np.asarray(mesh.devices).reshape(FINE_SIZES), FINE)
    dp, node = FINE[:3], FINE[3:]
    placed = (P(dp + node, None), P(dp + node, None), P(), P(dp, None, node, None), P(dp, None, node, None))
    return jax.shard_map(
        shards,
        mesh=fine,
        in_specs=placed,
        out_specs=(P(node, None), P(dp, None, node, None), P(dp, None, node, None)),
        check_vma=False,
    )
```

```python
import functools
import math

import jax
import jax.numpy as jnp
import numpy as np
from jax import lax
from jax.experimental import pallas as pl
from jax.experimental.pallas import tpu as pltpu
from jax.sharding import Mesh, PartitionSpec as P

B = 512
SLOTS = 2
BETA = 0.9
EXTRA_CHUNK = 128
FLOW = B + EXTRA_CHUNK
HALF = B // 2

FINE = ("z_hi", "x", "core", "y", "z_lo")
FINE_SIZES = (4, 4, 2, 4, 2)
VMEM_LIMIT = 24 * 1024 * 1024

COEF = [6.25 / 4, -(1.25 + 1.25**5) / 4] + [
    -math.comb(5, k) * 1.25 ** (5 - k) * (-0.25) ** k / 4 for k in range(1, 6)
]

ANY = pl.BlockSpec(memory_space=pl.ANY)
HBM = pl.BlockSpec(memory_space=pltpu.HBM)
SMEM = pl.BlockSpec(memory_space=pltpu.SMEM)
VMEM = pl.BlockSpec(memory_space=pltpu.VMEM)
PARAMS = pltpu.CompilerParams(vmem_limit_bytes=VMEM_LIMIT)


def swap(value, axis, mask):
    size = FINE_SIZES[FINE.index(axis)]
    return lax.ppermute(value, axis, [(i, i ^ mask) for i in range(size)])


def aligned(index, step):
    return pl.multiple_of(index * step, step)


def fill_positions(place, position):
    for block in range(32):
        position[place[len(FINE) + block]] = block


X_DIRECT = 4 * FLOW
X_MSG = 6 * FLOW + B
Y_DIRECT = 4 * B
Y_MSG = 6 * B + B
OWN_MSG = 4 * FLOW + 4 * B
X_FWD = slice(X_DIRECT, 6 * FLOW + HALF)
Y_FWD = slice(Y_DIRECT, 6 * B + HALF)


class Packer:
    def __init__(self, place, d, position, sem):
        fill_positions(place, position)
        self.position, self.place, self.d, self.sem = position, place, d, sem
        self.cores = (place[2], 1 - place[2])
        self.copies = []

    def copy(self, source, first, width, target, at):
        self.copies.append(
            pltpu.make_async_copy(source.at[:, pl.ds(first, width)], target.at[:, pl.ds(at, width)], self.sem)
        )
        self.copies[-1].start()

    def flow_x(self, flow, r, core, target, at):
        to_x = self.place[1] ^ r
        block = self.position[(flow * 4 + to_x) * 2 + core]
        self.copy(self.d, aligned(block, B), B, target, at)
        chunk = 32 * B // EXTRA_CHUNK + flow * 8 + to_x * 2 + core
        self.copy(self.d, aligned(chunk, EXTRA_CHUNK), EXTRA_CHUNK, target, at + B)

    def flow_y(self, flow, r, core, target, at):
        to_y = self.place[3] ^ r
        for q in range(4):
            block = self.position[(flow * 4 + (self.place[1] ^ q)) * 2 + core]
            self.copy(self.d, pl.multiple_of(block * B + to_y * 128, 128), 128, target, at + q * 128)

    def finish(self):
        for c in self.copies:
            c.wait()


NEIGHBOURS = ((1, 0), (3, 1))


def pack_x_kernel(place, d, xb, x1, x3, position, sem):
    packer = Packer(place, d, position, sem)
    for (near, through), out in zip(NEIGHBOURS, (x1, x3)):
        for i, core in enumerate(packer.cores):
            packer.flow_x(0, near, core, out, i * 2 * FLOW)
            packer.flow_x(1, near, core, out, i * 2 * FLOW + FLOW)
            packer.flow_x(through, 2, core, out, X_DIRECT + i * FLOW)
        for i, h in enumerate((through, 1 - through)):
            packer.copy(xb, h * HALF, HALF, out, 6 * FLOW + i * HALF)
    packer.finish()


def pack_y_kernel(place, d, xb, y1, y3, position, sem):
    packer = Packer(place, d, position, sem)
    for (near, through), out in zip(NEIGHBOURS, (y1, y3)):
        for i, core in enumerate(packer.cores):
            packer.flow_y(2, near, core, out, i * 2 * B)
            packer.flow_y(3, near, core, out, i * 2 * B + B)
            packer.flow_y(2 + through, 2, core, out, Y_DIRECT + i * B)
        for i, h in enumerate((through, 1 - through)):
            packer.copy(xb, h * HALF, HALF, out, 6 * B + i * HALF)
    packer.finish()


def pack_own_kernel(place, d, out, position, sem):
    packer = Packer(place, d, position, sem)
    for i, core in enumerate(packer.cores):
        for flow in range(2):
            packer.flow_x(flow, 0, core, out, (i * 2 + flow) * FLOW)
            packer.flow_y(2 + flow, 0, core, out, 4 * FLOW + (i * 2 + flow) * B)
    packer.finish()


PACK_PARAMS = pltpu.CompilerParams(vmem_limit_bytes=50 * 1024 * 1024)


def packed(kernel, name, widths, place, d, *more):
    rows = d.shape[0]
    return pl.pallas_call(
        kernel,
        out_shape=[jax.ShapeDtypeStruct((rows, w), jnp.bfloat16) for w in widths],
        in_specs=[SMEM, HBM] + [ANY] * len(more),
        out_specs=[VMEM] * len(widths),
        scratch_shapes=[pltpu.SMEM((32,), jnp.int32), pltpu.SemaphoreType.DMA],
        compiler_params=PACK_PARAMS,
        name=name,
    )(place, d, *more)


def contract_rows(a, b):
    return lax.dot_general(a, b, (((0,), (0,)), ((), ())), preferred_element_type=jnp.float32)


def partial_kernel(which, width, own_at, own, xb, near1, near3, far1, far3, out, xs, ds):
    t = own.shape[0]
    keep = 2 * width
    at = which * keep
    rows = pl.ds(0, t)
    xs[rows, :] = xb[...]
    ds[rows, :] = own[:, own_at + at : own_at + at + keep]
    for i, ref in enumerate((near1, near3)):
        rows = pl.ds((1 + i) * t, t)
        ds[rows, :] = ref[:, at : at + keep]
        for k, h in enumerate((i, 1 - i)):
            xs[rows, h * HALF : (h + 1) * HALF] = ref[:, 6 * width + k * HALF : 6 * width + (k + 1) * HALF]
    rows = pl.ds(3 * t, t)
    for i, ref in enumerate((far1, far3)):
        ds[rows, i * width : (i + 1) * width] = ref[:, which * width : (which + 1) * width]
        xs[rows, i * HALF : (i + 1) * HALF] = ref[:, 2 * width :]
    out[...] = contract_rows(xs[...], ds[...]).astype(out.dtype)


def partials(which, width, own_at, pieces):
    t = pieces[0].shape[0]
    return pl.pallas_call(
        functools.partial(partial_kernel, which, width, own_at),
        out_shape=jax.ShapeDtypeStruct((B, 2 * width), jnp.bfloat16),
        in_specs=[VMEM] * len(pieces),
        out_specs=VMEM,
        scratch_shapes=[pltpu.VMEM((4 * t, B), jnp.bfloat16), pltpu.VMEM((4 * t, 2 * width), jnp.bfloat16)],
        compiler_params=PARAMS,
        name="partials",
    )(*pieces)


def wide_sum_kernel(place, near, far, *outs):
    for s, ref in enumerate(outs):
        rows = pl.ds(aligned(place[3] ^ s, 128), 128)
        ref[...] = (near[rows, :].astype(jnp.float32) + far[rows, :].astype(jnp.float32)).astype(ref.dtype)


def tall_sum_kernel(place, near, far, *outs):
    for q, ref in enumerate(outs):
        for flow in range(2):
            at = slice(flow * B + q * 128, flow * B + (q + 1) * 128)
            ref[:, flow * 128 : (flow + 1) * 128] = (
                near[:, at].astype(jnp.float32) + far[:, at].astype(jnp.float32)
            ).astype(ref.dtype)


def chip_sum(kernel, name, shape, place, near, far):
    return pl.pallas_call(
        kernel,
        out_shape=[jax.ShapeDtypeStruct(shape, k) for k in [jnp.float32] + [jnp.bfloat16] * 3],
        in_specs=[SMEM] + [VMEM] * 2,
        out_specs=[VMEM] * 4,
        compiler_params=PARAMS,
        name=name,
    )(place, near, far)


PIECE = 96


def ring_sum_kernel(ry1, rx1, ry3, rx3, ry2, rx2, py0, px0, out):
    wide = py0[...] + ry1[...].astype(jnp.float32) + ry2[...].astype(jnp.float32) + ry3[...].astype(jnp.float32)
    tall = px0[...] + rx1[...].astype(jnp.float32) + rx2[...].astype(jnp.float32) + rx3[...].astype(jnp.float32)
    wide = wide.astype(jnp.bfloat16)
    tall = tall.astype(jnp.bfloat16)
    for z in range(4):
        for low in range(2):
            first = (z * 2 + low) * PIECE
            if z < 2:
                out[first : first + 64, :] = wide[low * 64 : low * 64 + 64, z * FLOW : z * FLOW + B]
            else:
                for g in range(4):
                    from_row = low * 256 + g * 64
                    out[first : first + 64, g * 128 : (g + 1) * 128] = tall[
                        from_row : from_row + 64, (z - 2) * 128 : (z - 1) * 128
                    ]
            for h in range(2):
                for flow in range(2):
                    k = low * 64 + h * 32
                    at = h * 256 + flow * 128
                    out[first + 64 : first + PIECE, at : at + 128] = wide[
                        k : k + 32, flow * FLOW + B : (flow + 1) * FLOW
                    ]


def ring_sum(parts):
    return pl.pallas_call(
        ring_sum_kernel,
        out_shape=jax.ShapeDtypeStruct((8 * PIECE, B), jnp.bfloat16),
        in_specs=[VMEM] * 8,
        out_specs=VMEM,
        compiler_params=PARAMS,
        name="ring_sum",
    )(*parts)


def line_sum_kernel(arrived, out):
    total = arrived[0].astype(jnp.float32)
    for i in range(1, 8):
        total = total + arrived[i].astype(jnp.float32)
    out[...] = total.astype(jnp.bfloat16)


def line_sum(arrived):
    return pl.pallas_call(
        line_sum_kernel,
        out_shape=jax.ShapeDtypeStruct((PIECE, B), jnp.bfloat16),
        in_specs=[VMEM],
        out_specs=VMEM,
        compiler_params=PARAMS,
        name="line_sum",
    )(arrived)


def choose_kernel(place, q0, q1, q2, q3, out, position, held):
    fill_positions(place, position)
    my_x, my_core, my_low = place[1], place[2], place[4]
    mine = position[(place[0] * 4 + my_x) * 2 + my_core]

    @pl.when(mine >= 4)
    def _():
        out[...] = jnp.zeros(out.shape, jnp.bfloat16)

    @pl.when(mine < 4)
    def _():
        for r, ref in enumerate((q0, q1, q2, q3)):
            held[my_x ^ r] = ref[...]
        flow = mine >> 1
        for xl in range(2):
            at_x = 2 * (mine & 1) + xl
            for flip in range(2):
                to = aligned(xl * 2 + (my_core ^ flip), 128)
                for w in range(2):
                    for h in range(2):
                        rows = pl.ds(pl.multiple_of((my_low ^ w) * 64 + h * 32, 32), 32)
                        from_row = (flip * 2 + w) * 32
                        out[rows, pl.ds(to, 128)] = held[
                            at_x, from_row : from_row + 32, pl.ds(aligned(h * 2 + flow, 128), 128)
                        ]


def choose(place, pieces):
    return pl.pallas_call(
        choose_kernel,
        out_shape=jax.ShapeDtypeStruct((128, B), jnp.bfloat16),
        in_specs=[SMEM] + [VMEM] * 4,
        out_specs=VMEM,
        scratch_shapes=[pltpu.SMEM((32,), jnp.int32), pltpu.VMEM((4, 128, B), jnp.bfloat16)],
        compiler_params=PARAMS,
        name="choose",
    )(place, *pieces)


def cast_kernel(left, right, out):
    out[:SLOTS] = left[...].astype(jnp.bfloat16)
    out[SLOTS:] = right[...].astype(jnp.bfloat16)


def cast_rows(left, right):
    return pl.pallas_call(
        cast_kernel,
        out_shape=jax.ShapeDtypeStruct((2 * SLOTS, 64, B), jnp.bfloat16),
        in_specs=[VMEM] * 2,
        out_specs=VMEM,
        compiler_params=PARAMS,
        name="cast_rows",
    )(left, right)


def whole_kernel(place, s0, s1, s2, s3, out):
    for r, piece in enumerate((s0, s1, s2, s3)):
        for w in range(2):
            rows = pl.ds(aligned((place[3] ^ r) * 2 + (place[4] ^ w), 64), 64)
            for k in range(2 * SLOTS):
                out[k, rows, :] = piece[w * 2 * SLOTS + k]


def whole(place, pieces):
    return pl.pallas_call(
        whole_kernel,
        out_shape=jax.ShapeDtypeStruct((2 * SLOTS, B, B), jnp.bfloat16),
        in_specs=[SMEM] + [VMEM] * 4,
        out_specs=VMEM,
        compiler_params=PARAMS,
        name="whole",
    )(place, *pieces)


def root_kernel(slot, place, r0, r1, r2, r3, statistics, left_rows, right_rows, *refs):
    if slot:
        left_first, right_first, directions, left_new, right_new, g_ref, a_ref, m_ref = refs
        left_new[0] = left_first[...]
        right_new[0] = right_first[...]
    else:
        directions, left_new, right_new, g_ref, a_ref, m_ref = refs
    my_z, my_y, my_low = place[0], place[3], place[4]
    node = my_y * 2 + my_low
    first_row = aligned(node, 64)
    for r, piece in enumerate((r0, r1, r2, r3)):
        at_y = my_y ^ r
        if slot:
            g_ref[pl.ds(aligned(at_y, 128), 128), :] = piece[...]
            continue
        for w in range(2):
            at_low = my_low ^ w
            base = w * 64

            @pl.when(my_z < 2)
            def _():
                g_ref[pl.ds(pl.multiple_of(at_y * 128 + at_low * 64, 64), 64), :] = piece[base : base + 64, :]

            @pl.when(my_z >= 2)
            def _():
                for g in range(4):
                    g_ref[
                        pl.ds(pl.multiple_of(at_low * 256 + g * 64, 64), 64),
                        pl.ds(aligned(at_y, 128), 128),
                    ] = piece[base : base + 64, g * 128 : (g + 1) * 128]

    def scaled(gram, old_rows, new_rows, which):
        a_ref[which] = gram
        rows = BETA * old_rows[slot] + a_ref[which, pl.ds(first_row, 64), :] * (1.0 / B)
        if slot:
            new_rows[slot] = rows
        else:
            new_rows[...] = rows
        full = BETA * statistics[which * SLOTS + slot].astype(jnp.float32) + gram * (1.0 / B)
        norm = B * jnp.sqrt(jnp.sum(full * full, keepdims=True) * (1.0 / (B * B)) + 1e-06)
        matrix = full / norm
        a_ref[which] = matrix
        m_ref[which] = matrix.astype(jnp.bfloat16)
        return lax.rsqrt(jnp.sqrt(norm))

    g = g_ref[...]
    left_gram = lax.dot_general(g, g, (((1,), (1,)), ((), ())), preferred_element_type=jnp.float32)
    right_gram = contract_rows(g, g)
    left_scale = scaled(left_gram, left_rows, left_new, 0)
    right_scale = scaled(right_gram, right_rows, right_new, 1)
    power = a_ref[0, pl.ds(first_row, 64), :]
    column = lax.broadcasted_iota(jnp.int32, (64, B), 1)
    row = lax.broadcasted_iota(jnp.int32, (64, B), 0) + first_row
    total = jnp.where(row == column, COEF[0], 0.0) + COEF[1] * power
    for k in range(2, 7):
        power = jnp.dot(power.astype(jnp.bfloat16), m_ref[0], preferred_element_type=jnp.float32)
        total = total + COEF[k] * power
    root = (total * left_scale).astype(jnp.bfloat16)
    half = jnp.dot(root, g, preferred_element_type=jnp.float32).astype(jnp.bfloat16)
    power = half.astype(jnp.float32)
    total = COEF[0] * power
    for k in range(1, 7):
        power = jnp.dot(power.astype(jnp.bfloat16), m_ref[1], preferred_element_type=jnp.float32)
        total = total + COEF[k] * power
    directions[...] = (total * right_scale).astype(jnp.bfloat16)


def roots(slot, place, pieces, statistics, left_rows, right_rows, *first):
    new = jax.ShapeDtypeStruct((SLOTS, 64, B) if slot else (64, B), jnp.float32)
    return pl.pallas_call(
        functools.partial(root_kernel, slot),
        out_shape=[jax.ShapeDtypeStruct((64, B), jnp.bfloat16), new, new],
        in_specs=[SMEM] + [VMEM] * (7 + len(first)),
        out_specs=[VMEM] * 3,
        scratch_shapes=[
            pltpu.VMEM((B, B), jnp.bfloat16),
            pltpu.VMEM((2, B, B), jnp.float32),
            pltpu.VMEM((2, B, B), jnp.bfloat16),
        ],
        compiler_params=PARAMS,
        name="roots",
    )(place, *pieces, statistics, left_rows, right_rows, *first)


def place_kernel(place, *refs):
    sources, out, position, sem = refs[:8], refs[8], refs[9], refs[10]
    fill_positions(place, position)
    my_z, my_x, my_core = place[0], place[1], place[2]

    def find(slot, r, a, held, near1, near3, far):
        if r == 0:
            return held, slot * 3 * 4 + a
        if slot == 0 and r == 2:
            return (near3, 4 + a) if a < 2 else (near1, 2 + a)
        if slot == 0:
            return held, (1 if r == 1 else 2) * 4 + a
        if r == 2:
            return far, a
        return (near1 if r == 1 else near3), a

    for wait in (False, True):
        for slot in range(SLOTS):
            for flip in range(2):
                for r in range(4):
                    for a in range(4):
                        source, row = find(slot, r, a, *sources[flip * 4 : flip * 4 + 4])
                        block = position[((my_z ^ a) * 4 + (my_x ^ r)) * 2 + (my_core ^ flip)]
                        copy = pltpu.make_async_copy(
                            source.at[pl.ds(row * 64, 64), :],
                            out.at[:, pl.ds(aligned(jnp.minimum(block + slot * 32, 35), B), B)],
                            sem,
                        )
                        act = copy.wait if wait else copy.start
                        if slot == 0:
                            act()
                        else:
                            pl.when(block < 4)(act)


def put_blocks(place, sources, blocks):
    return pl.pallas_call(
        place_kernel,
        out_shape=jax.ShapeDtypeStruct((64, blocks * B), jnp.bfloat16),
        in_specs=[SMEM] + [ANY] * 8,
        out_specs=ANY,
        scratch_shapes=[pltpu.SMEM((32,), jnp.int32), pltpu.SemaphoreType.DMA],
        compiler_params=PARAMS,
        name="put_blocks",
    )(place, *sources)


def around_z(rows):
    a2, a1, a3 = swap(rows, "z_hi", 2), swap(rows, "z_hi", 1), swap(rows, "z_hi", 3)
    return jnp.concatenate([rows, a1, a2, a3])


def shards(x_band, d_gate_up, owner, stat_left, stat_right):
    place = jnp.concatenate([jnp.stack([lax.axis_index(a) for a in FINE]).astype(jnp.int32), owner])
    bucket = d_gate_up.shape[1] // B

    x1, x3 = packed(pack_x_kernel, "pack_x", [X_MSG] * 2, place, d_gate_up, x_band)
    x1, x3 = swap(x1, "x", 1), swap(x3, "x", 3)
    y1, y3 = packed(pack_y_kernel, "pack_y", [Y_MSG] * 2, place, d_gate_up, x_band)
    y1, y3 = swap(y1, "y", 1), swap(y3, "y", 3)
    (own,) = packed(pack_own_kernel, "pack_own", [OWN_MSG], place, d_gate_up)
    statistics = cast_rows(stat_left[0], stat_right[0])
    statistics = jnp.concatenate([statistics, swap(statistics, "z_lo", 1)])
    f0, f1 = swap(x1[:, X_FWD], "x", 3), swap(x3[:, X_FWD], "x", 1)
    y1_on, y3_on, statistics = lax.optimization_barrier((y1[:, Y_FWD], y3[:, Y_FWD], statistics))
    f2, f3 = swap(y1_on, "y", 3), swap(y3_on, "y", 1)
    on_x, on_y = (own, x_band, x1, x3, f0, f1), (own, x_band, y1, y3, f2, f3)
    far_wide = swap(partials(1, FLOW, 0, on_x), "core", 1)
    far_tall = swap(partials(1, B, 4 * FLOW, on_y), "core", 1)
    wide, tall = partials(0, FLOW, 0, on_x), partials(0, B, 4 * FLOW, on_y)
    py0, py1, py2, py3 = chip_sum(wide_sum_kernel, "wide_sum", (128, 2 * FLOW), place, wide, far_wide)
    px0, px1, px2, px3 = chip_sum(tall_sum_kernel, "tall_sum", (B, 256), place, tall, far_tall)
    ry1, rx1 = swap(py1, "y", 1), swap(px1, "x", 1)
    ry3, rx3 = swap(py3, "y", 3), swap(px3, "x", 3)
    ry2, rx2 = swap(py2, "y", 2), swap(px2, "x", 2)
    message = ring_sum((ry1, rx1, ry3, rx3, ry2, rx2, py0, px0))

    message, statistics = lax.optimization_barrier((message, statistics))
    s2, s1, s3 = swap(statistics, "y", 2), swap(statistics, "y", 1), swap(statistics, "y", 3)
    message = lax.all_to_all(message, ("z_hi", "z_lo"), 0, 0, tiled=True)
    line = line_sum(message.reshape(8, PIECE, B))

    main, extra = line[:64], line[64:]
    far = swap(line, "z_lo", 1)
    extra_core = swap(extra, "core", 1)
    diagonal = [(c * 2 + w, 3 - (c * 2 + w)) for c in range(2) for w in range(2)]
    extra_far = lax.ppermute(extra, ("core", "z_lo"), diagonal)
    m0 = jnp.concatenate([main, far[:64]])
    m0, s1, s2, s3 = lax.optimization_barrier((m0, s1, s2, s3))
    statistics = whole(place, (statistics, s1, s2, s3))
    m2, m1, m3 = swap(m0, "y", 2), swap(m0, "y", 1), swap(m0, "y", 3)
    q0 = jnp.concatenate([extra, far[64:], extra_core, extra_far])
    q2, q1, q3 = swap(q0, "x", 2), swap(q0, "x", 1), swap(q0, "x", 3)
    first, left_first, right_first = roots(0, place, (m0, m1, m2, m3), statistics, stat_left[0], stat_right[0])
    e0 = choose(place, (q0, q1, q2, q3))
    e2, e1, e3 = swap(e0, "y", 2), swap(e0, "y", 1), swap(e0, "y", 3)
    first, e1, e2, e3 = lax.optimization_barrier((first, e1, e2, e3))
    plane = around_z(first)
    second, left_new, right_new = roots(
        1, place, (e0, e1, e2, e3), statistics, stat_left[0], stat_right[0], left_first, right_first
    )
    plane, second = lax.optimization_barrier((plane, second))
    first1, first3 = swap(plane, "x", 1), swap(plane, "x", 3)
    second = around_z(second)
    far = swap(second, "x", 2)
    near1 = swap(jnp.concatenate([second, first3[128:]]), "x", 1)
    near3 = swap(jnp.concatenate([second, first1[:128]]), "x", 3)
    held = jnp.concatenate([plane, first1, first3, second])
    sources = (held, near1, near3, far)
    out = put_blocks(place, sources + tuple(swap(v, "core", 1) for v in sources), bucket)
    return (out, left_new[None], right_new[None])


def solution(mesh):
    fine = Mesh(np.asarray(mesh.devices).reshape(FINE_SIZES), FINE)
    dp, node = FINE[:3], FINE[3:]
    placed = (P(dp + node, None), P(dp + node, None), P(), P(dp, None, node, None), P(dp, None, node, None))
    return jax.shard_map(
        shards,
        mesh=fine,
        in_specs=placed,
        out_specs=(P(node, None), P(dp, None, node, None), P(dp, None, node, None)),
        check_vma=False,
    )
```

```python
import functools
import math

import jax
import jax.numpy as jnp
import numpy as np
from jax import lax
from jax.experimental import pallas as pl
from jax.experimental.pallas import tpu as pltpu
from jax.sharding import Mesh, PartitionSpec as P

B = 512
SLOTS = 2
BETA = 0.9
EXTRA_CHUNK = 128
FLOW = B + EXTRA_CHUNK
HALF = B // 2

FINE = ("z_hi", "x", "core", "y", "z_lo")
FINE_SIZES = (4, 4, 2, 4, 2)
VMEM_LIMIT = 24 * 1024 * 1024

COEF = [6.25 / 4, -(1.25 + 1.25**5) / 4] + [
    -math.comb(5, k) * 1.25 ** (5 - k) * (-0.25) ** k / 4 for k in range(1, 6)
]

ANY = pl.BlockSpec(memory_space=pl.ANY)
HBM = pl.BlockSpec(memory_space=pltpu.HBM)
SMEM = pl.BlockSpec(memory_space=pltpu.SMEM)
VMEM = pl.BlockSpec(memory_space=pltpu.VMEM)
PARAMS = pltpu.CompilerParams(vmem_limit_bytes=VMEM_LIMIT)


def swap(value, axis, mask):
    size = FINE_SIZES[FINE.index(axis)]
    return lax.ppermute(value, axis, [(i, i ^ mask) for i in range(size)])


def aligned(index, step):
    return pl.multiple_of(index * step, step)


def fill_positions(place, position):
    for block in range(32):
        position[place[len(FINE) + block]] = block


X_DIRECT = 4 * FLOW
X_MSG = 6 * FLOW + B
Y_DIRECT = 4 * B
Y_MSG = 6 * B + B
OWN_MSG = 4 * FLOW + 4 * B
X_FWD = slice(X_DIRECT, 6 * FLOW + HALF)
Y_FWD = slice(Y_DIRECT, 6 * B + HALF)


class Packer:
    def __init__(self, place, d, position, sem):
        fill_positions(place, position)
        self.position, self.place, self.d, self.sem = position, place, d, sem
        self.cores = (place[2], 1 - place[2])
        self.copies = []

    def copy(self, source, first, width, target, at):
        self.copies.append(
            pltpu.make_async_copy(source.at[:, pl.ds(first, width)], target.at[:, pl.ds(at, width)], self.sem)
        )
        self.copies[-1].start()

    def flow_x(self, flow, r, core, target, at):
        to_x = self.place[1] ^ r
        block = self.position[(flow * 4 + to_x) * 2 + core]
        self.copy(self.d, aligned(block, B), B, target, at)
        chunk = 32 * B // EXTRA_CHUNK + flow * 8 + to_x * 2 + core
        self.copy(self.d, aligned(chunk, EXTRA_CHUNK), EXTRA_CHUNK, target, at + B)

    def flow_y(self, flow, r, core, target, at):
        to_y = self.place[3] ^ r
        for q in range(4):
            block = self.position[(flow * 4 + (self.place[1] ^ q)) * 2 + core]
            self.copy(self.d, pl.multiple_of(block * B + to_y * 128, 128), 128, target, at + q * 128)

    def finish(self):
        for c in self.copies:
            c.wait()


NEIGHBOURS = ((1, 0), (3, 1))


def pack_x_kernel(place, d, xb, x1, x3, position, sem):
    packer = Packer(place, d, position, sem)
    for (near, through), out in zip(NEIGHBOURS, (x1, x3)):
        for i, core in enumerate(packer.cores):
            packer.flow_x(0, near, core, out, i * 2 * FLOW)
            packer.flow_x(1, near, core, out, i * 2 * FLOW + FLOW)
            packer.flow_x(through, 2, core, out, X_DIRECT + i * FLOW)
        for i, h in enumerate((through, 1 - through)):
            packer.copy(xb, h * HALF, HALF, out, 6 * FLOW + i * HALF)
    packer.finish()


def pack_y_kernel(place, d, xb, y1, y3, position, sem):
    packer = Packer(place, d, position, sem)
    for (near, through), out in zip(NEIGHBOURS, (y1, y3)):
        for i, core in enumerate(packer.cores):
            packer.flow_y(2, near, core, out, i * 2 * B)
            packer.flow_y(3, near, core, out, i * 2 * B + B)
            packer.flow_y(2 + through, 2, core, out, Y_DIRECT + i * B)
        for i, h in enumerate((through, 1 - through)):
            packer.copy(xb, h * HALF, HALF, out, 6 * B + i * HALF)
    packer.finish()


def pack_own_kernel(place, d, out, position, sem):
    packer = Packer(place, d, position, sem)
    for i, core in enumerate(packer.cores):
        for flow in range(2):
            packer.flow_x(flow, 0, core, out, (i * 2 + flow) * FLOW)
            packer.flow_y(2 + flow, 0, core, out, 4 * FLOW + (i * 2 + flow) * B)
    packer.finish()


PACK_PARAMS = pltpu.CompilerParams(vmem_limit_bytes=50 * 1024 * 1024)


def packed(kernel, name, widths, place, d, *more):
    rows = d.shape[0]
    return pl.pallas_call(
        kernel,
        out_shape=[jax.ShapeDtypeStruct((rows, w), jnp.bfloat16) for w in widths],
        in_specs=[SMEM, HBM] + [ANY] * len(more),
        out_specs=[VMEM] * len(widths),
        scratch_shapes=[pltpu.SMEM((32,), jnp.int32), pltpu.SemaphoreType.DMA],
        compiler_params=PACK_PARAMS,
        name=name,
    )(place, d, *more)


def contract_rows(a, b):
    return lax.dot_general(a, b, (((0,), (0,)), ((), ())), preferred_element_type=jnp.float32)


def partial_kernel(which, width, own_at, own, xb, near1, near3, far1, far3, out, xs, ds):
    t = own.shape[0]
    keep = 2 * width
    at = which * keep
    rows = pl.ds(0, t)
    xs[rows, :] = xb[...]
    ds[rows, :] = own[:, own_at + at : own_at + at + keep]
    for i, ref in enumerate((near1, near3)):
        rows = pl.ds((1 + i) * t, t)
        ds[rows, :] = ref[:, at : at + keep]
        for k, h in enumerate((i, 1 - i)):
            xs[rows, h * HALF : (h + 1) * HALF] = ref[:, 6 * width + k * HALF : 6 * width + (k + 1) * HALF]
    rows = pl.ds(3 * t, t)
    for i, ref in enumerate((far1, far3)):
        ds[rows, i * width : (i + 1) * width] = ref[:, which * width : (which + 1) * width]
        xs[rows, i * HALF : (i + 1) * HALF] = ref[:, 2 * width :]
    out[...] = contract_rows(xs[...], ds[...]).astype(out.dtype)


def partials(which, width, own_at, pieces):
    t = pieces[0].shape[0]
    return pl.pallas_call(
        functools.partial(partial_kernel, which, width, own_at),
        out_shape=jax.ShapeDtypeStruct((B, 2 * width), jnp.bfloat16),
        in_specs=[VMEM] * len(pieces),
        out_specs=VMEM,
        scratch_shapes=[pltpu.VMEM((4 * t, B), jnp.bfloat16), pltpu.VMEM((4 * t, 2 * width), jnp.bfloat16)],
        compiler_params=PARAMS,
        name="partials",
    )(*pieces)


def wide_sum_kernel(place, near, far, *outs):
    for s, ref in enumerate(outs):
        rows = pl.ds(aligned(place[3] ^ s, 128), 128)
        ref[...] = (near[rows, :].astype(jnp.float32) + far[rows, :].astype(jnp.float32)).astype(ref.dtype)


def tall_sum_kernel(place, near, far, *outs):
    for q, ref in enumerate(outs):
        for flow in range(2):
            at = slice(flow * B + q * 128, flow * B + (q + 1) * 128)
            ref[:, flow * 128 : (flow + 1) * 128] = (
                near[:, at].astype(jnp.float32) + far[:, at].astype(jnp.float32)
            ).astype(ref.dtype)


def chip_sum(kernel, name, shape, place, near, far):
    return pl.pallas_call(
        kernel,
        out_shape=[jax.ShapeDtypeStruct(shape, k) for k in [jnp.float32] + [jnp.bfloat16] * 3],
        in_specs=[SMEM] + [VMEM] * 2,
        out_specs=[VMEM] * 4,
        compiler_params=PARAMS,
        name=name,
    )(place, near, far)


PIECE = 96


def ring_sum_kernel(ry1, rx1, ry3, rx3, ry2, rx2, py0, px0, out):
    wide = py0[...] + ry1[...].astype(jnp.float32) + ry2[...].astype(jnp.float32) + ry3[...].astype(jnp.float32)
    tall = px0[...] + rx1[...].astype(jnp.float32) + rx2[...].astype(jnp.float32) + rx3[...].astype(jnp.float32)
    wide = wide.astype(jnp.bfloat16)
    tall = tall.astype(jnp.bfloat16)
    for z in range(4):
        for low in range(2):
            first = (z * 2 + low) * PIECE
            if z < 2:
                out[first : first + 64, :] = wide[low * 64 : low * 64 + 64, z * FLOW : z * FLOW + B]
            else:
                for g in range(4):
                    from_row = low * 256 + g * 64
                    out[first : first + 64, g * 128 : (g + 1) * 128] = tall[
                        from_row : from_row + 64, (z - 2) * 128 : (z - 1) * 128
                    ]
            for h in range(2):
                for flow in range(2):
                    k = low * 64 + h * 32
                    at = h * 256 + flow * 128
                    out[first + 64 : first + PIECE, at : at + 128] = wide[
                        k : k + 32, flow * FLOW + B : (flow + 1) * FLOW
                    ]


def ring_sum(parts):
    return pl.pallas_call(
        ring_sum_kernel,
        out_shape=jax.ShapeDtypeStruct((8 * PIECE, B), jnp.bfloat16),
        in_specs=[VMEM] * 8,
        out_specs=VMEM,
        compiler_params=PARAMS,
        name="ring_sum",
    )(*parts)


def line_sum_kernel(arrived, out):
    total = arrived[0].astype(jnp.float32)
    for i in range(1, 8):
        total = total + arrived[i].astype(jnp.float32)
    out[...] = total.astype(jnp.bfloat16)


def line_sum(arrived):
    return pl.pallas_call(
        line_sum_kernel,
        out_shape=jax.ShapeDtypeStruct((PIECE, B), jnp.bfloat16),
        in_specs=[VMEM],
        out_specs=VMEM,
        compiler_params=PARAMS,
        name="line_sum",
    )(arrived)


def choose_kernel(place, q0, q1, q2, q3, out, position, held):
    fill_positions(place, position)
    my_x, my_core, my_low = place[1], place[2], place[4]
    mine = position[(place[0] * 4 + my_x) * 2 + my_core]

    @pl.when(mine >= 4)
    def _():
        out[...] = jnp.zeros(out.shape, jnp.bfloat16)

    @pl.when(mine < 4)
    def _():
        for r, ref in enumerate((q0, q1, q2, q3)):
            held[my_x ^ r] = ref[...]
        flow = mine >> 1
        for xl in range(2):
            at_x = 2 * (mine & 1) + xl
            for flip in range(2):
                to = aligned(xl * 2 + (my_core ^ flip), 128)
                for w in range(2):
                    for h in range(2):
                        rows = pl.ds(pl.multiple_of((my_low ^ w) * 64 + h * 32, 32), 32)
                        from_row = (flip * 2 + w) * 32
                        out[rows, pl.ds(to, 128)] = held[
                            at_x, from_row : from_row + 32, pl.ds(aligned(h * 2 + flow, 128), 128)
                        ]


def choose(place, pieces):
    return pl.pallas_call(
        choose_kernel,
        out_shape=jax.ShapeDtypeStruct((128, B), jnp.bfloat16),
        in_specs=[SMEM] + [VMEM] * 4,
        out_specs=VMEM,
        scratch_shapes=[pltpu.SMEM((32,), jnp.int32), pltpu.VMEM((4, 128, B), jnp.bfloat16)],
        compiler_params=PARAMS,
        name="choose",
    )(place, *pieces)


def cast_kernel(left, right, out):
    out[:SLOTS] = left[...].astype(jnp.bfloat16)
    out[SLOTS:] = right[...].astype(jnp.bfloat16)


def cast_rows(left, right):
    return pl.pallas_call(
        cast_kernel,
        out_shape=jax.ShapeDtypeStruct((2 * SLOTS, 64, B), jnp.bfloat16),
        in_specs=[VMEM] * 2,
        out_specs=VMEM,
        compiler_params=PARAMS,
        name="cast_rows",
    )(left, right)


def whole_kernel(place, s0, s1, s2, s3, out):
    for r, piece in enumerate((s0, s1, s2, s3)):
        for w in range(2):
            rows = pl.ds(aligned((place[3] ^ r) * 2 + (place[4] ^ w), 64), 64)
            for k in range(2 * SLOTS):
                out[k, rows, :] = piece[w * 2 * SLOTS + k]


def whole(place, pieces):
    return pl.pallas_call(
        whole_kernel,
        out_shape=jax.ShapeDtypeStruct((2 * SLOTS, B, B), jnp.bfloat16),
        in_specs=[SMEM] + [VMEM] * 4,
        out_specs=VMEM,
        compiler_params=PARAMS,
        name="whole",
    )(place, *pieces)


def root_kernel(slot, place, r0, r1, r2, r3, statistics, left_rows, right_rows, *refs):
    if slot:
        left_first, right_first, directions, left_new, right_new, g_ref, a_ref, m_ref = refs
        left_new[0] = left_first[...]
        right_new[0] = right_first[...]
    else:
        directions, left_new, right_new, g_ref, a_ref, m_ref = refs
    my_z, my_y, my_low = place[0], place[3], place[4]
    node = my_y * 2 + my_low
    first_row = aligned(node, 64)
    for r, piece in enumerate((r0, r1, r2, r3)):
        at_y = my_y ^ r
        if slot:
            g_ref[pl.ds(aligned(at_y, 128), 128), :] = piece[...]
            continue
        for w in range(2):
            at_low = my_low ^ w
            base = w * 64

            @pl.when(my_z < 2)
            def _():
                g_ref[pl.ds(pl.multiple_of(at_y * 128 + at_low * 64, 64), 64), :] = piece[base : base + 64, :]

            @pl.when(my_z >= 2)
            def _():
                for g in range(4):
                    g_ref[
                        pl.ds(pl.multiple_of(at_low * 256 + g * 64, 64), 64),
                        pl.ds(aligned(at_y, 128), 128),
                    ] = piece[base : base + 64, g * 128 : (g + 1) * 128]

    def scaled(gram, old_rows, new_rows, which):
        a_ref[which] = gram
        rows = BETA * old_rows[slot] + a_ref[which, pl.ds(first_row, 64), :] * (1.0 / B)
        if slot:
            new_rows[slot] = rows
        else:
            new_rows[...] = rows
        full = BETA * statistics[which * SLOTS + slot].astype(jnp.float32) + gram * (1.0 / B)
        norm = B * jnp.sqrt(jnp.sum(full * full, keepdims=True) * (1.0 / (B * B)) + 1e-06)
        matrix = full / norm
        a_ref[which] = matrix
        m_ref[which] = matrix.astype(jnp.bfloat16)
        return lax.rsqrt(jnp.sqrt(norm))

    g = g_ref[...]
    left_gram = lax.dot_general(g, g, (((1,), (1,)), ((), ())), preferred_element_type=jnp.float32)
    right_gram = contract_rows(g, g)
    left_scale = scaled(left_gram, left_rows, left_new, 0)
    right_scale = scaled(right_gram, right_rows, right_new, 1)
    power = a_ref[0, pl.ds(first_row, 64), :]
    column = lax.broadcasted_iota(jnp.int32, (64, B), 1)
    row = lax.broadcasted_iota(jnp.int32, (64, B), 0) + first_row
    total = jnp.where(row == column, COEF[0], 0.0) + COEF[1] * power
    for k in range(2, 7):
        power = jnp.dot(power.astype(jnp.bfloat16), m_ref[0], preferred_element_type=jnp.float32)
        total = total + COEF[k] * power
    root = (total * left_scale).astype(jnp.bfloat16)
    half = jnp.dot(root, g, preferred_element_type=jnp.float32).astype(jnp.bfloat16)
    power = half.astype(jnp.float32)
    total = COEF[0] * power
    for k in range(1, 7):
        power = jnp.dot(power.astype(jnp.bfloat16), m_ref[1], preferred_element_type=jnp.float32)
        total = total + COEF[k] * power
    directions[...] = (total * right_scale).astype(jnp.bfloat16)


def roots(slot, place, pieces, statistics, left_rows, right_rows, *first):
    new = jax.ShapeDtypeStruct((SLOTS, 64, B) if slot else (64, B), jnp.float32)
    return pl.pallas_call(
        functools.partial(root_kernel, slot),
        out_shape=[jax.ShapeDtypeStruct((64, B), jnp.bfloat16), new, new],
        in_specs=[SMEM] + [VMEM] * (7 + len(first)),
        out_specs=[VMEM] * 3,
        scratch_shapes=[
            pltpu.VMEM((B, B), jnp.bfloat16),
            pltpu.VMEM((2, B, B), jnp.float32),
            pltpu.VMEM((2, B, B), jnp.bfloat16),
        ],
        compiler_params=PARAMS,
        name="roots",
    )(place, *pieces, statistics, left_rows, right_rows, *first)


def place_kernel(place, *refs):
    sources, out, position, sem = refs[:16], refs[16], refs[17], refs[18]
    fill_positions(place, position)
    my_z, my_x, my_core = place[0], place[1], place[2]

    for wait in (False, True):
        for slot in range(SLOTS):
            for flip in range(2):
                for r in range(4):
                    for a in range(4):
                        source = sources[((1 - slot) * 2 + flip) * 4 + r]
                        block = position[((my_z ^ a) * 4 + (my_x ^ r)) * 2 + (my_core ^ flip)]
                        copy = pltpu.make_async_copy(
                            source.at[pl.ds(a * 64, 64), :],
                            out.at[:, pl.ds(aligned(jnp.minimum(block + slot * 32, 35), B), B)],
                            sem,
                        )
                        act = copy.wait if wait else copy.start
                        if slot == 0:
                            act()
                        else:
                            pl.when(block < 4)(act)


def put_blocks(place, sources, blocks):
    return pl.pallas_call(
        place_kernel,
        out_shape=jax.ShapeDtypeStruct((64, blocks * B), jnp.bfloat16),
        in_specs=[SMEM] + [ANY] * 16,
        out_specs=ANY,
        scratch_shapes=[pltpu.SMEM((32,), jnp.int32), pltpu.SemaphoreType.DMA],
        compiler_params=PARAMS,
        name="put_blocks",
    )(place, *sources)


def around_z(rows):
    a2, a1, a3 = swap(rows, "z_hi", 2), swap(rows, "z_hi", 1), swap(rows, "z_hi", 3)
    return jnp.concatenate([rows, a1, a2, a3])


def around_x(plane):
    b2, b1, b3 = swap(plane, "x", 2), swap(plane, "x", 1), swap(plane, "x", 3)
    return plane, b1, b2, b3


def shards(x_band, d_gate_up, owner, stat_left, stat_right):
    place = jnp.concatenate([jnp.stack([lax.axis_index(a) for a in FINE]).astype(jnp.int32), owner])
    bucket = d_gate_up.shape[1] // B

    x1, x3 = packed(pack_x_kernel, "pack_x", [X_MSG] * 2, place, d_gate_up, x_band)
    x1, x3 = swap(x1, "x", 1), swap(x3, "x", 3)
    y1, y3 = packed(pack_y_kernel, "pack_y", [Y_MSG] * 2, place, d_gate_up, x_band)
    y1, y3 = swap(y1, "y", 1), swap(y3, "y", 3)
    (own,) = packed(pack_own_kernel, "pack_own", [OWN_MSG], place, d_gate_up)
    statistics = cast_rows(stat_left[0], stat_right[0])
    statistics = jnp.concatenate([statistics, swap(statistics, "z_lo", 1)])
    f0, f1 = swap(x1[:, X_FWD], "x", 3), swap(x3[:, X_FWD], "x", 1)
    y1_on, y3_on, statistics = lax.optimization_barrier((y1[:, Y_FWD], y3[:, Y_FWD], statistics))
    f2, f3 = swap(y1_on, "y", 3), swap(y3_on, "y", 1)
    on_x, on_y = (own, x_band, x1, x3, f0, f1), (own, x_band, y1, y3, f2, f3)
    far_wide = swap(partials(1, FLOW, 0, on_x), "core", 1)
    far_tall = swap(partials(1, B, 4 * FLOW, on_y), "core", 1)
    wide, tall = partials(0, FLOW, 0, on_x), partials(0, B, 4 * FLOW, on_y)
    py0, py1, py2, py3 = chip_sum(wide_sum_kernel, "wide_sum", (128, 2 * FLOW), place, wide, far_wide)
    px0, px1, px2, px3 = chip_sum(tall_sum_kernel, "tall_sum", (B, 256), place, tall, far_tall)
    ry1, rx1 = swap(py1, "y", 1), swap(px1, "x", 1)
    ry3, rx3 = swap(py3, "y", 3), swap(px3, "x", 3)
    ry2, rx2 = swap(py2, "y", 2), swap(px2, "x", 2)
    message = ring_sum((ry1, rx1, ry3, rx3, ry2, rx2, py0, px0))

    message, statistics = lax.optimization_barrier((message, statistics))
    s2, s1, s3 = swap(statistics, "y", 2), swap(statistics, "y", 1), swap(statistics, "y", 3)
    message = lax.all_to_all(message, ("z_hi", "z_lo"), 0, 0, tiled=True)
    line = line_sum(message.reshape(8, PIECE, B))

    main, extra = line[:64], line[64:]
    far = swap(line, "z_lo", 1)
    extra_core = swap(extra, "core", 1)
    diagonal = [(c * 2 + w, 3 - (c * 2 + w)) for c in range(2) for w in range(2)]
    extra_far = lax.ppermute(extra, ("core", "z_lo"), diagonal)
    m0 = jnp.concatenate([main, far[:64]])
    m0, s1, s2, s3 = lax.optimization_barrier((m0, s1, s2, s3))
    statistics = whole(place, (statistics, s1, s2, s3))
    m2, m1, m3 = swap(m0, "y", 2), swap(m0, "y", 1), swap(m0, "y", 3)
    q0 = jnp.concatenate([extra, far[64:], extra_core, extra_far])
    q2, q1, q3 = swap(q0, "x", 2), swap(q0, "x", 1), swap(q0, "x", 3)
    first, left_first, right_first = roots(0, place, (m0, m1, m2, m3), statistics, stat_left[0], stat_right[0])
    e0 = choose(place, (q0, q1, q2, q3))
    e2, e1, e3 = swap(e0, "y", 2), swap(e0, "y", 1), swap(e0, "y", 3)
    first, e1, e2, e3 = lax.optimization_barrier((first, e1, e2, e3))
    second, left_new, right_new = roots(
        1, place, (e0, e1, e2, e3), statistics, stat_left[0], stat_right[0], left_first, right_first
    )
    plane = around_z(first)
    _, second = lax.optimization_barrier((plane, second))
    first = around_x(plane)
    plane = around_z(second)
    first, _ = lax.optimization_barrier((first, plane))
    second = around_x(plane)
    sources = [swap(v, "core", flip) if flip else v for part in (second, first) for flip in range(2) for v in part]
    out = put_blocks(place, sources, bucket)
    return (out, left_new[None], right_new[None])


def solution(mesh):
    fine = Mesh(np.asarray(mesh.devices).reshape(FINE_SIZES), FINE)
    dp, node = FINE[:3], FINE[3:]
    placed = (P(dp + node, None), P(dp + node, None), P(), P(dp, None, node, None), P(dp, None, node, None))
    return jax.shard_map(
        shards,
        mesh=fine,
        in_specs=placed,
        out_specs=(P(node, None), P(dp, None, node, None), P(dp, None, node, None)),
        check_vma=False,
    )
```

```python
import functools
import math

import jax
import jax.numpy as jnp
import numpy as np
from jax import lax
from jax.experimental import pallas as pl
from jax.experimental.pallas import tpu as pltpu
from jax.sharding import Mesh, PartitionSpec as P

B = 512
SLOTS = 2
BETA = 0.9
EXTRA_CHUNK = 128
FLOW = B + EXTRA_CHUNK
HALF = B // 2

FINE = ("z_hi", "x", "core", "y", "z_lo")
FINE_SIZES = (4, 4, 2, 4, 2)
VMEM_LIMIT = 24 * 1024 * 1024

COEF = [6.25 / 4, -(1.25 + 1.25**5) / 4] + [
    -math.comb(5, k) * 1.25 ** (5 - k) * (-0.25) ** k / 4 for k in range(1, 6)
]

ANY = pl.BlockSpec(memory_space=pl.ANY)
HBM = pl.BlockSpec(memory_space=pltpu.HBM)
SMEM = pl.BlockSpec(memory_space=pltpu.SMEM)
VMEM = pl.BlockSpec(memory_space=pltpu.VMEM)
PARAMS = pltpu.CompilerParams(vmem_limit_bytes=VMEM_LIMIT)


def swap(value, axis, mask):
    size = FINE_SIZES[FINE.index(axis)]
    return lax.ppermute(value, axis, [(i, i ^ mask) for i in range(size)])


def aligned(index, step):
    return pl.multiple_of(index * step, step)


def fill_positions(place, position):
    for block in range(32):
        position[place[len(FINE) + block]] = block


X_DIRECT = 4 * FLOW
X_MSG = 6 * FLOW + B
Y_DIRECT = 4 * B
Y_MSG = 6 * B + B
OWN_MSG = 4 * FLOW + 4 * B
X_FWD = slice(X_DIRECT, 6 * FLOW + HALF)
Y_FWD = slice(Y_DIRECT, 6 * B + HALF)


class Packer:
    def __init__(self, place, d, position, sem):
        fill_positions(place, position)
        self.position, self.place, self.d, self.sem = position, place, d, sem
        self.cores = (place[2], 1 - place[2])
        self.copies = []

    def copy(self, source, first, width, target, at):
        self.copies.append(
            pltpu.make_async_copy(source.at[:, pl.ds(first, width)], target.at[:, pl.ds(at, width)], self.sem)
        )
        self.copies[-1].start()

    def flow_x(self, flow, r, core, target, at):
        to_x = self.place[1] ^ r
        block = self.position[(flow * 4 + to_x) * 2 + core]
        self.copy(self.d, aligned(block, B), B, target, at)
        chunk = 32 * B // EXTRA_CHUNK + flow * 8 + to_x * 2 + core
        self.copy(self.d, aligned(chunk, EXTRA_CHUNK), EXTRA_CHUNK, target, at + B)

    def flow_y(self, flow, r, core, target, at):
        to_y = self.place[3] ^ r
        for q in range(4):
            block = self.position[(flow * 4 + (self.place[1] ^ q)) * 2 + core]
            self.copy(self.d, pl.multiple_of(block * B + to_y * 128, 128), 128, target, at + q * 128)

    def finish(self):
        for c in self.copies:
            c.wait()


NEIGHBOURS = ((1, 0), (3, 1))


def pack_x_kernel(place, d, xb, x1, x3, position, sem):
    packer = Packer(place, d, position, sem)
    for (near, through), out in zip(NEIGHBOURS, (x1, x3)):
        for i, core in enumerate(packer.cores):
            packer.flow_x(0, near, core, out, i * 2 * FLOW)
            packer.flow_x(1, near, core, out, i * 2 * FLOW + FLOW)
            packer.flow_x(through, 2, core, out, X_DIRECT + i * FLOW)
        for i, h in enumerate((through, 1 - through)):
            packer.copy(xb, h * HALF, HALF, out, 6 * FLOW + i * HALF)
    packer.finish()


def pack_y_kernel(place, d, xb, y1, y3, position, sem):
    packer = Packer(place, d, position, sem)
    for (near, through), out in zip(NEIGHBOURS, (y1, y3)):
        for i, core in enumerate(packer.cores):
            packer.flow_y(2, near, core, out, i * 2 * B)
            packer.flow_y(3, near, core, out, i * 2 * B + B)
            packer.flow_y(2 + through, 2, core, out, Y_DIRECT + i * B)
        for i, h in enumerate((through, 1 - through)):
            packer.copy(xb, h * HALF, HALF, out, 6 * B + i * HALF)
    packer.finish()


def pack_own_kernel(place, d, out, position, sem):
    packer = Packer(place, d, position, sem)
    for i, core in enumerate(packer.cores):
        for flow in range(2):
            packer.flow_x(flow, 0, core, out, (i * 2 + flow) * FLOW)
            packer.flow_y(2 + flow, 0, core, out, 4 * FLOW + (i * 2 + flow) * B)
    packer.finish()


PACK_PARAMS = pltpu.CompilerParams(vmem_limit_bytes=50 * 1024 * 1024)


def packed(kernel, name, widths, place, d, *more):
    rows = d.shape[0]
    return pl.pallas_call(
        kernel,
        out_shape=[jax.ShapeDtypeStruct((rows, w), jnp.bfloat16) for w in widths],
        in_specs=[SMEM, HBM] + [ANY] * len(more),
        out_specs=[VMEM] * len(widths),
        scratch_shapes=[pltpu.SMEM((32,), jnp.int32), pltpu.SemaphoreType.DMA],
        compiler_params=PACK_PARAMS,
        name=name,
    )(place, d, *more)


def contract_rows(a, b):
    return lax.dot_general(a, b, (((0,), (0,)), ((), ())), preferred_element_type=jnp.float32)


def partial_kernel(which, width, own_at, own, xb, near1, near3, far1, far3, out, xs, ds):
    t = own.shape[0]
    keep = 2 * width
    at = which * keep
    rows = pl.ds(0, t)
    xs[rows, :] = xb[...]
    ds[rows, :] = own[:, own_at + at : own_at + at + keep]
    for i, ref in enumerate((near1, near3)):
        rows = pl.ds((1 + i) * t, t)
        ds[rows, :] = ref[:, at : at + keep]
        for k, h in enumerate((i, 1 - i)):
            xs[rows, h * HALF : (h + 1) * HALF] = ref[:, 6 * width + k * HALF : 6 * width + (k + 1) * HALF]
    rows = pl.ds(3 * t, t)
    for i, ref in enumerate((far1, far3)):
        ds[rows, i * width : (i + 1) * width] = ref[:, which * width : (which + 1) * width]
        xs[rows, i * HALF : (i + 1) * HALF] = ref[:, 2 * width :]
    out[...] = contract_rows(xs[...], ds[...]).astype(out.dtype)


def partials(which, width, own_at, pieces):
    t = pieces[0].shape[0]
    return pl.pallas_call(
        functools.partial(partial_kernel, which, width, own_at),
        out_shape=jax.ShapeDtypeStruct((B, 2 * width), jnp.bfloat16),
        in_specs=[VMEM] * len(pieces),
        out_specs=VMEM,
        scratch_shapes=[pltpu.VMEM((4 * t, B), jnp.bfloat16), pltpu.VMEM((4 * t, 2 * width), jnp.bfloat16)],
        compiler_params=PARAMS,
        name="partials",
    )(*pieces)


def wide_sum_kernel(place, near, far, *outs):
    for s, ref in enumerate(outs):
        rows = pl.ds(aligned(place[3] ^ s, 128), 128)
        ref[...] = (near[rows, :].astype(jnp.float32) + far[rows, :].astype(jnp.float32)).astype(ref.dtype)


def tall_sum_kernel(place, near, far, *outs):
    for q, ref in enumerate(outs):
        for flow in range(2):
            at = slice(flow * B + q * 128, flow * B + (q + 1) * 128)
            ref[:, flow * 128 : (flow + 1) * 128] = (
                near[:, at].astype(jnp.float32) + far[:, at].astype(jnp.float32)
            ).astype(ref.dtype)


def chip_sum(kernel, name, shape, place, near, far):
    return pl.pallas_call(
        kernel,
        out_shape=[jax.ShapeDtypeStruct(shape, k) for k in [jnp.float32] + [jnp.bfloat16] * 3],
        in_specs=[SMEM] + [VMEM] * 2,
        out_specs=[VMEM] * 4,
        compiler_params=PARAMS,
        name=name,
    )(place, near, far)


PIECE = 96


def ring_sum_kernel(ry1, rx1, ry3, rx3, ry2, rx2, py0, px0, out):
    wide = py0[...] + ry1[...].astype(jnp.float32) + ry2[...].astype(jnp.float32) + ry3[...].astype(jnp.float32)
    tall = px0[...] + rx1[...].astype(jnp.float32) + rx2[...].astype(jnp.float32) + rx3[...].astype(jnp.float32)
    wide = wide.astype(jnp.bfloat16)
    tall = tall.astype(jnp.bfloat16)
    for z in range(4):
        for low in range(2):
            first = (z * 2 + low) * PIECE
            if z < 2:
                out[first : first + 64, :] = wide[low * 64 : low * 64 + 64, z * FLOW : z * FLOW + B]
            else:
                for g in range(4):
                    from_row = low * 256 + g * 64
                    out[first : first + 64, g * 128 : (g + 1) * 128] = tall[
                        from_row : from_row + 64, (z - 2) * 128 : (z - 1) * 128
                    ]
            for h in range(2):
                for flow in range(2):
                    k = low * 64 + h * 32
                    at = h * 256 + flow * 128
                    out[first + 64 : first + PIECE, at : at + 128] = wide[
                        k : k + 32, flow * FLOW + B : (flow + 1) * FLOW
                    ]


def ring_sum(parts):
    return pl.pallas_call(
        ring_sum_kernel,
        out_shape=jax.ShapeDtypeStruct((8 * PIECE, B), jnp.bfloat16),
        in_specs=[VMEM] * 8,
        out_specs=VMEM,
        compiler_params=PARAMS,
        name="ring_sum",
    )(*parts)


def line_sum_kernel(arrived, out):
    total = arrived[0].astype(jnp.float32)
    for i in range(1, 8):
        total = total + arrived[i].astype(jnp.float32)
    out[...] = total.astype(jnp.bfloat16)


def line_sum(arrived):
    return pl.pallas_call(
        line_sum_kernel,
        out_shape=jax.ShapeDtypeStruct((PIECE, B), jnp.bfloat16),
        in_specs=[VMEM],
        out_specs=VMEM,
        compiler_params=PARAMS,
        name="line_sum",
    )(arrived)


def choose_kernel(place, q0, q1, q2, q3, out, position, held):
    fill_positions(place, position)
    my_x, my_core, my_low = place[1], place[2], place[4]
    mine = position[(place[0] * 4 + my_x) * 2 + my_core]

    @pl.when(mine >= 4)
    def _():
        out[...] = jnp.zeros(out.shape, jnp.bfloat16)

    @pl.when(mine < 4)
    def _():
        for r, ref in enumerate((q0, q1, q2, q3)):
            held[my_x ^ r] = ref[...]
        flow = mine >> 1
        for xl in range(2):
            at_x = 2 * (mine & 1) + xl
            for flip in range(2):
                to = aligned(xl * 2 + (my_core ^ flip), 128)
                for w in range(2):
                    for h in range(2):
                        rows = pl.ds(pl.multiple_of((my_low ^ w) * 64 + h * 32, 32), 32)
                        from_row = (flip * 2 + w) * 32
                        out[rows, pl.ds(to, 128)] = held[
                            at_x, from_row : from_row + 32, pl.ds(aligned(h * 2 + flow, 128), 128)
                        ]


def choose(place, pieces):
    return pl.pallas_call(
        choose_kernel,
        out_shape=jax.ShapeDtypeStruct((128, B), jnp.bfloat16),
        in_specs=[SMEM] + [VMEM] * 4,
        out_specs=VMEM,
        scratch_shapes=[pltpu.SMEM((32,), jnp.int32), pltpu.VMEM((4, 128, B), jnp.bfloat16)],
        compiler_params=PARAMS,
        name="choose",
    )(place, *pieces)


def cast_kernel(left, right, out):
    out[:SLOTS] = left[...].astype(jnp.bfloat16)
    out[SLOTS:] = right[...].astype(jnp.bfloat16)


def cast_rows(left, right):
    return pl.pallas_call(
        cast_kernel,
        out_shape=jax.ShapeDtypeStruct((2 * SLOTS, 64, B), jnp.bfloat16),
        in_specs=[VMEM] * 2,
        out_specs=VMEM,
        compiler_params=PARAMS,
        name="cast_rows",
    )(left, right)


def whole_kernel(place, s0, s1, s2, s3, out):
    for r, piece in enumerate((s0, s1, s2, s3)):
        for w in range(2):
            rows = pl.ds(aligned((place[3] ^ r) * 2 + (place[4] ^ w), 64), 64)
            for k in range(2 * SLOTS):
                out[k, rows, :] = piece[w * 2 * SLOTS + k]


def whole(place, pieces):
    return pl.pallas_call(
        whole_kernel,
        out_shape=jax.ShapeDtypeStruct((2 * SLOTS, B, B), jnp.bfloat16),
        in_specs=[SMEM] + [VMEM] * 4,
        out_specs=VMEM,
        compiler_params=PARAMS,
        name="whole",
    )(place, *pieces)


def root_kernel(slot, place, r0, r1, r2, r3, statistics, left_rows, right_rows, *refs):
    if slot:
        left_first, right_first, directions, left_new, right_new, g_ref, a_ref, m_ref = refs
        left_new[0] = left_first[...]
        right_new[0] = right_first[...]
    else:
        directions, left_new, right_new, g_ref, a_ref, m_ref = refs
    my_z, my_y, my_low = place[0], place[3], place[4]
    node = my_y * 2 + my_low
    first_row = aligned(node, 64)
    for r, piece in enumerate((r0, r1, r2, r3)):
        at_y = my_y ^ r
        if slot:
            g_ref[pl.ds(aligned(at_y, 128), 128), :] = piece[...]
            continue
        for w in range(2):
            at_low = my_low ^ w
            base = w * 64

            @pl.when(my_z < 2)
            def _():
                g_ref[pl.ds(pl.multiple_of(at_y * 128 + at_low * 64, 64), 64), :] = piece[base : base + 64, :]

            @pl.when(my_z >= 2)
            def _():
                for g in range(4):
                    g_ref[
                        pl.ds(pl.multiple_of(at_low * 256 + g * 64, 64), 64),
                        pl.ds(aligned(at_y, 128), 128),
                    ] = piece[base : base + 64, g * 128 : (g + 1) * 128]

    def scaled(gram, old_rows, new_rows, which):
        a_ref[which] = gram
        rows = BETA * old_rows[slot] + a_ref[which, pl.ds(first_row, 64), :] * (1.0 / B)
        if slot:
            new_rows[slot] = rows
        else:
            new_rows[...] = rows
        full = BETA * statistics[which * SLOTS + slot].astype(jnp.float32) + gram * (1.0 / B)
        norm = B * jnp.sqrt(jnp.sum(full * full, keepdims=True) * (1.0 / (B * B)) + 1e-06)
        matrix = full / norm
        a_ref[which] = matrix
        m_ref[which] = matrix.astype(jnp.bfloat16)
        return lax.rsqrt(jnp.sqrt(norm))

    g = g_ref[...]
    left_gram = lax.dot_general(g, g, (((1,), (1,)), ((), ())), preferred_element_type=jnp.float32)
    right_gram = contract_rows(g, g)
    left_scale = scaled(left_gram, left_rows, left_new, 0)
    right_scale = scaled(right_gram, right_rows, right_new, 1)
    power = a_ref[0, pl.ds(first_row, 64), :]
    column = lax.broadcasted_iota(jnp.int32, (64, B), 1)
    row = lax.broadcasted_iota(jnp.int32, (64, B), 0) + first_row
    total = jnp.where(row == column, COEF[0], 0.0) + COEF[1] * power
    for k in range(2, 7):
        power = jnp.dot(power.astype(jnp.bfloat16), m_ref[0], preferred_element_type=jnp.float32)
        total = total + COEF[k] * power
    root = (total * left_scale).astype(jnp.bfloat16)
    half = jnp.dot(root, g, preferred_element_type=jnp.float32).astype(jnp.bfloat16)
    power = half.astype(jnp.float32)
    total = COEF[0] * power
    for k in range(1, 7):
        power = jnp.dot(power.astype(jnp.bfloat16), m_ref[1], preferred_element_type=jnp.float32)
        total = total + COEF[k] * power
    directions[...] = (total * right_scale).astype(jnp.bfloat16)


def roots(slot, place, pieces, statistics, left_rows, right_rows, *first):
    new = jax.ShapeDtypeStruct((SLOTS, 64, B) if slot else (64, B), jnp.float32)
    return pl.pallas_call(
        functools.partial(root_kernel, slot),
        out_shape=[jax.ShapeDtypeStruct((64, B), jnp.bfloat16), new, new],
        in_specs=[SMEM] + [VMEM] * (7 + len(first)),
        out_specs=[VMEM] * 3,
        scratch_shapes=[
            pltpu.VMEM((B, B), jnp.bfloat16),
            pltpu.VMEM((2, B, B), jnp.float32),
            pltpu.VMEM((2, B, B), jnp.bfloat16),
        ],
        compiler_params=PARAMS,
        name="roots",
    )(place, *pieces, statistics, left_rows, right_rows, *first)


def place_kernel(place, *refs):
    sources, out, position, sem = refs[:12], refs[12], refs[13], refs[14]
    fill_positions(place, position)
    my_z, my_x, my_core = place[0], place[1], place[2]

    def find(slot, r, a, far, near1, near3, held, low, high):
        if slot:
            return (held, 12 + a) if r == 0 else ((near1, far, near3)[r - 1], a)
        if r == 2:
            return (low, a) if a < 2 else (high, a - 2)
        return held, (0, 1, 0, 2)[r] * 4 + a

    for wait in (False, True):
        for slot in range(SLOTS):
            for flip in range(2):
                for r in range(4):
                    for a in range(4):
                        source, row = find(slot, r, a, *sources[flip * 6 : flip * 6 + 6])
                        block = position[((my_z ^ a) * 4 + (my_x ^ r)) * 2 + (my_core ^ flip)]
                        copy = pltpu.make_async_copy(
                            source.at[pl.ds(row * 64, 64), :],
                            out.at[:, pl.ds(aligned(jnp.minimum(block + slot * 32, 35), B), B)],
                            sem,
                        )
                        act = copy.wait if wait else copy.start
                        if slot == 0:
                            act()
                        else:
                            pl.when(block < 4)(act)


def put_blocks(place, sources, blocks):
    return pl.pallas_call(
        place_kernel,
        out_shape=jax.ShapeDtypeStruct((64, blocks * B), jnp.bfloat16),
        in_specs=[SMEM] + [ANY] * 12,
        out_specs=ANY,
        scratch_shapes=[pltpu.SMEM((32,), jnp.int32), pltpu.SemaphoreType.DMA],
        compiler_params=PARAMS,
        name="put_blocks",
    )(place, *sources)


def around_z(rows):
    a2, a1, a3 = swap(rows, "z_hi", 2), swap(rows, "z_hi", 1), swap(rows, "z_hi", 3)
    return jnp.concatenate([rows, a1, a2, a3])


def shards(x_band, d_gate_up, owner, stat_left, stat_right):
    place = jnp.concatenate([jnp.stack([lax.axis_index(a) for a in FINE]).astype(jnp.int32), owner])
    bucket = d_gate_up.shape[1] // B

    x1, x3 = packed(pack_x_kernel, "pack_x", [X_MSG] * 2, place, d_gate_up, x_band)
    x1, x3 = swap(x1, "x", 1), swap(x3, "x", 3)
    y1, y3 = packed(pack_y_kernel, "pack_y", [Y_MSG] * 2, place, d_gate_up, x_band)
    y1, y3 = swap(y1, "y", 1), swap(y3, "y", 3)
    (own,) = packed(pack_own_kernel, "pack_own", [OWN_MSG], place, d_gate_up)
    statistics = cast_rows(stat_left[0], stat_right[0])
    statistics = jnp.concatenate([statistics, swap(statistics, "z_lo", 1)])
    f0, f1 = swap(x1[:, X_FWD], "x", 3), swap(x3[:, X_FWD], "x", 1)
    y1_on, y3_on, statistics = lax.optimization_barrier((y1[:, Y_FWD], y3[:, Y_FWD], statistics))
    f2, f3 = swap(y1_on, "y", 3), swap(y3_on, "y", 1)
    on_x, on_y = (own, x_band, x1, x3, f0, f1), (own, x_band, y1, y3, f2, f3)
    far_wide = swap(partials(1, FLOW, 0, on_x), "core", 1)
    far_tall = swap(partials(1, B, 4 * FLOW, on_y), "core", 1)
    wide, tall = partials(0, FLOW, 0, on_x), partials(0, B, 4 * FLOW, on_y)
    py0, py1, py2, py3 = chip_sum(wide_sum_kernel, "wide_sum", (128, 2 * FLOW), place, wide, far_wide)
    px0, px1, px2, px3 = chip_sum(tall_sum_kernel, "tall_sum", (B, 256), place, tall, far_tall)
    ry1, rx1 = swap(py1, "y", 1), swap(px1, "x", 1)
    ry3, rx3 = swap(py3, "y", 3), swap(px3, "x", 3)
    ry2, rx2 = swap(py2, "y", 2), swap(px2, "x", 2)
    message = ring_sum((ry1, rx1, ry3, rx3, ry2, rx2, py0, px0))

    message, statistics = lax.optimization_barrier((message, statistics))
    s2, s1, s3 = swap(statistics, "y", 2), swap(statistics, "y", 1), swap(statistics, "y", 3)
    message = lax.all_to_all(message, ("z_hi", "z_lo"), 0, 0, tiled=True)
    line = line_sum(message.reshape(8, PIECE, B))

    main, extra = line[:64], line[64:]
    far = swap(line, "z_lo", 1)
    extra_core = swap(extra, "core", 1)
    diagonal = [(c * 2 + w, 3 - (c * 2 + w)) for c in range(2) for w in range(2)]
    extra_far = lax.ppermute(extra, ("core", "z_lo"), diagonal)
    m0 = jnp.concatenate([main, far[:64]])
    m0, s1, s2, s3 = lax.optimization_barrier((m0, s1, s2, s3))
    statistics = whole(place, (statistics, s1, s2, s3))
    m2, m1, m3 = swap(m0, "y", 2), swap(m0, "y", 1), swap(m0, "y", 3)
    q0 = jnp.concatenate([extra, far[64:], extra_core, extra_far])
    q2, q1, q3 = swap(q0, "x", 2), swap(q0, "x", 1), swap(q0, "x", 3)
    first, left_first, right_first = roots(0, place, (m0, m1, m2, m3), statistics, stat_left[0], stat_right[0])
    e0 = choose(place, (q0, q1, q2, q3))
    e2, e1, e3 = swap(e0, "y", 2), swap(e0, "y", 1), swap(e0, "y", 3)
    first, e1, e2, e3 = lax.optimization_barrier((first, e1, e2, e3))
    a2, a1, a3 = swap(first, "z_hi", 2), swap(first, "z_hi", 1), swap(first, "z_hi", 3)
    second, left_new, right_new = roots(
        1, place, (e0, e1, e2, e3), statistics, stat_left[0], stat_right[0], left_first, right_first
    )
    second, a2 = lax.optimization_barrier((second, a2))
    plane = jnp.concatenate([first, a1, a2, a3])
    second = around_z(second)
    first1, first3 = swap(plane, "x", 1), swap(plane, "x", 3)
    far, near1, near3 = swap(second, "x", 2), swap(second, "x", 1), swap(second, "x", 3)
    first1, first3, _ = lax.optimization_barrier((first1, first3, second))
    low, high = swap(first1[:128], "x", 3), swap(first3[128:], "x", 1)
    held = jnp.concatenate([plane, first1, first3, second])
    sources = (far, near1, near3, held, low, high)
    out = put_blocks(place, sources + tuple(swap(v, "core", 1) for v in sources), bucket)
    return (out, left_new[None], right_new[None])


def solution(mesh):
    fine = Mesh(np.asarray(mesh.devices).reshape(FINE_SIZES), FINE)
    dp, node = FINE[:3], FINE[3:]
    placed = (P(dp + node, None), P(dp + node, None), P(), P(dp, None, node, None), P(dp, None, node, None))
    return jax.shard_map(
        shards,
        mesh=fine,
        in_specs=placed,
        out_specs=(P(node, None), P(dp, None, node, None), P(dp, None, node, None)),
        check_vma=False,
    )
```
